128 devices in a mesh: gx: 8 (over x, core), gy: 16 (over z, y).
Axes of the slice: x: 4, y: 4, z: 4, core: 2. Of those that a mesh axis runs over, the one named last changes fastest.
Arguments:
- subvoxel_location_share: float32 [3, 2097152], P(None, ('gx', 'gy')), may hold values from 0.5 to 1.5
- point_motion_vector: float32 [3, 2097152], P(None, ('gx', 'gy')), may hold values from -5 to 5
- linear_gradient_matrix: float32 [9, 2097152], P(None, ('gx', 'gy')), may hold values from -3 to 3
- kirchhoff_tension_matrix: float32 [9, 2097152], P(None, ('gx', 'gy')), may hold values from -5 to 5
- point_inertia_amounts: float32 [2097152], P(('gx', 'gy')), may hold values from 0.5 to 2
- point_thermal_state: float32 [2097152], P(('gx', 'gy')), may hold values from 0.5 to 2
- anchor_voxel_shift: int32 [2097152], P(('gx', 'gy')), may hold values from 0 to 63
- group_resting_volume: int32 [16384], P(('gx', 'gy')), may hold values from 0 to 127
- group_migration_label: int32 [16384], P(('gx', 'gy')), may hold values from 0 to 8, as said below
- cylinder_shell_flag: int32 [32, 64, 512], P('gx', 'gy'), may hold values 0 or 1
- rough_surface_flag: int32 [32, 64, 512], P('gx', 'gy'), may hold values 0 or 1
- voxel_facing_choice: int32 [32, 64, 512], P('gx', 'gy'), may hold values from 0 to 63
- facing_unit_vectors: float32 [3, 64], replicated, may hold values from -1 to 1, as said below
- rim_thermal_level: float32 [32, 64, 512], P('gx', 'gy'), may hold values from 1 to 3
Outputs:
- next_motion_vector: float32 [3, 4194304], P(None, ('gx', 'gy'))
- next_gradient_matrix: float32 [9, 4194304], P(None, ('gx', 'gy'))
- next_thermal_state: float32 [4194304], P(('gx', 'gy'))
- grid_velocity: float32 [3, 32, 64, 512], P(None, 'gx', 'gy')
- grid_temperature: float32 [32, 64, 512], P('gx', 'gy')
The draws below stay inside these ranges and needn't reach their ends.
Inputs may be any that keep to these rules, and one draw needn't show every extreme that they name: `group_migration_label`: code 3*(dx+1)+(dy+1) sends a block to the tile offset by dx along x and dy along y, with wrap-around; code 4 keeps it. Among the 128 blocks of one tile at most 16 carry any one code other than 4, and in every draw some tile receives exactly 16 blocks from each of its eight neighbours. `anchor_voxel_shift`: the particle's base cell inside its block's brick is (o // 16, o // 4 % 4, o % 4). `facing_unit_vectors`: each column is a unit vector.
All inputs are finite; a program needn't handle non-finite values. No bound on the sum of `cylinder_shell_flag` or of `rough_surface_flag` on one device may be relied on, other than what follows from the above.
Results may differ from the reference program's by a relative error of at most 0.0003.
Values sent between devices are 32-bit elements; how exact they have to be, the bound alone decides.
No kernel may reach another device: no remote copies, remote signals or barrier semaphores. Data moves between devices by JAX's collectives and lax.ppermute only.
A program may use at most 128 MiB of HBM per device.

```python
import math
import jax
import jax.numpy as jnp
from jax import lax

CX = 4
CY = 4
MESH_HEIGHT_UP = 512
B_DEV = 128
MOVE = 16
GROUP_MATERIAL_PTS = 128
NNORM = 64
SWEEPS = 2
NTX = 8
NTY = 16
TILES = 128
MESH_WIDTH_EAST = 32
MESH_WIDTH_NORTH = 64
NBR = 128
B_NEW = 256
NBLK = 16384
MATERIAL_POINTS = 2097152
PLACES_AFTERWARD = 4194304


def shuffle_one(one_key):
    return jax.random.permutation(one_key, B_DEV)


def draw_group_migration_label(key, part):
    key = jax.random.fold_in(key, 11)
    key_count, key_crowd, key_order = jax.random.split(key, 3)
    counts = jax.random.randint(key_count, (TILES, 9), 0, max(MOVE // 4, 1) + 1)
    crowded = jax.random.randint(key_crowd, (), 0, TILES)
    tile_ids = jnp.arange(TILES, dtype=jnp.int32)
    code_list = jnp.arange(9, dtype=jnp.int32)
    target = (tile_ids[:, None] // NTY + code_list[None, :] // 3 - 1) % NTX * NTY + (tile_ids[:, None] % NTY + code_list[None, :] % 3 - 1) % NTY
    counts = jnp.where(target == crowded, MOVE, counts)
    counts = jnp.where(code_list[None, :] == 4, 0, counts)
    range_end = jnp.cumsum(counts, axis=1)
    range_start = range_end - counts
    tile_keys = jax.random.split(key_order, TILES)
    shuffled = jax.vmap(shuffle_one)(tile_keys)
    inside = (shuffled[:, :, None] >= range_start[:, None, :]) & (shuffled[:, :, None] < range_end[:, None, :])
    chosen = jnp.sum(inside.astype(jnp.int32) * code_list[None, None, :], axis=2) + 4 * (1 - jnp.any(inside, axis=2).astype(jnp.int32))
    return chosen.reshape(-1).astype(jnp.int32)


def draw_facing_unit_vectors(key, part):
    key = jax.random.fold_in(key, 5)
    key_lift, key_turn = jax.random.split(key)
    lift = jax.random.uniform(key_lift, (NNORM,), jnp.float32, -1.0, 1.0)
    turning = jax.random.uniform(key_turn, (NNORM,), jnp.float32, -math.pi, math.pi)
    radial = jnp.sqrt(1.0 - lift * lift)
    return jnp.stack([radial * jnp.cos(turning), radial * jnp.sin(turning), lift]).astype(jnp.float32)


def plant(entries, key, smallest, top_value):
    extent = entries.shape
    spot = [jax.random.randint(jax.random.fold_in(key, axis), (), 0, extent[axis]) for axis in range(len(extent))]
    entries = entries.at[tuple(spot)].set(smallest)
    longest = extent.index(max(extent))
    spot[longest] = (spot[longest] + 1) % extent[longest]
    return entries.at[tuple(spot)].set(top_value)


def levels(rng, dims, shards, smallest, high):
    def one(position, blocks):
        heights = jax.random.uniform(jax.random.fold_in(jax.random.fold_in(rng, 6), position), (blocks,), jnp.float32, smallest / len(shards), high / len(shards))
        return jnp.repeat(jnp.exp(heights), dims[position] // blocks).reshape((-1,) + (1,) * (len(dims) - position - 1))

    factor_of = one(*shards[0])
    for cut in shards[1:]:
        factor_of = factor_of * one(*cut)
    return factor_of


def bell_draw(rng, extent, width, most, shards=(), kind=jnp.bfloat16):
    gain = levels(rng, extent, shards, -0.22, 0.18) if shards else 1.0
    entries = jax.random.normal(rng, extent, jnp.float32) * width * gain
    return jnp.minimum(jnp.maximum(entries, -most), most).astype(kind)


def setup_inputs(seed: int = 0) -> dict:
    splits = jax.random.split(jax.random.key(seed), 15)
    subvoxel_location_share = jnp.clip(0.5 + 1.0 * jax.random.uniform(splits[0], (3, MATERIAL_POINTS), jnp.float32) ** levels(splits[0], (3, MATERIAL_POINTS), ((1, 128),), -0.2, 0.2), 0.5, 1.5)
    point_motion_vector = bell_draw(splits[1], (3, MATERIAL_POINTS), 1.0, 5.0, ((1, 128),), jnp.float32)
    linear_gradient_matrix = bell_draw(splits[2], (9, MATERIAL_POINTS), 0.5, 3.0, ((1, 128),), jnp.float32)
    kirchhoff_tension_matrix = bell_draw(splits[3], (9, MATERIAL_POINTS), 1.0, 5.0, ((1, 128),), jnp.float32)
    point_inertia_amounts = jnp.clip(jnp.exp(math.log(2.0) - 1.3862944 * jax.random.uniform(splits[4], (MATERIAL_POINTS,), jnp.float32) ** levels(splits[4], (MATERIAL_POINTS,), ((0, 128),), -0.2, 0.2)), 0.5, 2.0)
    point_thermal_state = jnp.clip(0.5 + 1.5 * jax.random.uniform(splits[5], (MATERIAL_POINTS,), jnp.float32) ** levels(splits[5], (MATERIAL_POINTS,), ((0, 128),), -0.2, 0.2), 0.5, 2.0)
    anchor_voxel_shift = plant(jax.random.randint(splits[6], (MATERIAL_POINTS,), 0, 64), jax.random.fold_in(splits[6], 1), 0, 63).astype(jnp.int32)
    group_resting_volume = plant(jax.random.randint(splits[7], (NBLK,), 0, NBR), jax.random.fold_in(splits[7], 1), 0, NBR - 1).astype(jnp.int32)
    group_migration_label = draw_group_migration_label(jax.random.fold_in(splits[14], 71), 0)
    cylinder_shell_flag = plant((jax.random.randint(splits[9], (MESH_WIDTH_EAST, MESH_WIDTH_NORTH, MESH_HEIGHT_UP), 0, 8) < 1).astype(jnp.int32), jax.random.fold_in(splits[9], 1), 0, 1)
    rough_surface_flag = plant((jax.random.randint(splits[10], (MESH_WIDTH_EAST, MESH_WIDTH_NORTH, MESH_HEIGHT_UP), 0, 4) < 1).astype(jnp.int32), jax.random.fold_in(splits[10], 1), 0, 1)
    voxel_facing_choice = plant(jax.random.randint(splits[11], (MESH_WIDTH_EAST, MESH_WIDTH_NORTH, MESH_HEIGHT_UP), 0, NNORM), jax.random.fold_in(splits[11], 1), 0, NNORM - 1).astype(jnp.int32)
    facing_unit_vectors = draw_facing_unit_vectors(jax.random.fold_in(splits[14], 71), 0)
    rim_thermal_level = jnp.clip(1.0 + 2.0 * jax.random.uniform(splits[13], (MESH_WIDTH_EAST, MESH_WIDTH_NORTH, MESH_HEIGHT_UP), jnp.float32) ** levels(splits[13], (MESH_WIDTH_EAST, MESH_WIDTH_NORTH, MESH_HEIGHT_UP), ((0, 8), (1, 16)), -0.2, 0.2), 1.0, 3.0)
    return dict(subvoxel_location_share=subvoxel_location_share, point_motion_vector=point_motion_vector, linear_gradient_matrix=linear_gradient_matrix, kirchhoff_tension_matrix=kirchhoff_tension_matrix, point_inertia_amounts=point_inertia_amounts, point_thermal_state=point_thermal_state, anchor_voxel_shift=anchor_voxel_shift, group_resting_volume=group_resting_volume, group_migration_label=group_migration_label, cylinder_shell_flag=cylinder_shell_flag, rough_surface_flag=rough_surface_flag, voxel_facing_choice=voxel_facing_choice, facing_unit_vectors=facing_unit_vectors, rim_thermal_level=rim_thermal_level)


precise = lax.Precision.HIGHEST
mass_floor = 0.25
slip_floor = 0.1
friction = 0.4
gravity_step = 0.5
conduct = 0.15
stress_coef = 0.25
per_turn = 32

def axis_weights(frac_part, start):
    steps_rel = jnp.arange(6, dtype=jnp.int32)[None, None, :] - start[:, :, None]
    inside = frac_part[:, :, None]
    near = 0.5 * (1.5 - inside) ** 2
    middle = 0.75 - (inside - 1.0) ** 2
    far_part = 0.5 * (inside - 0.5) ** 2
    weight = jnp.where(steps_rel == 0, near, jnp.where(steps_rel == 1, middle, jnp.where(steps_rel == 2, far_part, 0.0)))
    return (weight, steps_rel.astype(jnp.float32) - inside)

def outer_cube(first, second, third):
    cube = first[:, :, :, None, None] * second[:, :, None, :, None] * third[:, :, None, None, :]
    return cube.reshape(first.shape[0], first.shape[1], 216)

def block_weights(frac_part, offset):
    weight_x, dist_x = axis_weights(frac_part[0], offset // 16)
    weight_y, dist_y = axis_weights(frac_part[1], offset // 4 % 4)
    weight_z, dist_z = axis_weights(frac_part[2], offset % 4)
    return jnp.concatenate([outer_cube(weight_x, weight_y, weight_z), outer_cube(weight_x * dist_x, weight_y, weight_z), outer_cube(weight_x, weight_y * dist_y, weight_z), outer_cube(weight_x, weight_y, weight_z * dist_z)], axis=1)

def scatter_terms(frac_part, offset, vel_part, q_part, mass_part, temp_part):
    weights = block_weights(frac_part, offset)
    blank = jnp.zeros_like(mass_part)
    plain = jnp.stack([mass_part, mass_part * vel_part[0], mass_part * vel_part[1], mass_part * vel_part[2], mass_part * temp_part], axis=1)
    pieces = [plain]
    for column in range(3):
        pieces.append(jnp.stack([blank, q_part[column], q_part[3 + column], q_part[6 + column], blank], axis=1))
    left_side = jnp.concatenate(pieces, axis=2)
    return jnp.einsum('gcq,gqk->gck', left_side, weights, precision=precise)

def gather_terms(frac_part, offset, window):
    weights = block_weights(frac_part, offset)
    result = jnp.einsum('gck,gqk->cgq', window, weights, precision=precise)
    groups = window.shape[0]
    parts = weights.shape[1] // 4
    result = result.reshape(4, groups, 4, parts)
    vel_out = result[:3, :, 0]
    thermal_result = result[3, :, 0]
    aff_out = 4.0 * jnp.transpose(result[:3, :, 1:], (0, 2, 1, 3)).reshape(9, groups, parts)
    return (vel_out, aff_out, thermal_result)

def fold_axis(values, where_at):
    values = jnp.moveaxis(values, (where_at, where_at + 1), (0, 1))
    count = values.shape[0]
    rest = values.shape[2:]
    pad_rest = ((0, 0),) * len(rest)
    head = values[:, :4].reshape((4 * count,) + rest)
    tail = jnp.pad(values[:, 4:], ((0, 0), (0, 2)) + pad_rest).reshape((4 * count,) + rest)
    folded = jnp.pad(head, ((0, 4),) + pad_rest) + jnp.pad(tail, ((4, 0),) + pad_rest)
    return jnp.moveaxis(folded[:4 * count + 2], 0, where_at)

def unfold_axis(values, where_at):
    values = jnp.moveaxis(values, where_at, 0)
    count = (values.shape[0] - 2) // 4
    rest = values.shape[1:]
    ghost_extended_array = jnp.pad(values, ((0, 2),) + ((0, 0),) * len(rest))
    head = ghost_extended_array[:4 * count].reshape((count, 4) + rest)
    tail = ghost_extended_array[4:4 * count + 4].reshape((count, 4) + rest)[:, :2]
    return jnp.moveaxis(jnp.concatenate([head, tail], axis=1), (0, 1), (where_at, where_at + 1))

def ghost_from_bricks(deposit_accumulations, cells_x, cells_y, cells_z):
    shaped = deposit_accumulations.reshape(cells_x // 4, cells_y // 4, cells_z // 4, 5, 6, 6, 6).transpose(3, 0, 4, 1, 5, 2, 6)
    shaped = fold_axis(shaped, 1)
    shaped = fold_axis(shaped, 2)
    shaped = fold_axis(shaped, 3)
    return shaped[:, :, :, 1:-1]

def bricks_window(field):
    shaped = unfold_axis(field, 1)
    shaped = unfold_axis(shaped, 3)
    shaped = unfold_axis(shaped, 5)
    return shaped.transpose(1, 3, 5, 0, 2, 4, 6).reshape(-1, field.shape[0] * 216)

def advance_mesh_voxels(deposit_accumulations, solid, wall, voxel_facing_vectors, wall_temp, location_eastward, location_upward, width_x, height_z):
    denom = jnp.maximum(deposit_accumulations[0], mass_floor)
    moving = deposit_accumulations[1:4] / denom
    moving = jnp.stack([moving[0], moving[1], moving[2] - gravity_step])
    spin = 2.0 / height_z
    rel_x = location_eastward + 0.5 - 0.5 * width_x
    rel_z = location_upward + 0.5 - 0.5 * height_z
    cell_shape = denom.shape
    wall_vel = jnp.stack([jnp.broadcast_to(spin * rel_z, cell_shape), jnp.zeros(cell_shape, denom.dtype), jnp.broadcast_to(-spin * rel_x, cell_shape)])
    relative = moving - wall_vel
    normal_part = lax.optimization_barrier(jnp.sum(relative * voxel_facing_vectors, axis=0))
    tangent = relative - normal_part * voxel_facing_vectors
    tangent_len = jnp.sqrt(lax.optimization_barrier(jnp.sum(tangent * tangent, axis=0)))
    factor = jnp.maximum(0.0, 1.0 + friction * normal_part / jnp.maximum(tangent_len, slip_floor))
    slipped = wall_vel + tangent * factor
    moving = jnp.where((wall == 1) & (normal_part < 0.0), slipped, moving)
    moving = jnp.where(solid == 1, wall_vel, moving)
    thermal_result = jnp.where(solid == 1, wall_temp, deposit_accumulations[4] / denom)
    return (moving, thermal_result)

def diffusion_pass_thermal(ghost_extended_array, interior_material_region, shell_interior_region):
    core = ghost_extended_array[1:-1, 1:-1]
    z_up = jnp.concatenate([core[:, :, 1:], core[:, :, -1:]], axis=2)
    z_down = jnp.concatenate([core[:, :, :1], core[:, :, :-1]], axis=2)
    laplace = ghost_extended_array[:-2, 1:-1] + ghost_extended_array[2:, 1:-1] + ghost_extended_array[1:-1, :-2] + ghost_extended_array[1:-1, 2:] + z_up + z_down - 6.0 * core
    return jnp.where(interior_material_region == 1, shell_interior_region, core + conduct * laplace)

def cut_blocks(values, start):
    return lax.dynamic_slice_in_dim(values, start, per_turn, 1)

def tile_scatter(pack):
    frac_t, vel_t, q_t, mass_t, temp_t, offset_t, brick_t = pack

    def scatter_turn(turn_no):
        start = turn_no * per_turn
        return scatter_terms(cut_blocks(frac_t, start), cut_blocks(offset_t, start)[0], cut_blocks(vel_t, start), cut_blocks(q_t, start), cut_blocks(mass_t, start)[0], cut_blocks(temp_t, start)[0])
    terms = lax.map(scatter_turn, jnp.arange(B_NEW // per_turn, dtype=jnp.int32)).reshape(B_NEW, 5 * 216)
    segment = jnp.where(brick_t >= 0, brick_t, NBR)
    deposit_accumulations = jax.ops.segment_sum(terms, segment, num_segments=NBR + 1)[:NBR]
    return ghost_from_bricks(deposit_accumulations, CX, CY, MESH_HEIGHT_UP)

def tile_gather(local, frac_t, offset_t, brick_t):
    brick_win = bricks_window(local)
    windows = jnp.take(brick_win, jnp.maximum(brick_t, 0), axis=0)
    live = (brick_t >= 0).astype(jnp.float32)

    def gather_turn(turn_no):
        start = turn_no * per_turn
        window = lax.dynamic_slice_in_dim(windows, start, per_turn, 0).reshape(per_turn, 4, 216)
        keep = lax.dynamic_slice_in_dim(live, start, per_turn, 0)
        vel_out, aff_out, thermal_result = gather_terms(cut_blocks(frac_t, start), cut_blocks(offset_t, start)[0], window)
        return (vel_out * keep[None, :, None], aff_out * keep[None, :, None], thermal_result * keep[:, None])
    vel_out, aff_out, thermal_result = lax.map(gather_turn, jnp.arange(B_NEW // per_turn, dtype=jnp.int32))
    return (jnp.moveaxis(vel_out, 0, 1).reshape(3, B_NEW * GROUP_MATERIAL_PTS), jnp.moveaxis(aff_out, 0, 1).reshape(9, B_NEW * GROUP_MATERIAL_PTS), thermal_result.reshape(B_NEW * GROUP_MATERIAL_PTS))

def reference(subvoxel_location_share, point_motion_vector, linear_gradient_matrix, kirchhoff_tension_matrix, point_inertia_amounts, point_thermal_state, anchor_voxel_shift, group_resting_volume, group_migration_label, cylinder_shell_flag, rough_surface_flag, voxel_facing_choice, facing_unit_vectors, rim_thermal_level):
    block_ids = jnp.arange(NBLK, dtype=jnp.int32)
    tile_of = block_ids // B_DEV
    slot_of = block_ids % B_DEV
    marks = (group_migration_label[:, None] == jnp.arange(9, dtype=jnp.int32)[None, :]).astype(jnp.int32)
    running = jnp.cumsum(marks.reshape(TILES, B_DEV, 9), axis=1).reshape(NBLK, 9)
    ranking = lax.optimization_barrier(jnp.sum((running - 1) * marks, axis=1))
    shift_x = group_migration_label // 3 - 1
    shift_y = group_migration_label % 3 - 1
    dest_tile = (tile_of // NTY + shift_x) % NTX * NTY + (tile_of % NTY + shift_y) % NTY
    group_no = 8 - group_migration_label
    group_no = jnp.where(group_no < 4, group_no, group_no - 1)
    new_slot = jnp.where(group_migration_label == 4, slot_of, B_DEV + MOVE * group_no + ranking)
    target = dest_tile * B_NEW + new_slot
    q_term = point_inertia_amounts[None] * linear_gradient_matrix - stress_coef * kirchhoff_tension_matrix

    def migrated_points(values):
        channels = values.shape[0]
        shaped = values.reshape(channels, NBLK, GROUP_MATERIAL_PTS)
        placed = jnp.zeros((channels, TILES * B_NEW, GROUP_MATERIAL_PTS), values.dtype).at[:, target].set(shaped)
        return jnp.moveaxis(placed.reshape(channels, TILES, B_NEW, GROUP_MATERIAL_PTS), 1, 0)
    frac_new = migrated_points(subvoxel_location_share)
    vel_new = migrated_points(point_motion_vector)
    q_new = migrated_points(q_term)
    mass_new = migrated_points(point_inertia_amounts[None])
    refreshed_thermal = migrated_points(point_thermal_state[None])
    offset_new = migrated_points(anchor_voxel_shift[None])
    brick_new = jnp.full((TILES * B_NEW,), -1, jnp.int32).at[target].set(group_resting_volume).reshape(TILES, B_NEW)
    ghosts = lax.map(tile_scatter, (frac_new, vel_new, q_new, mass_new, refreshed_thermal, offset_new, brick_new))
    shaped = ghosts.reshape(NTX, NTY, 5, CX + 2, CY + 2, MESH_HEIGHT_UP)
    core = shaped[:, :, :, 1:CX + 1]
    core = core.at[:, :, :, CX - 1].add(jnp.roll(shaped[:, :, :, 0], -1, axis=0))
    core = core.at[:, :, :, 0].add(jnp.roll(shaped[:, :, :, CX + 1], 1, axis=0))
    inner = core[:, :, :, :, 1:CY + 1]
    inner = inner.at[:, :, :, :, CY - 1].add(jnp.roll(core[:, :, :, :, 0], -1, axis=1))
    inner = inner.at[:, :, :, :, 0].add(jnp.roll(core[:, :, :, :, CY + 1], 1, axis=1))
    deposit_accumulations = jnp.transpose(inner, (2, 0, 3, 1, 4, 5)).reshape(5, MESH_WIDTH_EAST, MESH_WIDTH_NORTH, MESH_HEIGHT_UP)
    location_eastward = jnp.arange(MESH_WIDTH_EAST, dtype=jnp.int32).astype(jnp.float32)[:, None, None]
    location_upward = jnp.arange(MESH_HEIGHT_UP, dtype=jnp.int32).astype(jnp.float32)[None, None, :]
    voxel_facing_vectors = jnp.take(facing_unit_vectors, voxel_facing_choice, axis=1)
    voxel_motion_vector, thermal_amount = advance_mesh_voxels(deposit_accumulations, cylinder_shell_flag, rough_surface_flag, voxel_facing_vectors, rim_thermal_level, location_eastward, location_upward, MESH_WIDTH_EAST, MESH_HEIGHT_UP)
    for sweep_no in range(SWEEPS):
        thermal_amount = diffusion_pass_thermal(jnp.pad(thermal_amount, ((1, 1), (1, 1), (0, 0)), mode='wrap'), cylinder_shell_flag, rim_thermal_level)
    field = jnp.concatenate([voxel_motion_vector, thermal_amount[None]], axis=0)
    field = jnp.pad(field, ((0, 0), (1, 1), (1, 1), (0, 0)), mode='wrap')
    field = jnp.pad(field, ((0, 0), (0, 0), (0, 0), (1, 1)))

    def gather_tile(pack):
        tile_no, frac_t, offset_t, brick_t = pack
        anchor = jnp.zeros((), jnp.int32)
        corner_x = (tile_no // NTY * CX).astype(jnp.int32)
        corner_y = (tile_no % NTY * CY).astype(jnp.int32)
        local = lax.dynamic_slice(field, (anchor, corner_x, corner_y, anchor), (4, CX + 2, CY + 2, MESH_HEIGHT_UP + 2))
        return tile_gather(local, frac_t, offset_t, brick_t)
    vel_out, aff_out, thermal_result = lax.map(gather_tile, (jnp.arange(TILES, dtype=jnp.int32), frac_new, offset_new, brick_new))
    next_motion_vector = jnp.moveaxis(vel_out, 0, 1).reshape(3, PLACES_AFTERWARD)
    next_gradient_matrix = jnp.moveaxis(aff_out, 0, 1).reshape(9, PLACES_AFTERWARD)
    next_thermal_state = thermal_result.reshape(PLACES_AFTERWARD)
    return (next_motion_vector, next_gradient_matrix, next_thermal_state, voxel_motion_vector, thermal_amount)
```

```python
import jax
import jax.numpy as jnp
from jax import lax
from jax.experimental import pallas as pl
from jax.experimental.pallas import tpu as pltpu
from jax.sharding import PartitionSpec as P

f32 = jnp.float32
bf16 = jnp.bfloat16
mass_floor = 0.25
slip_floor = 0.1
friction = 0.4
gravity_step = 0.5
conduct = 0.15
stress_coef = 0.25
mib = 1024 * 1024
pieces = 31
tiles = 9
msg_tiles = 13
msg_rows = msg_tiles * 16


def axis_tables(shift, inside, scale):
    near = 0.5 * (1.5 - inside) ** 2
    middle = 0.75 - (inside - 1.0) ** 2
    far = 0.5 * (inside - 0.5) ** 2
    at = [shift == step for step in range(4)]
    zero = jnp.zeros_like(inside)
    weight = [
        jnp.where(at[0], near, zero),
        jnp.where(at[0], middle, jnp.where(at[1], near, zero)),
        jnp.where(at[0], far, jnp.where(at[1], middle, jnp.where(at[2], near, zero))),
        jnp.where(at[1], far, jnp.where(at[2], middle, jnp.where(at[3], near, zero))),
        jnp.where(at[2], far, jnp.where(at[3], middle, zero)),
        jnp.where(at[3], far, zero),
    ]
    place = shift.astype(f32) + inside
    first = [weight[step] * (scale * (step - place)) for step in range(6)]
    return weight, first


def split_two(value):
    high = value.astype(bf16).astype(f32)
    return high, value - high


def deposit_kernel(
    code_s, brick_s, f_hbm, v_hbm, c_hbm, k_hbm, m_hbm, t_hbm, o_hbm,
    own_ref, frac_ref, xm_ref, ym_ref, yp_ref, xp_ref,
    f_ref, v_ref, c_ref, k_ref, m_ref, t_ref, o_ref, sems,
    raw, sa, sb, acc, cnt, out,
):
    pairs = (
        (f_hbm, f_ref), (v_hbm, v_ref), (c_hbm, c_ref), (k_hbm, k_ref),
        (m_hbm, m_ref), (t_hbm, t_ref), (o_hbm, o_ref),
    )
    copies = [pltpu.make_async_copy(a, b, sems.at[n]) for n, (a, b) in enumerate(pairs)]
    for copy in copies:
        copy.start()
    def clear(step, carry):
        acc[pl.ds(pl.multiple_of(step * 256, 256), 256), :] = jnp.zeros((256, 128), f32)
        return carry

    lax.fori_loop(0, 32, clear, 0)
    out[...] = jnp.zeros(out.shape, f32)
    sa[...] = jnp.zeros(sa.shape, f32)
    sb[...] = jnp.zeros(sb.shape, f32)
    for code in range(9):
        cnt[code] = 0
    for copy in copies:
        copy.wait()
    row_no = lax.broadcasted_iota(jnp.int32, (32, 1), 0)

    def group(g, carry):
        for j in range(8):
            lanes = pl.ds(pl.multiple_of((g * 8 + j) * 128, 128), 128)
            raw[j * 40 : j * 40 + 3, :] = f_ref[:, lanes]
            raw[j * 40 + 3 : j * 40 + 6, :] = v_ref[:, lanes]
            raw[j * 40 + 8 : j * 40 + 17, :] = c_ref[:, lanes]
            raw[j * 40 + 24 : j * 40 + 33, :] = k_ref[:, lanes]
        rows = pl.ds(pl.multiple_of(g * 8, 8), 8)
        mass = m_ref[rows, :]
        heat = mass * t_ref[rows, :]
        offset = o_ref[rows, :]

        def get(row):
            return raw[pl.ds(row, 8, stride=40), :]

        inside = [get(d) for d in range(3)]
        for d in range(3):
            frac_ref[d, rows, :] = inside[d]
        wx, rx = axis_tables(offset >> 4, inside[0], 1.0)
        for a in range(3):
            push = mass * get(3 + a)
            q = [
                mass * get(8 + a * 3 + k) - stress_coef * get(24 + a * 3 + k) for k in range(3)
            ]
            for j in range(6):
                sa[pl.ds((a * 6 + j) * 8, 8), :] = push * wx[j] + q[0] * rx[j]
                sa[pl.ds((32 + a * 6 + j) * 8, 8), :] = q[1] * wx[j]
                sa[pl.ds((64 + a * 6 + j) * 8, 8), :] = q[2] * wx[j]
        for j in range(6):
            sa[pl.ds((18 + j) * 8, 8), :] = mass * wx[j]
            sa[pl.ds((24 + j) * 8, 8), :] = heat * wx[j]
        wy, ry = axis_tables((offset >> 2) & 3, inside[1], 1.0)
        wz, rz = axis_tables(offset & 3, inside[2], 1.0)
        for jy in range(6):
            for jz in range(6):
                r = jy * 6 + jz
                sb[pl.ds(r * 8, 8), :] = wy[jy] * wz[jz]
                sb[pl.ds((40 + r) * 8, 8), :] = ry[jy] * wz[jz]
                sb[pl.ds((80 + r) * 8, 8), :] = wy[jy] * rz[jz]
        sums = []
        for j in range(8):
            left = jnp.concatenate(
                [sa[pl.ds(n * 256 + j, 32, stride=8), :] for n in range(3)], axis=1
            )
            right = jnp.concatenate(
                [sb[pl.ds(n * 320 + j, 40, stride=8), :] for n in range(3)], axis=1
            )
            left = jnp.concatenate(split_two(left), axis=0).astype(bf16)
            right = jnp.concatenate(split_two(right), axis=0).astype(bf16)
            both = lax.dot_general(
                left, right, (((1,), (1,)), ((), ())), preferred_element_type=f32
            )
            both = both[:32] + both[32:]
            sums.append(both[:, :40] + both[:, 40:])
        for j in range(8):
            b = g * 8 + j
            code = code_s[b]
            rank = cnt[code]
            cnt[code] = rank + 1
            stays = code == 4
            way = jnp.where(code > 4, code - 1, code)
            brick = brick_s[b]
            target = jnp.where(stays, brick, 128 + way * 16 + rank)
            mark = jnp.where(stays, 0, brick + 1).astype(f32)
            spot = pl.ds(pl.multiple_of(target * 32, 32), 32)
            acc[spot, 0:40] = acc[spot, 0:40] + (sums[j] + jnp.where(row_no == 30, mark, 0.0))
            at = jnp.where(stays, 8 * msg_rows, (way * msg_tiles + 9) * 16 + rank)
            for d in range(3):
                out[pl.ds(at + d * 16, 1), :] = raw[j * 40 + d : j * 40 + d + 1, :]
            out[pl.ds(at + 48, 1), :] = o_ref[pl.ds(b, 1), :].astype(f32)
        return carry

    lax.fori_loop(0, 16, group, 0)
    lane = lax.broadcasted_iota(jnp.int32, (8, 128), 1)

    def packed(chunk):
        total = [jnp.zeros((8, 128), f32) for _ in range(tiles)]
        for i in range(pieces):
            piece = acc[pl.ds(chunk * 256 + i, 8, stride=32), :]
            if i == 30:
                piece = jnp.where(lane < 36, piece, 0.0)
            tile, at = divmod(i * 36, 128)
            if at:
                piece = pltpu.roll(piece, at, 1)
            if at + 36 > 128:
                total[tile] = total[tile] + jnp.where(lane >= at, piece, 0.0)
                total[tile + 1] = total[tile + 1] + jnp.where(lane < at, piece, 0.0)
            else:
                total[tile] = total[tile] + piece
        return total

    def pack_own(chunk, carry):
        for tile, value in enumerate(packed(chunk)):
            own_ref[tile, pl.ds(pl.multiple_of(chunk * 8, 8), 8), :] = value
        return carry

    def pack_out(chunk, carry):
        base = (chunk // 2) * msg_rows + (chunk % 2) * 8
        for tile, value in enumerate(packed(chunk + 16)):
            out[pl.ds(pl.multiple_of(base + tile * 16, 8), 8), :] = value
        return carry

    lax.fori_loop(0, 16, pack_own, 0)
    lax.fori_loop(0, 16, pack_out, 0)
    xm_ref[...] = out[0 : 3 * msg_rows, :]
    ym_ref[...] = out[3 * msg_rows : 4 * msg_rows, :]
    yp_ref[...] = out[4 * msg_rows : 5 * msg_rows, :]
    xp_ref[...] = out[5 * msg_rows : 8 * msg_rows, :]


def runs_left():
    return (
        [(3, x, 0, 4) for x in range(2, 6)]
        + [(4, x, 0, 4) for x in range(2, 6)]
        + [(c, x, 0, 4) for c in range(3) for x in (4, 5)]
    )


def runs_below():
    return (
        [(3, x, 2, 4) for x in range(4)]
        + [(4, x, 2, 4) for x in range(4)]
        + [(c, x, 4, 2) for c in range(3) for x in range(4)]
    )


def runs_diagonal():
    return (
        [(3, x, 2, 4) for x in range(2, 6)]
        + [(4, x, 2, 4) for x in range(2, 6)]
        + [(c, x, 4, 2) for c in range(3) for x in (4, 5)]
    )


def runs_own():
    return [(c, x, 0, 4) for c in range(5) for x in range(4)]


def total_kernel(own_ref, rxp, rxm, ryp, rym, ml, mb, md, mo, brick_ref, wide, grid):
    places = [(ryp, 0), (rxp, 1), (rym, 0), (ryp, 1), (rym, 1), (ryp, 2), (rxm, 1), (rym, 2)]

    def arrived(tile):
        return jnp.concatenate(
            [ref[pl.ds((at * msg_tiles + tile) * 16, 16), :] for ref, at in places], axis=0
        )

    rows = lax.broadcasted_iota(jnp.int32, (128, 128), 0)
    lanes = lax.broadcasted_iota(jnp.int32, (128, 128), 1)
    column = arrived(8)[:, 56:57]
    row = jnp.sum(jnp.where(rows == lanes, column, 0.0), axis=0, keepdims=True)
    brick_ref[...] = row.astype(jnp.int32) - 1
    hits = (row == (rows + 1).astype(f32)).astype(f32).astype(bf16)
    hits = jnp.concatenate([hits, hits], axis=1)
    for tile in range(tiles):
        high, low = split_two(arrived(tile))
        stack = jnp.concatenate([high.astype(bf16), low.astype(bf16)], axis=0)
        value = own_ref[tile] + jnp.dot(hits, stack, preferred_element_type=f32)
        wide[tile * 128 : tile * 128 + 128, :] = jnp.transpose(value)
    lane = lax.broadcasted_iota(jnp.int32, (184, 128), 1)

    def layer(jz):
        return wide[pl.ds(jz, 184, stride=6), :]

    grid[0] = layer(1) + jnp.where(lane == 0, 0.0, pltpu.roll(layer(5), 1, 1))
    grid[1] = layer(2)
    grid[2] = layer(3)
    grid[3] = layer(4) + jnp.where(lane == 127, 0.0, pltpu.roll(layer(0), 127, 1))
    for ref, runs in ((ml, runs_left()), (mb, runs_below()), (md, runs_diagonal()), (mo, runs_own())):
        for kz in range(4):
            to = 0
            for c, x, y, count in runs:
                ref[kz, to : to + count, :] = grid[kz, c * 36 + x * 6 + y : c * 36 + x * 6 + y + count, :]
                to += count
            if to < ref.shape[1]:
                ref[kz, to:, :] = jnp.zeros((ref.shape[1] - to, 128), f32)


def static_kernel(
    table, solid_ref, rough_ref, choice_ref, rim_ref, own, ml, mb, md, cells
):
    for x in range(4):
        rows = slice(x * 4, x * 4 + 4)
        cells[rows, :] = solid_ref[x].astype(f32)
        cells[16 + x * 4 : 20 + x * 4, :] = rough_ref[x].astype(f32)
        cells[32 + x * 4 : 36 + x * 4, :] = choice_ref[x].astype(f32)
        cells[48 + x * 4 : 52 + x * 4, :] = rim_ref[x]
    value = cells[...]
    high, rest = split_two(value[48:64])
    middle, low = split_two(rest)
    value = jnp.concatenate([value[0:48], high, middle, low], axis=0).astype(bf16)
    source = lax.broadcasted_iota(jnp.int32, (512, 512), 0)
    wanted = (source % 4) * 128 + source // 4
    permute = (wanted == lax.broadcasted_iota(jnp.int32, (512, 512), 1)).astype(f32).astype(bf16)
    value = jnp.dot(value, permute, preferred_element_type=f32)
    rim = value[48:64] + value[64:80] + value[80:96]
    choice = value[32:48]
    normal = [jnp.zeros(choice.shape, f32) for _ in range(3)]
    for n in range(table.shape[1]):
        hit = choice == float(n)
        normal = [jnp.where(hit, table[d, n], normal[d]) for d in range(3)]
    for kz in range(4):
        lanes = slice(kz * 128, kz * 128 + 128)
        for field, part in enumerate((value[0:16], rim, value[16:32], *normal)):
            own[kz, field * 16 : field * 16 + 16, :] = part[:, lanes]
        ml[kz, 30:32, :] = jnp.zeros((2, 128), f32)
        mb[kz, 30:32, :] = jnp.zeros((2, 128), f32)
        md[kz, 22:24, :] = jnp.zeros((2, 128), f32)
        for field in range(2):
            for x in range(3):
                at = field * 9 + x * 3
                low_row, high_row = field * 16 + x * 4, field * 16 + x * 4 + 4
                ml[kz, at : at + 3, :] = own[kz, high_row : high_row + 3, :]
                mb[kz, at : at + 3, :] = own[kz, low_row + 1 : low_row + 4, :]
                md[kz, at : at + 3, :] = own[kz, high_row + 1 : high_row + 4, :]
        for field in range(4):
            row = field * 16 + 32
            ml[kz, 18 + field * 3 : 21 + field * 3, :] = own[kz, row + 12 : row + 15, :]
            for x in range(3):
                at = 18 + field * 3 + x
                mb[kz, at : at + 1, :] = own[kz, row + x * 4 + 3 : row + x * 4 + 4, :]
            md[kz, 18 + field : 19 + field, :] = own[kz, row + 15 : row + 16, :]


def update_kernel(
    mo, rl, rb, rd, own, sl, sb, sd, hl, hb, hd, ko, warm, push, region, rough, normal
):
    for kz in range(4):
        for field in range(2):
            to = 3 * field
            for x in range(3):
                at = field * 9 + x * 3
                inner, outer = x * 6, (x + 3) * 6
                row = field * 16 + x * 4
                region[to, kz, inner : inner + 3, :] = sd[kz, at : at + 3, :]
                region[to, kz, inner + 3 : inner + 6, :] = sl[kz, at : at + 3, :]
                region[to, kz, outer : outer + 3, :] = sb[kz, at : at + 3, :]
                region[to, kz, outer + 3 : outer + 6, :] = own[kz, row : row + 3, :]
        for field in range(4):
            ref = rough if field == 0 else normal.at[field - 1]
            at = 18 + field * 3
            row = 32 + field * 16
            ref[kz, 0:1, :] = sd[kz, 18 + field : 19 + field, :]
            ref[kz, 1:4, :] = sl[kz, at : at + 3, :]
            for x in range(3):
                to = (x + 1) * 4
                ref[kz, to : to + 1, :] = sb[kz, at + x : at + x + 1, :]
                ref[kz, to + 1 : to + 4, :] = own[kz, row + x * 4 : row + x * 4 + 3, :]
    warm[...] = jnp.zeros(warm.shape, f32)
    for kz in range(4):
        for ref, dx, dy in ((mo, 2, 2), (rl, 0, 2), (rb, 2, 0), (rd, 0, 0)):
            for c in range(2):
                for x in range(4):
                    at = (48 if ref is mo else 0) + c * 16 + x * 4
                    to = (x + dx) * 6 + dy
                    warm[c, kz, to : to + 4, :] = warm[c, kz, to : to + 4, :] + ref[kz, at : at + 4, :]
        for c in range(3):
            push[c, kz] = mo[kz, c * 16 : c * 16 + 16, :]
            push[c, kz, 0:8, :] = push[c, kz, 0:8, :] + rl[kz, 32 + c * 8 : 40 + c * 8, :]
            for x in range(4):
                at = 32 + c * 8 + x * 2
                push[c, kz, x * 4 : x * 4 + 2, :] = push[c, kz, x * 4 : x * 4 + 2, :] + rb[kz, at : at + 2, :]
            for x in range(2):
                at = 32 + c * 4 + x * 2
                push[c, kz, x * 4 : x * 4 + 2, :] = push[c, kz, x * 4 : x * 4 + 2, :] + rd[kz, at : at + 2, :]
        for x in range(4):
            for c in range(2):
                push[3 + c, kz, x * 4 : x * 4 + 4, :] = (
                    warm[0, kz, (x + 2) * 6 + 2 : (x + 2) * 6 + 6, :]
                    if c == 0
                    else region[0, kz, (x + 2) * 6 + 2 : (x + 2) * 6 + 6, :]
                )
    width_x = 4 * lax.axis_size("gx")
    height_z = 512
    spin = 2.0 / height_z
    shape = (16, 128)
    cell_x = lax.broadcasted_iota(jnp.int32, shape, 0) // 4 - 1 + 4 * lax.axis_index("gx")
    cell_x = jnp.where(cell_x < 0, cell_x + width_x, cell_x).astype(f32)
    wall_w = -spin * (cell_x + 0.5 - 0.5 * width_x)
    for kz in range(4):
        cell_z = (lax.broadcasted_iota(jnp.int32, shape, 1) * 4 + kz).astype(f32)
        wall = [spin * (cell_z + 0.5 - 0.5 * height_z), jnp.zeros(shape, f32), wall_w]
        inverse = 1.0 / jnp.maximum(push[3, kz], mass_floor)
        moving = [push[a, kz] * inverse for a in range(3)]
        moving[2] = moving[2] - gravity_step
        relative = [moving[a] - wall[a] for a in range(3)]
        facing = [normal[a, kz] for a in range(3)]
        normal_part = sum(relative[a] * facing[a] for a in range(3))
        tangent = [relative[a] - normal_part * facing[a] for a in range(3)]
        length = jnp.sqrt(sum(part * part for part in tangent))
        factor = jnp.maximum(
            0.0, 1.0 + friction * normal_part / jnp.maximum(length, slip_floor)
        )
        slips = (rough[kz] == 1.0) & (normal_part < 0.0)
        solid = push[4, kz] == 1.0
        for a in range(3):
            value = jnp.where(slips, wall[a] + tangent[a] * factor, moving[a])
            push[a, kz] = jnp.where(solid, wall[a], value)
        heat = warm[1, kz, 0:36, :] / jnp.maximum(warm[0, kz, 0:36, :], mass_floor)
        warm[1, kz, 0:36, :] = jnp.where(region[0, kz] == 1.0, region[3, kz], heat)
    for kz in range(4):
        ko[kz, 0:36, :] = warm[1, kz, 0:36, :]
        ko[kz, 36:40, :] = jnp.zeros((4, 128), f32)
        ko[kz, 88:124, :] = region[0, kz]
        ko[kz, 124:128, :] = jnp.zeros((4, 128), f32)
        hl[kz, 0:24, :] = warm[1, kz, 12:36, :]
        for c in range(3):
            ko[kz, 40 + c * 16 : 56 + c * 16, :] = push[c, kz]
            hl[kz, 24 + c * 8 : 32 + c * 8, :] = push[c, kz, 0:8, :]
            for x in range(4):
                at = 24 + c * 8 + x * 2
                hb[kz, at : at + 2, :] = push[c, kz, x * 4 : x * 4 + 2, :]
            for x in range(2):
                at = 16 + c * 4 + x * 2
                hd[kz, at : at + 2, :] = push[c, kz, x * 4 : x * 4 + 2, :]
        for x in range(6):
            hb[kz, x * 4 : x * 4 + 4, :] = warm[1, kz, x * 6 + 2 : x * 6 + 6, :]
        for x in range(4):
            hd[kz, x * 4 : x * 4 + 4, :] = warm[1, kz, (x + 2) * 6 + 2 : (x + 2) * 6 + 6, :]
        for x in range(3):
            row = (x + 2) * 6
            hl[kz, 48 + x * 5 : 53 + x * 5, :] = region[0, kz, row + 1 : row + 6, :]
            hd[kz, 28 + x * 3 : 31 + x * 3, :] = region[0, kz, row + 2 : row + 5, :]
        for x in range(5):
            row = (x + 1) * 6
            hb[kz, 48 + x * 3 : 51 + x * 3, :] = region[0, kz, row + 2 : row + 5, :]
        hl[kz, 63:64, :] = jnp.zeros((1, 128), f32)
        hb[kz, 63:64, :] = jnp.zeros((1, 128), f32)
        hd[kz, 37:40, :] = jnp.zeros((3, 128), f32)


def collect_kernel(
    code_s, brick_s, came_s, ko, rl, rb, rd, frac, o_ref, rxp, rxm, ryp, rym,
    move_ref, grad_ref, warm_ref, gvel_ref, gtemp_ref,
    heat, solid, speed, cells, fine, coarse, turn, lu, fo, sb, sw,
):
    lane = lax.broadcasted_iota(jnp.int32, (8, 128), 1)[0:1]
    heat[...] = jnp.zeros(heat.shape, f32)
    solid[...] = jnp.zeros(solid.shape, f32)
    for kz in range(4):
        for x in range(6):
            to = 16 + x * 10
            heat[0, kz, to : to + 6, :] = ko[kz, x * 6 : x * 6 + 6, :]
            heat[0, kz, to + 6 : to + 10, :] = rb[kz, x * 4 : x * 4 + 4, :]
            solid[kz, x * 10 : x * 10 + 6, :] = ko[kz, 88 + x * 6 : 94 + x * 6, :]
        for x in range(4):
            to = 16 + (x + 6) * 10
            heat[0, kz, to : to + 6, :] = rl[kz, x * 6 : x * 6 + 6, :]
            heat[0, kz, to + 6 : to + 10, :] = rd[kz, x * 4 : x * 4 + 4, :]
        for x in range(3):
            to = (x + 6) * 10
            solid[kz, to + 1 : to + 6, :] = rl[kz, 48 + x * 5 : 53 + x * 5, :]
            solid[kz, to + 6 : to + 9, :] = rd[kz, 28 + x * 3 : 31 + x * 3, :]
        for x in range(5):
            to = (x + 1) * 10
            solid[kz, to + 6 : to + 9, :] = rb[kz, 48 + x * 3 : 51 + x * 3, :]
        for c in range(3):
            for x in range(4):
                speed[c, kz, x * 6 : x * 6 + 4, :] = ko[kz, 40 + c * 16 + x * 4 : 44 + c * 16 + x * 4, :]
                at = 24 + c * 8 + x * 2
                speed[c, kz, x * 6 + 4 : x * 6 + 6, :] = rb[kz, at : at + 2, :]
            for x in range(2):
                at = 24 + c * 8 + x * 4
                speed[c, kz, 24 + x * 6 : 28 + x * 6, :] = rl[kz, at : at + 4, :]
                at = 16 + c * 4 + x * 2
                speed[c, kz, 28 + x * 6 : 30 + x * 6, :] = rd[kz, at : at + 2, :]
    for sweep in range(2):
        now, later = sweep, sweep + 1
        layers = [heat[now, kz, 16:120, :] for kz in range(4)]
        above = jnp.where(lane == 127, layers[3], pltpu.roll(layers[0], 127, 1))
        below = jnp.where(lane == 0, layers[0], pltpu.roll(layers[3], 1, 1))
        for kz in range(4):
            upper = layers[kz + 1] if kz < 3 else above
            lower = layers[kz - 1] if kz else below
            laplace = (
                heat[now, kz, 6:110, :]
                + heat[now, kz, 26:130, :]
                + heat[now, kz, 15:119, :]
                + heat[now, kz, 17:121, :]
                + upper
                + lower
                - 6.0 * layers[kz]
            )
            heat[later, kz, 16:120, :] = jnp.where(
                solid[kz] == 1.0, heat[0, kz, 16:120, :], layers[kz] + conduct * laplace
            )
    for kz in range(4):
        for x in range(6):
            to = 16 + (x + 2) * 10 + 2
            speed[3, kz, x * 6 : x * 6 + 6, :] = heat[2, kz, to : to + 6, :]
    for c in range(4):
        for kz in range(4):
            for x in range(4):
                at = (x + 1) * 6 + 1
                cells[c * 16 + x * 4 : c * 16 + x * 4 + 4, kz * 128 : kz * 128 + 128] = speed[c, kz, at : at + 4, :]
    source = lax.broadcasted_iota(jnp.int32, (512, 512), 0)
    wanted = (source % 128) * 4 + source // 128
    permute = (wanted == lax.broadcasted_iota(jnp.int32, (512, 512), 1)).astype(f32).astype(bf16)
    value = cells[...]
    high, rest = split_two(value)
    middle, low = split_two(rest)
    spread = jnp.concatenate([high, middle, low], axis=0).astype(bf16)
    spread = jnp.dot(spread, permute, preferred_element_type=f32)
    value = spread[0:64] + spread[64:128] + spread[128:192]
    for x in range(4):
        for c in range(3):
            gvel_ref[c, x] = value[c * 16 + x * 4 : c * 16 + x * 4 + 4]
        gtemp_ref[x] = value[48 + x * 4 : 52 + x * 4]
    for c in range(4):
        for jz in range(6):
            kz = (jz - 1) % 4
            layer = speed[c, kz]
            if jz == 0:
                layer = jnp.where(lane == 0, 0.0, pltpu.roll(layer, 1, 1))
            if jz == 5:
                layer = jnp.where(lane == 127, 0.0, pltpu.roll(layer, 127, 1))
            high, low = split_two(layer)
            coarse[c, jz] = high
            fine[c, jz] = low
    turn[...] = jnp.zeros(turn.shape, f32)
    for jx in range(6):
        for c in range(4):
            side = c % 2
            for jz in range(6):
                rows = slice(jx * 6, jx * 6 + 6)
                turn[side, jz * 6 : jz * 6 + 6, :] = coarse[c, jz, rows, :]
                turn[side, 40 + jz * 6 : 46 + jz * 6, :] = fine[c, jz, rows, :]
                turn[side, 80 + jz * 6 : 86 + jz * 6, :] = coarse[c, jz, rows, :]
            lu[pl.ds(jx * 4 + c, 128, stride=24), :] = jnp.transpose(turn[side])
    for d in range(3):
        fo[d, 0:128, :] = frac[d]
    fo[3, 0:128, :] = o_ref[...].astype(f32)
    places = [(ryp, 0), (rxp, 1), (rym, 0), (ryp, 1), (rym, 1), (ryp, 2), (rxm, 1), (rym, 2)]
    for g, (ref, at) in enumerate(places):
        for d in range(4):
            fo[d, 128 + g * 16 : 144 + g * 16, :] = ref[pl.ds((at * msg_tiles + 9 + d) * 16, 16), :]
    sb[...] = jnp.zeros(sb.shape, f32)

    def group(g, carry):
        rows = pl.ds(pl.multiple_of(g * 8, 8), 8)
        offset = fo[3, rows, :].astype(jnp.int32)
        wx, rx = axis_tables(offset >> 4, fo[0, rows, :], 4.0)
        for j in range(6):
            for copy in range(4):
                sw[pl.ds((j * 4 + copy) * 8, 8), :] = wx[j]
                sw[pl.ds((24 + j * 4 + copy) * 8, 8), :] = rx[j]
        wy, ry = axis_tables((offset >> 2) & 3, fo[1, rows, :], 4.0)
        wz, rz = axis_tables(offset & 3, fo[2, rows, :], 4.0)
        for jz in range(6):
            for jy in range(6):
                r = jz * 6 + jy
                sb[pl.ds(r * 8, 8), :] = wy[jy] * wz[jz]
                sb[pl.ds((40 + r) * 8, 8), :] = ry[jy] * wz[jz]
                sb[pl.ds((80 + r) * 8, 8), :] = wy[jy] * rz[jz]
        for j in range(8):
            slot = g * 8 + j
            home = jnp.minimum(slot, 127)
            stays = jnp.where(code_s[home] == 4, brick_s[home], -1)
            brick = jnp.where(slot < 128, stays, came_s[0, jnp.maximum(slot - 128, 0)])
            live = jnp.where(brick >= 0, 1.0, 0.0).astype(f32)
            spot = pl.ds(pl.multiple_of(jnp.maximum(brick, 0) * 24, 8), 24)
            left = lu[spot, :].astype(bf16)
            right = jnp.concatenate(
                [sb[pl.ds(n * 320 + j, 40, stride=8), :] for n in range(3)], axis=1
            )
            high, low = split_two(right)
            right = jnp.concatenate([high, high, low, jnp.zeros((8, 384), f32)], axis=0).astype(bf16)
            both = jnp.dot(left, right, preferred_element_type=f32)
            plain = sw[pl.ds(j, 24, stride=8), :]
            tilt = sw[pl.ds(192 + j, 24, stride=8), :]

            def over_x(weight, column):
                part = weight * both[:, column * 128 : column * 128 + 128]
                part = part[0:8] + part[8:16] + part[16:24]
                return (part[0:4] + part[4:8]) * live

            lanes = pl.ds(pl.multiple_of(slot * 128, 128), 128)
            moved = over_x(plain, 0)
            move_ref[:, lanes] = moved[0:3]
            warm_ref[pl.ds(slot, 1), :] = moved[3:4]
            for k, (weight, column) in enumerate(((tilt, 0), (plain, 1), (plain, 2))):
                part = over_x(weight, column)
                for a in range(3):
                    grad_ref[a * 3 + k : a * 3 + k + 1, lanes] = part[a : a + 1]
        return carry

    lax.fori_loop(0, 32, group, 0)


def neighbor(value, dx, dy):
    size_x, size_y = lax.axis_size("gx"), lax.axis_size("gy")
    if dy == 0:
        return lax.ppermute(value, "gx", [(i, (i + dx) % size_x) for i in range(size_x)])
    if dx == 0:
        return lax.ppermute(value, "gy", [(i, (i + dy) % size_y) for i in range(size_y)])
    pairs = [
        (i * size_y + j, (i + dx) % size_x * size_y + (j + dy) % size_y)
        for i in range(size_x)
        for j in range(size_y)
    ]
    return lax.ppermute(value, ("gx", "gy"), pairs)


def call(kernel, name, inputs, scalars, outputs, scratch, left_there=0, limit=50):
    in_specs = (
        [pl.BlockSpec(memory_space=pltpu.SMEM)] * scalars
        + [pl.BlockSpec(memory_space=pltpu.HBM)] * left_there
        + [pl.BlockSpec(memory_space=pltpu.VMEM)] * (len(inputs) - scalars - left_there)
    )
    return pl.pallas_call(
        kernel,
        name=name,
        out_shape=[jax.ShapeDtypeStruct(shape, dtype) for shape, dtype in outputs],
        in_specs=in_specs,
        out_specs=[pl.BlockSpec(memory_space=pltpu.VMEM)] * len(outputs),
        scratch_shapes=scratch,
        compiler_params=pltpu.CompilerParams(vmem_limit_bytes=limit * mib),
    )(*inputs)


def vmem(*shape):
    return pltpu.VMEM(shape, f32)


def on_device(
    subvoxel_location_share,
    point_motion_vector,
    linear_gradient_matrix,
    kirchhoff_tension_matrix,
    point_inertia_amounts,
    point_thermal_state,
    anchor_voxel_shift,
    group_resting_volume,
    group_migration_label,
    cylinder_shell_flag,
    rough_surface_flag,
    voxel_facing_choice,
    facing_unit_vectors,
    rim_thermal_level,
):
    offset = anchor_voxel_shift.reshape(128, 128)
    own, frac, xm, ym, yp, xp = call(
        deposit_kernel,
        "deposit",
        (
            group_migration_label,
            group_resting_volume,
            subvoxel_location_share,
            point_motion_vector,
            linear_gradient_matrix,
            kirchhoff_tension_matrix,
            point_inertia_amounts.reshape(128, 128),
            point_thermal_state.reshape(128, 128),
            offset,
        ),
        2,
        [
            ((tiles, 128, 128), f32),
            ((3, 128, 128), f32),
            ((3 * msg_rows, 128), f32),
            ((msg_rows, 128), f32),
            ((msg_rows, 128), f32),
            ((3 * msg_rows, 128), f32),
        ],
        [
            vmem(3, 16384),
            vmem(3, 16384),
            vmem(9, 16384),
            vmem(9, 16384),
            vmem(128, 128),
            vmem(128, 128),
            pltpu.VMEM((128, 128), jnp.int32),
            pltpu.SemaphoreType.DMA((7,)),
            vmem(320, 128),
            vmem(96 * 8, 128),
            vmem(120 * 8, 128),
            vmem(256 * 32, 128),
            pltpu.SMEM((16,), jnp.int32),
            vmem(8 * msg_rows + 64, 128),
        ],
        7,
        64,
    )
    rxp = neighbor(xp, 1, 0)
    rxm = neighbor(xm, -1, 0)
    ryp = neighbor(
        jnp.concatenate([rxp[2 * msg_rows :], yp, rxm[2 * msg_rows :]], axis=0), 0, 1
    )
    rym = neighbor(jnp.concatenate([rxp[:msg_rows], ym, rxm[:msg_rows]], axis=0), 0, -1)

    static, sl, sb, sd = call(
        static_kernel,
        "static",
        (
            facing_unit_vectors,
            cylinder_shell_flag,
            rough_surface_flag,
            voxel_facing_choice,
            rim_thermal_level,
        ),
        1,
        [
            ((4, 96, 128), f32),
            ((4, 32, 128), f32),
            ((4, 32, 128), f32),
            ((4, 24, 128), f32),
        ],
        [vmem(64, 512)],
    )
    sl, sb, sd = neighbor(sl, 1, 0), neighbor(sb, 0, 1), neighbor(sd, 1, 1)

    ml, mb, md, mo, came = call(
        total_kernel,
        "total",
        (own, rxp, rxm, ryp, rym),
        0,
        [
            ((4, 56, 128), f32),
            ((4, 56, 128), f32),
            ((4, 48, 128), f32),
            ((4, 80, 128), f32),
            ((1, 128), jnp.int32),
        ],
        [vmem(tiles * 128, 128), vmem(4, 184, 128)],
    )
    hl, hb, hd, ko = call(
        update_kernel,
        "update",
        (mo, neighbor(ml, 1, 0), neighbor(mb, 0, 1), neighbor(md, 1, 1), static, sl, sb, sd),
        0,
        [
            ((4, 64, 128), f32),
            ((4, 64, 128), f32),
            ((4, 40, 128), f32),
            ((4, 128, 128), f32),
        ],
        [
            vmem(2, 4, 40, 128),
            vmem(5, 4, 16, 128),
            vmem(4, 4, 36, 128),
            vmem(4, 16, 128),
            vmem(3, 4, 16, 128),
        ],
    )
    move, grad, warm, gvel, gtemp = call(
        collect_kernel,
        "collect",
        (
            group_migration_label,
            group_resting_volume,
            came,
            ko,
            neighbor(hl, -1, 0),
            neighbor(hb, 0, -1),
            neighbor(hd, -1, -1),
            frac,
            offset,
            rxp,
            rxm,
            ryp,
            rym,
        ),
        3,
        [
            ((3, 32768), f32),
            ((9, 32768), f32),
            ((256, 128), f32),
            ((3, 4, 4, 512), f32),
            ((4, 4, 512), f32),
        ],
        [
            vmem(3, 4, 136, 128),
            vmem(4, 104, 128),
            vmem(4, 4, 40, 128),
            vmem(64, 512),
            vmem(4, 6, 40, 128),
            vmem(4, 6, 40, 128),
            vmem(2, 128, 128),
            vmem(128 * 24, 128),
            vmem(4, 256, 128),
            vmem(120 * 8, 128),
            vmem(48 * 8, 128),
        ],
    )
    return move, grad, warm.reshape(-1), gvel, gtemp


def solution(mesh):
    in_specs = (
        P(None, ("gx", "gy")),
        P(None, ("gx", "gy")),
        P(None, ("gx", "gy")),
        P(None, ("gx", "gy")),
        P(("gx", "gy")),
        P(("gx", "gy")),
        P(("gx", "gy")),
        P(("gx", "gy")),
        P(("gx", "gy")),
        P("gx", "gy", None),
        P("gx", "gy", None),
        P("gx", "gy", None),
        P(),
        P("gx", "gy", None),
    )
    out_specs = (
        P(None, ("gx", "gy")),
        P(None, ("gx", "gy")),
        P(("gx", "gy")),
        P(None, "gx", "gy", None),
        P("gx", "gy", None),
    )
    return jax.shard_map(
        on_device, mesh=mesh, in_specs=in_specs, out_specs=out_specs, check_vma=False
    )
```

```python
import jax
import jax.numpy as jnp
from jax import lax
from jax.experimental import pallas as pl
from jax.experimental.pallas import tpu as pltpu
from jax.sharding import PartitionSpec as P

f32 = jnp.float32
bf16 = jnp.bfloat16
mass_floor = 0.25
slip_floor = 0.1
friction = 0.4
gravity_step = 0.5
conduct = 0.15
stress_coef = 0.25
mib = 1024 * 1024
pieces = 31
tiles = 9
msg_rows = tiles * 16
way_rows = 64


def axis_tables(shift, inside, scale):
    near = 0.5 * (1.5 - inside) ** 2
    middle = 0.75 - (inside - 1.0) ** 2
    far = 0.5 * (inside - 0.5) ** 2
    at = [shift == step for step in range(4)]
    zero = jnp.zeros_like(inside)
    weight = [
        jnp.where(at[0], near, zero),
        jnp.where(at[0], middle, jnp.where(at[1], near, zero)),
        jnp.where(at[0], far, jnp.where(at[1], middle, jnp.where(at[2], near, zero))),
        jnp.where(at[1], far, jnp.where(at[2], middle, jnp.where(at[3], near, zero))),
        jnp.where(at[2], far, jnp.where(at[3], middle, zero)),
        jnp.where(at[3], far, zero),
    ]
    place = shift.astype(f32) + inside
    first = [weight[step] * (scale * (step - place)) for step in range(6)]
    return weight, first


def split_two(value):
    high = value.astype(bf16).astype(f32)
    return high, value - high


def clear_rows(ref, rows):
    def step(n, carry):
        ref[pl.ds(pl.multiple_of(n * 128, 128), 128), :] = jnp.zeros((128, 128), f32)
        return carry

    lax.fori_loop(0, rows // 128, step, 0)


def deposit_blocks(
    base, count, info_s, brick_s, target_of, hbm_refs, vmem_refs, sems, first, second, acc, after
):
    copies = [
        pltpu.make_async_copy(a, b, sems.at[n]) for n, (a, b) in enumerate(zip(hbm_refs, vmem_refs))
    ]
    for copy in copies:
        copy.start()
    f_ref, v_ref, c_ref, k_ref, m_ref, t_ref, o_ref = vmem_refs
    clear_rows(acc, 128 * 32)
    for _, sa, sb in (first, second):
        sa[...] = jnp.zeros(sa.shape, f32)
        sb[...] = jnp.zeros(sb.shape, f32)
    for copy in copies:
        copy.wait()
    row_no = lax.broadcasted_iota(jnp.int32, (32, 1), 0)

    def build(g, raw, sa, sb):
        blocks = [info_s[base + g * 8 + j] for j in range(8)]
        for j in range(8):
            lanes = pl.ds(pl.multiple_of(blocks[j] * 128, 128), 128)
            raw[j * 40 : j * 40 + 3, :] = f_ref[:, lanes]
            raw[j * 40 + 3 : j * 40 + 6, :] = v_ref[:, lanes]
            raw[j * 40 + 6 : j * 40 + 7, :] = m_ref[pl.ds(blocks[j], 1), :]
            raw[j * 40 + 7 : j * 40 + 8, :] = t_ref[pl.ds(blocks[j], 1), :]
            raw[j * 40 + 8 : j * 40 + 17, :] = c_ref[:, lanes]
            raw[j * 40 + 24 : j * 40 + 33, :] = k_ref[:, lanes]
            raw[j * 40 + 33 : j * 40 + 34, :] = o_ref[pl.ds(blocks[j], 1), :].astype(f32)

        def get(row):
            return raw[pl.ds(row, 8, stride=40), :]

        mass = get(6)
        heat = mass * get(7)
        offset = get(33).astype(jnp.int32)
        inside = [get(d) for d in range(3)]
        wx, rx = axis_tables(offset >> 4, inside[0], 1.0)
        for a in range(3):
            push = mass * get(3 + a)
            q = [
                mass * get(8 + a * 3 + k) - stress_coef * get(24 + a * 3 + k) for k in range(3)
            ]
            for j in range(6):
                sa[pl.ds((a * 6 + j) * 8, 8), :] = push * wx[j] + q[0] * rx[j]
                sa[pl.ds((32 + a * 6 + j) * 8, 8), :] = q[1] * wx[j]
                sa[pl.ds((64 + a * 6 + j) * 8, 8), :] = q[2] * wx[j]
        for j in range(6):
            sa[pl.ds((18 + j) * 8, 8), :] = mass * wx[j]
            sa[pl.ds((24 + j) * 8, 8), :] = heat * wx[j]
        wy, ry = axis_tables((offset >> 2) & 3, inside[1], 1.0)
        wz, rz = axis_tables(offset & 3, inside[2], 1.0)
        for jy in range(6):
            for jz in range(6):
                r = jy * 6 + jz
                sb[pl.ds(r * 8, 8), :] = wy[jy] * wz[jz]
                sb[pl.ds((40 + r) * 8, 8), :] = ry[jy] * wz[jz]
                sb[pl.ds((80 + r) * 8, 8), :] = wy[jy] * rz[jz]

    def work(g, raw, sa, sb):
        blocks = [info_s[base + g * 8 + j] for j in range(8)]
        sums = []
        for j in range(8):
            left = jnp.concatenate(
                [sa[pl.ds(n * 256 + j, 32, stride=8), :] for n in range(3)], axis=1
            )
            right = jnp.concatenate(
                [sb[pl.ds(n * 320 + j, 40, stride=8), :] for n in range(3)], axis=1
            )
            left = jnp.concatenate(split_two(left), axis=0).astype(bf16)
            right = jnp.concatenate(split_two(right), axis=0).astype(bf16)
            both = lax.dot_general(
                left, right, (((1,), (1,)), ((), ())), preferred_element_type=f32
            )
            both = both[:32] + both[32:]
            sums.append(both[:, :40] + both[:, 40:])
        for j in range(8):
            target, mark = target_of(g * 8 + j, blocks[j])
            spot = pl.ds(pl.multiple_of(target * 32, 32), 32)
            acc[spot, 0:40] = acc[spot, 0:40] + (sums[j] + jnp.where(row_no == 30, mark, 0.0))
            after(j, blocks[j], raw)

    def pair(i, carry):
        build(2 * i + 1, *second)
        work(2 * i, *first)
        build(2 * i + 2, *first)
        work(2 * i + 1, *second)
        return carry

    build(0, *first)
    lax.fori_loop(0, (count + 15) // 16, pair, 0)


def packed(acc, chunk):
    lane = lax.broadcasted_iota(jnp.int32, (8, 128), 1)
    total = [jnp.zeros((8, 128), f32) for _ in range(tiles)]
    for i in range(pieces):
        piece = acc[pl.ds(chunk * 256 + i, 8, stride=32), :]
        if i == 30:
            piece = jnp.where(lane < 36, piece, 0.0)
        tile, at = divmod(i * 36, 128)
        if at:
            piece = pltpu.roll(piece, at, 1)
        if at + 36 > 128:
            total[tile] = total[tile] + jnp.where(lane >= at, piece, 0.0)
            total[tile + 1] = total[tile + 1] + jnp.where(lane < at, piece, 0.0)
        else:
            total[tile] = total[tile] + piece
    return total


def outgoing_kernel(
    info_s, brick_s, f_hbm, v_hbm, c_hbm, k_hbm, m_hbm, t_hbm, o_hbm,
    xm_ref, ym_ref, yp_ref, xp_ref,
    f_ref, v_ref, c_ref, k_ref, m_ref, t_ref, o_ref, sems, raw, sa, sb, raw2, sa2, sb2, acc,
):
    def target_of(entry, block):
        return info_s[160 + entry], (brick_s[block] + 1).astype(f32)

    deposit_blocks(
        0, info_s[544], info_s, brick_s, target_of,
        (f_hbm, v_hbm, c_hbm, k_hbm, m_hbm, t_hbm, o_hbm),
        (f_ref, v_ref, c_ref, k_ref, m_ref, t_ref, o_ref),
        sems, (raw, sa, sb), (raw2, sa2, sb2), acc, lambda j, block, raw: None,
    )
    for first, count, ref in ((0, 3, xm_ref), (3, 1, ym_ref), (4, 1, yp_ref), (5, 3, xp_ref)):
        for n in range(count):
            for half in range(2):

                def some(n=n, half=half, first=first, ref=ref):
                    for tile, value in enumerate(packed(acc, (first + n) * 2 + half)):
                        at = n * msg_rows + tile * 16 + half * 8
                        ref[at : at + 8, :] = value

                def none(n=n, half=half, ref=ref):
                    for tile in range(tiles):
                        at = n * msg_rows + tile * 16 + half * 8
                        ref[at : at + 8, :] = jnp.zeros((8, 128), f32)

                lax.cond(info_s[552 + first + n] > half * 8, some, none)


def staying_kernel(
    info_s, brick_s, f_hbm, v_hbm, c_hbm, k_hbm, m_hbm, t_hbm, o_hbm,
    own_ref, frac_ref,
    f_ref, v_ref, c_ref, k_ref, m_ref, t_ref, o_ref, sems, raw, sa, sb, raw2, sa2, sb2, acc,
):
    frac_ref[...] = jnp.zeros(frac_ref.shape, f32)

    def target_of(entry, block):
        return jnp.where(entry < info_s[545], brick_s[block], 128), jnp.float32(0.0)

    def after(j, block, raw):
        for d in range(3):
            frac_ref[d, pl.ds(block, 1), :] = raw[j * 40 + d : j * 40 + d + 1, :]

    deposit_blocks(
        320, info_s[545], info_s, brick_s, target_of,
        (f_hbm, v_hbm, c_hbm, k_hbm, m_hbm, t_hbm, o_hbm),
        (f_ref, v_ref, c_ref, k_ref, m_ref, t_ref, o_ref),
        sems, (raw, sa, sb), (raw2, sa2, sb2), acc, after,
    )

    def pack_own(chunk, carry):
        for tile, value in enumerate(packed(acc, chunk)):
            own_ref[tile, pl.ds(pl.multiple_of(chunk * 8, 8), 8), :] = value
        return carry

    lax.fori_loop(0, 16, pack_own, 0)


def runs_left():
    return (
        [(3, x, 0, 4) for x in range(2, 6)]
        + [(4, x, 0, 4) for x in range(2, 6)]
        + [(c, x, 0, 4) for c in range(3) for x in (4, 5)]
    )


def runs_below():
    return (
        [(3, x, 2, 4) for x in range(4)]
        + [(4, x, 2, 4) for x in range(4)]
        + [(c, x, 4, 2) for c in range(3) for x in range(4)]
    )


def runs_diagonal():
    return (
        [(3, x, 2, 4) for x in range(2, 6)]
        + [(4, x, 2, 4) for x in range(2, 6)]
        + [(c, x, 4, 2) for c in range(3) for x in (4, 5)]
    )


def runs_own():
    return [(c, x, 0, 4) for c in range(5) for x in range(4)]


def total_kernel(own_ref, rxp, rxm, ryp, rym, ml, mb, md, mo, brick_ref, wide, grid):
    places = [(ryp, 0), (rxp, 1), (rym, 0), (ryp, 1), (rym, 1), (ryp, 2), (rxm, 1), (rym, 2)]

    def arrived(tile):
        return jnp.concatenate(
            [ref[pl.ds(at * msg_rows + tile * 16, 16), :] for ref, at in places], axis=0
        )

    rows = lax.broadcasted_iota(jnp.int32, (128, 128), 0)
    lanes = lax.broadcasted_iota(jnp.int32, (128, 128), 1)
    column = arrived(8)[:, 56:57]
    row = jnp.sum(jnp.where(rows == lanes, column, 0.0), axis=0, keepdims=True)
    brick_ref[...] = row.astype(jnp.int32) - 1
    hits = (row == (rows + 1).astype(f32)).astype(f32).astype(bf16)
    hits = jnp.concatenate([hits, hits], axis=1)
    for tile in range(tiles):
        high, low = split_two(arrived(tile))
        stack = jnp.concatenate([high.astype(bf16), low.astype(bf16)], axis=0)
        value = own_ref[tile] + jnp.dot(hits, stack, preferred_element_type=f32)
        wide[tile * 128 : tile * 128 + 128, :] = jnp.transpose(value)
    lane = lax.broadcasted_iota(jnp.int32, (184, 128), 1)

    def layer(jz):
        return wide[pl.ds(jz, 184, stride=6), :]

    grid[0] = layer(1) + jnp.where(lane == 0, 0.0, pltpu.roll(layer(5), 1, 1))
    grid[1] = layer(2)
    grid[2] = layer(3)
    grid[3] = layer(4) + jnp.where(lane == 127, 0.0, pltpu.roll(layer(0), 127, 1))
    for ref, runs in ((ml, runs_left()), (mb, runs_below()), (md, runs_diagonal()), (mo, runs_own())):
        for kz in range(4):
            to = 0
            for c, x, y, count in runs:
                ref[kz, to : to + count, :] = grid[kz, c * 36 + x * 6 + y : c * 36 + x * 6 + y + count, :]
                to += count
            if to < ref.shape[1]:
                ref[kz, to:, :] = jnp.zeros((ref.shape[1] - to, 128), f32)


def prepare_kernel(
    table, code_s, solid_ref, rough_ref, choice_ref, rim_ref, f_ref, o_ref,
    info, own, xp, xm, cells, fo, cnt,
):
    fo[...] = jnp.zeros(fo.shape, f32)
    for n in range(10):
        cnt[n] = 0

    def sort(b, carry):
        code = code_s[b]
        rank = cnt[code]
        cnt[code] = rank + 1
        leaves = code != 4
        way = jnp.where(code > 4, code - 1, code)
        gone = cnt[9]
        slot = way * 16 + rank
        info[jnp.where(leaves, gone, 320 + b - gone)] = b
        info[jnp.where(leaves, 160 + gone, 639)] = slot
        cnt[9] = gone + jnp.where(leaves, 1, 0)
        at = pl.multiple_of(jnp.where(leaves, slot, 128) * 4, 4)
        lanes = pl.ds(pl.multiple_of(b * 128, 128), 128)
        fo[pl.ds(at, 3), :] = f_ref[:, lanes]
        fo[pl.ds(at + 3, 1), :] = o_ref[pl.ds(b, 1), :].astype(f32)
        return carry

    lax.fori_loop(0, 128, sort, 0, unroll=4)
    gone = cnt[9]
    for n in range(24):
        info[gone + n] = 0
        info[160 + gone + n] = 128
        info[320 + 128 - gone + n] = 0
    for n in range(8):
        info[552 + n] = cnt[n if n < 4 else n + 1]
    info[544] = gone
    info[545] = 128 - gone
    for x in range(4):
        rows = slice(x * 4, x * 4 + 4)
        cells[rows, :] = solid_ref[x].astype(f32)
        cells[16 + x * 4 : 20 + x * 4, :] = rough_ref[x].astype(f32)
        cells[32 + x * 4 : 36 + x * 4, :] = choice_ref[x].astype(f32)
        cells[48 + x * 4 : 52 + x * 4, :] = rim_ref[x]
    value = cells[...]
    high, rest = split_two(value[48:64])
    middle, low = split_two(rest)
    value = jnp.concatenate([value[0:48], high, middle, low], axis=0).astype(bf16)
    source = lax.broadcasted_iota(jnp.int32, (512, 512), 0)
    wanted = (source % 4) * 128 + source // 4
    permute = (wanted == lax.broadcasted_iota(jnp.int32, (512, 512), 1)).astype(f32).astype(bf16)
    value = jnp.dot(value, permute, preferred_element_type=f32)
    rim = value[48:64] + value[64:80] + value[80:96]
    choice = value[32:48]
    normal = [jnp.zeros(choice.shape, f32) for _ in range(3)]
    for n in range(table.shape[1]):
        hit = choice == float(n)
        normal = [jnp.where(hit, table[d, n], normal[d]) for d in range(3)]
    for kz in range(4):
        lanes = slice(kz * 128, kz * 128 + 128)
        for field, part in enumerate((value[0:16], rim, value[16:32], *normal)):
            own[kz, field * 16 : field * 16 + 16, :] = part[:, lanes]
        at = 192 + kz * 40
        xp[at : at + 12, :] = own[kz, 4:16, :]
        xp[at + 12 : at + 24, :] = own[kz, 20:32, :]
        for field in range(4):
            row = 32 + field * 16
            xp[at + 24 + field * 4 : at + 28 + field * 4, :] = own[kz, row + 12 : row + 16, :]
        xm[192 + kz * 8 : 200 + kz * 8, :] = own[kz, 0:8, :]
    xm[0:192, :] = fo[0:192, :]
    for way in range(2):
        own[4 + way, 0:64, :] = fo[192 + way * 64 : 256 + way * 64, :]
        own[4 + way, 64:96, :] = jnp.zeros((32, 128), f32)
    xp[0:192, :] = fo[320:512, :]


def relay_kernel(left, right, own, up, down):
    for way, ref in ((0, down), (1, up)):
        at = 128 * way
        ref[0:64, :] = left[at : at + 64, :]
        ref[64:128, :] = own[4 + way, 0:64, :]
        ref[128:192, :] = right[at : at + 64, :]
    for kz in range(4):
        lrow, rrow = 192 + kz * 40, 192 + kz * 8
        to = 192 + kz * 64
        for x in range(4):
            up[to + x * 3 : to + x * 3 + 3, :] = own[kz, x * 4 + 1 : x * 4 + 4, :]
        for x in range(3):
            row = 16 + x * 4
            up[to + 12 + x * 3 : to + 15 + x * 3, :] = own[kz, row + 1 : row + 4, :]
            up[to + 33 + x * 3 : to + 36 + x * 3, :] = left[lrow + x * 4 + 1 : lrow + x * 4 + 4, :]
            row = lrow + 12 + x * 4
            up[to + 42 + x * 3 : to + 45 + x * 3, :] = left[row + 1 : row + 4, :]
            for field in range(4):
                row = 32 + field * 16 + x * 4 + 3
                at = to + 21 + field * 3 + x
                up[at : at + 1, :] = own[kz, row : row + 1, :]
        for field in range(4):
            row = lrow + 24 + field * 4 + 3
            up[to + 51 + field : to + 52 + field, :] = left[row : row + 1, :]
        for x in range(2):
            up[to + 55 + x * 3 : to + 58 + x * 3, :] = right[rrow + x * 4 + 1 : rrow + x * 4 + 4, :]
        up[to + 61 : to + 64, :] = jnp.zeros((3, 128), f32)
        to = 192 + kz * 24
        for x in range(4):
            down[to + x * 2 : to + x * 2 + 2, :] = own[kz, x * 4 : x * 4 + 2, :]
        for x in range(3):
            down[to + 8 + x * 2 : to + 10 + x * 2, :] = left[lrow + x * 4 : lrow + x * 4 + 2, :]
        for x in range(2):
            down[to + 14 + x * 2 : to + 16 + x * 2, :] = right[rrow + x * 4 : rrow + x * 4 + 2, :]
        down[to + 18 : to + 24, :] = jnp.zeros((6, 128), f32)


def assemble_kernel(own, left, right, below, above, region, rough, normal, solid):
    solid[...] = jnp.zeros(solid.shape, f32)
    for kz in range(4):
        lrow, rrow, brow, arow = 192 + kz * 40, 192 + kz * 8, 192 + kz * 64, 192 + kz * 24
        for x in range(3):
            for field in range(2):
                inner, outer = x * 6, (x + 3) * 6
                diagonal = brow + 33 + field * 9 + x * 3
                region[field, kz, inner : inner + 3, :] = below[diagonal : diagonal + 3, :]
                row = lrow + field * 12 + x * 4
                region[field, kz, inner + 3 : inner + 6, :] = left[row : row + 3, :]
                row = brow + field * 12 + x * 3
                region[field, kz, outer : outer + 3, :] = below[row : row + 3, :]
                row = field * 16 + x * 4
                region[field, kz, outer + 3 : outer + 6, :] = own[kz, row : row + 3, :]
            to = x * 10
            solid[kz, to : to + 3, :] = below[brow + 33 + x * 3 : brow + 36 + x * 3, :]
            solid[kz, to + 3 : to + 7, :] = left[lrow + x * 4 : lrow + x * 4 + 4, :]
            solid[kz, to + 7 : to + 9, :] = above[arow + 8 + x * 2 : arow + 10 + x * 2, :]
        for x in range(4):
            to = (x + 3) * 10
            solid[kz, to : to + 3, :] = below[brow + x * 3 : brow + x * 3 + 3, :]
            solid[kz, to + 3 : to + 7, :] = own[kz, x * 4 : x * 4 + 4, :]
            solid[kz, to + 7 : to + 9, :] = above[arow + x * 2 : arow + x * 2 + 2, :]
        for x in range(2):
            to = (x + 7) * 10
            solid[kz, to : to + 3, :] = below[brow + 55 + x * 3 : brow + 58 + x * 3, :]
            solid[kz, to + 3 : to + 7, :] = right[rrow + x * 4 : rrow + x * 4 + 4, :]
            solid[kz, to + 7 : to + 9, :] = above[arow + 14 + x * 2 : arow + 16 + x * 2, :]
        for field in range(4):
            ref = rough if field == 0 else normal.at[field - 1]
            ref[kz, 0:1, :] = below[brow + 51 + field : brow + 52 + field, :]
            row = lrow + 24 + field * 4
            ref[kz, 1:4, :] = left[row : row + 3, :]
            for x in range(3):
                to = (x + 1) * 4
                row = brow + 21 + field * 3 + x
                ref[kz, to : to + 1, :] = below[row : row + 1, :]
                row = 32 + field * 16 + x * 4
                ref[kz, to + 1 : to + 4, :] = own[kz, row : row + 3, :]


def update_kernel(mo, rl, rb, rd, region, rough, normal, hl, hb, hd, ko, warm, push):
    warm[...] = jnp.zeros(warm.shape, f32)
    for kz in range(4):
        for ref, dx, dy in ((mo, 2, 2), (rl, 0, 2), (rb, 2, 0), (rd, 0, 0)):
            for c in range(2):
                for x in range(4):
                    at = (48 if ref is mo else 0) + c * 16 + x * 4
                    to = (x + dx) * 6 + dy
                    warm[c, kz, to : to + 4, :] = warm[c, kz, to : to + 4, :] + ref[kz, at : at + 4, :]
        for c in range(3):
            push[c, kz] = mo[kz, c * 16 : c * 16 + 16, :]
            push[c, kz, 0:8, :] = push[c, kz, 0:8, :] + rl[kz, 32 + c * 8 : 40 + c * 8, :]
            for x in range(4):
                at = 32 + c * 8 + x * 2
                push[c, kz, x * 4 : x * 4 + 2, :] = push[c, kz, x * 4 : x * 4 + 2, :] + rb[kz, at : at + 2, :]
            for x in range(2):
                at = 32 + c * 4 + x * 2
                push[c, kz, x * 4 : x * 4 + 2, :] = push[c, kz, x * 4 : x * 4 + 2, :] + rd[kz, at : at + 2, :]
        for x in range(4):
            for c in range(2):
                push[3 + c, kz, x * 4 : x * 4 + 4, :] = (
                    warm[0, kz, (x + 2) * 6 + 2 : (x + 2) * 6 + 6, :]
                    if c == 0
                    else region[0, kz, (x + 2) * 6 + 2 : (x + 2) * 6 + 6, :]
                )
    width_x = 4 * lax.axis_size("gx")
    height_z = 512
    spin = 2.0 / height_z
    shape = (16, 128)
    cell_x = lax.broadcasted_iota(jnp.int32, shape, 0) // 4 - 1 + 4 * lax.axis_index("gx")
    cell_x = jnp.where(cell_x < 0, cell_x + width_x, cell_x).astype(f32)
    wall_w = -spin * (cell_x + 0.5 - 0.5 * width_x)
    for kz in range(4):
        cell_z = (lax.broadcasted_iota(jnp.int32, shape, 1) * 4 + kz).astype(f32)
        wall = [spin * (cell_z + 0.5 - 0.5 * height_z), jnp.zeros(shape, f32), wall_w]
        inverse = 1.0 / jnp.maximum(push[3, kz], mass_floor)
        moving = [push[a, kz] * inverse for a in range(3)]
        moving[2] = moving[2] - gravity_step
        relative = [moving[a] - wall[a] for a in range(3)]
        facing = [normal[a, kz] for a in range(3)]
        normal_part = sum(relative[a] * facing[a] for a in range(3))
        tangent = [relative[a] - normal_part * facing[a] for a in range(3)]
        length = jnp.sqrt(sum(part * part for part in tangent))
        factor = jnp.maximum(
            0.0, 1.0 + friction * normal_part / jnp.maximum(length, slip_floor)
        )
        slips = (rough[kz] == 1.0) & (normal_part < 0.0)
        solid = push[4, kz] == 1.0
        for a in range(3):
            value = jnp.where(slips, wall[a] + tangent[a] * factor, moving[a])
            push[a, kz] = jnp.where(solid, wall[a], value)
        heat = warm[1, kz, 0:36, :] / jnp.maximum(warm[0, kz, 0:36, :], mass_floor)
        warm[1, kz, 0:36, :] = jnp.where(region[0, kz] == 1.0, region[1, kz], heat)
    for kz in range(4):
        ko[kz, 0:36, :] = warm[1, kz, 0:36, :]
        ko[kz, 36:40, :] = jnp.zeros((4, 128), f32)
        hl[kz, 0:24, :] = warm[1, kz, 12:36, :]
        for c in range(3):
            ko[kz, 40 + c * 16 : 56 + c * 16, :] = push[c, kz]
            hl[kz, 24 + c * 8 : 32 + c * 8, :] = push[c, kz, 0:8, :]
            for x in range(4):
                at = 24 + c * 8 + x * 2
                hb[kz, at : at + 2, :] = push[c, kz, x * 4 : x * 4 + 2, :]
            for x in range(2):
                at = 16 + c * 4 + x * 2
                hd[kz, at : at + 2, :] = push[c, kz, x * 4 : x * 4 + 2, :]
        for x in range(6):
            hb[kz, x * 4 : x * 4 + 4, :] = warm[1, kz, x * 6 + 2 : x * 6 + 6, :]
        for x in range(4):
            hd[kz, x * 4 : x * 4 + 4, :] = warm[1, kz, (x + 2) * 6 + 2 : (x + 2) * 6 + 6, :]
        hd[kz, 28:32, :] = jnp.zeros((4, 128), f32)


def collect_kernel(
    code_s, brick_s, came_s, ko, rl, rb, rd, solid, frac, o_ref, rxp, rxm, ryp, rym,
    move_ref, grad_ref, warm_ref, gvel_ref, gtemp_ref,
    heat, speed, cells, fine, coarse, turn, lu, fo, sb, sw, sb2, sw2,
):
    lane = lax.broadcasted_iota(jnp.int32, (8, 128), 1)[0:1]
    heat[...] = jnp.zeros(heat.shape, f32)
    for kz in range(4):
        for x in range(6):
            to = 16 + x * 10
            heat[0, kz, to : to + 6, :] = ko[kz, x * 6 : x * 6 + 6, :]
            heat[0, kz, to + 6 : to + 10, :] = rb[kz, x * 4 : x * 4 + 4, :]
        for x in range(4):
            to = 16 + (x + 6) * 10
            heat[0, kz, to : to + 6, :] = rl[kz, x * 6 : x * 6 + 6, :]
            heat[0, kz, to + 6 : to + 10, :] = rd[kz, x * 4 : x * 4 + 4, :]
        for c in range(3):
            for x in range(4):
                speed[c, kz, x * 6 : x * 6 + 4, :] = ko[kz, 40 + c * 16 + x * 4 : 44 + c * 16 + x * 4, :]
                at = 24 + c * 8 + x * 2
                speed[c, kz, x * 6 + 4 : x * 6 + 6, :] = rb[kz, at : at + 2, :]
            for x in range(2):
                at = 24 + c * 8 + x * 4
                speed[c, kz, 24 + x * 6 : 28 + x * 6, :] = rl[kz, at : at + 4, :]
                at = 16 + c * 4 + x * 2
                speed[c, kz, 28 + x * 6 : 30 + x * 6, :] = rd[kz, at : at + 2, :]
    for sweep in range(2):
        now, later = sweep, sweep + 1
        layers = [heat[now, kz, 16:120, :] for kz in range(4)]
        above = jnp.where(lane == 127, layers[3], pltpu.roll(layers[0], 127, 1))
        below = jnp.where(lane == 0, layers[0], pltpu.roll(layers[3], 1, 1))
        for kz in range(4):
            upper = layers[kz + 1] if kz < 3 else above
            lower = layers[kz - 1] if kz else below
            laplace = (
                heat[now, kz, 6:110, :]
                + heat[now, kz, 26:130, :]
                + heat[now, kz, 15:119, :]
                + heat[now, kz, 17:121, :]
                + upper
                + lower
                - 6.0 * layers[kz]
            )
            heat[later, kz, 16:120, :] = jnp.where(
                solid[kz] == 1.0, heat[0, kz, 16:120, :], layers[kz] + conduct * laplace
            )
    for kz in range(4):
        for x in range(6):
            to = 16 + (x + 2) * 10 + 2
            speed[3, kz, x * 6 : x * 6 + 6, :] = heat[2, kz, to : to + 6, :]
    for c in range(4):
        for kz in range(4):
            for x in range(4):
                at = (x + 1) * 6 + 1
                cells[c * 16 + x * 4 : c * 16 + x * 4 + 4, kz * 128 : kz * 128 + 128] = speed[c, kz, at : at + 4, :]
    source = lax.broadcasted_iota(jnp.int32, (512, 512), 0)
    wanted = (source % 128) * 4 + source // 128
    permute = (wanted == lax.broadcasted_iota(jnp.int32, (512, 512), 1)).astype(f32).astype(bf16)
    value = cells[...]
    high, rest = split_two(value)
    middle, low = split_two(rest)
    spread = jnp.concatenate([high, middle, low], axis=0).astype(bf16)
    spread = jnp.dot(spread, permute, preferred_element_type=f32)
    value = spread[0:64] + spread[64:128] + spread[128:192]
    for x in range(4):
        for c in range(3):
            gvel_ref[c, x] = value[c * 16 + x * 4 : c * 16 + x * 4 + 4]
        gtemp_ref[x] = value[48 + x * 4 : 52 + x * 4]
    for c in range(4):
        for jz in range(6):
            kz = (jz - 1) % 4
            layer = speed[c, kz]
            if jz == 0:
                layer = jnp.where(lane == 0, 0.0, pltpu.roll(layer, 1, 1))
            if jz == 5:
                layer = jnp.where(lane == 127, 0.0, pltpu.roll(layer, 127, 1))
            high, low = split_two(layer)
            coarse[c, jz] = high
            fine[c, jz] = low
    turn[...] = jnp.zeros(turn.shape, f32)
    for jx in range(6):
        for c in range(4):
            side = c % 2
            for jz in range(6):
                rows = slice(jx * 6, jx * 6 + 6)
                turn[side, jz * 6 : jz * 6 + 6, :] = coarse[c, jz, rows, :]
                turn[side, 40 + jz * 6 : 46 + jz * 6, :] = fine[c, jz, rows, :]
                turn[side, 80 + jz * 6 : 86 + jz * 6, :] = coarse[c, jz, rows, :]
            lu[pl.ds(jx * 4 + c, 128, stride=24), :] = jnp.transpose(turn[side])
    for d in range(3):
        fo[d, 0:128, :] = frac[d]
    fo[3, 0:128, :] = o_ref[...].astype(f32)
    places = [(ryp, 0), (rxp, 1), (rym, 0), (ryp, 1), (rym, 1), (ryp, 2), (rxm, 1), (rym, 2)]
    for g, (ref, at) in enumerate(places):
        for d in range(4):
            fo[d, 128 + g * 16 : 144 + g * 16, :] = ref[pl.ds(at * way_rows + d, 16, stride=4), :]
    sb[...] = jnp.zeros(sb.shape, f32)
    sb2[...] = jnp.zeros(sb2.shape, f32)

    def build(g, sb, sw):
        rows = pl.ds(pl.multiple_of(g * 8, 8), 8)
        offset = fo[3, rows, :].astype(jnp.int32)
        wx, rx = axis_tables(offset >> 4, fo[0, rows, :], 4.0)
        for j in range(6):
            for copy in range(4):
                sw[pl.ds((j * 4 + copy) * 8, 8), :] = wx[j]
                sw[pl.ds((24 + j * 4 + copy) * 8, 8), :] = rx[j]
        wy, ry = axis_tables((offset >> 2) & 3, fo[1, rows, :], 4.0)
        wz, rz = axis_tables(offset & 3, fo[2, rows, :], 4.0)
        for jz in range(6):
            for jy in range(6):
                r = jz * 6 + jy
                sb[pl.ds(r * 8, 8), :] = wy[jy] * wz[jz]
                sb[pl.ds((40 + r) * 8, 8), :] = ry[jy] * wz[jz]
                sb[pl.ds((80 + r) * 8, 8), :] = wy[jy] * rz[jz]

    def work(g, sb, sw):
        for j in range(8):
            slot = g * 8 + j
            home = jnp.minimum(slot, 127)
            stays = jnp.where(code_s[home] == 4, brick_s[home], -1)
            brick = jnp.where(slot < 128, stays, came_s[0, jnp.maximum(slot - 128, 0)])
            live = jnp.where(brick >= 0, 1.0, 0.0).astype(f32)
            spot = pl.ds(pl.multiple_of(jnp.maximum(brick, 0) * 24, 8), 24)
            left = lu[spot, :].astype(bf16)
            right = jnp.concatenate(
                [sb[pl.ds(n * 320 + j, 40, stride=8), :] for n in range(3)], axis=1
            )
            high, low = split_two(right)
            right = jnp.concatenate([high, high, low, jnp.zeros((8, 384), f32)], axis=0).astype(bf16)
            both = jnp.dot(left, right, preferred_element_type=f32)
            plain = sw[pl.ds(j, 24, stride=8), :]
            tilt = sw[pl.ds(192 + j, 24, stride=8), :]

            def over_x(weight, column):
                part = weight * both[:, column * 128 : column * 128 + 128]
                part = part[0:8] + part[8:16] + part[16:24]
                return (part[0:4] + part[4:8]) * live

            lanes = pl.ds(pl.multiple_of(slot * 128, 128), 128)
            moved = over_x(plain, 0)
            move_ref[:, lanes] = moved[0:3]
            warm_ref[pl.ds(slot, 1), :] = moved[3:4]
            for k, (weight, column) in enumerate(((tilt, 0), (plain, 1), (plain, 2))):
                part = over_x(weight, column)
                for a in range(3):
                    grad_ref[a * 3 + k : a * 3 + k + 1, lanes] = part[a : a + 1]

    def pair(i, carry):
        build(2 * i + 1, sb2, sw2)
        work(2 * i, sb, sw)
        build(jnp.minimum(2 * i + 2, 31), sb, sw)
        work(2 * i + 1, sb2, sw2)
        return carry

    build(0, sb, sw)
    lax.fori_loop(0, 16, pair, 0)


def neighbor(value, dx, dy):
    size_x, size_y = lax.axis_size("gx"), lax.axis_size("gy")
    if dy == 0:
        return lax.ppermute(value, "gx", [(i, (i + dx) % size_x) for i in range(size_x)])
    if dx == 0:
        return lax.ppermute(value, "gy", [(i, (i + dy) % size_y) for i in range(size_y)])
    pairs = [
        (i * size_y + j, (i + dx) % size_x * size_y + (j + dy) % size_y)
        for i in range(size_x)
        for j in range(size_y)
    ]
    return lax.ppermute(value, ("gx", "gy"), pairs)


def call(
    kernel, name, inputs, scalars, outputs, scratch, left_there=0, limit=50, flops=1e8, listed=0
):
    in_specs = (
        [pl.BlockSpec(memory_space=pltpu.SMEM)] * scalars
        + [pl.BlockSpec(memory_space=pltpu.HBM)] * left_there
        + [pl.BlockSpec(memory_space=pltpu.VMEM)] * (len(inputs) - scalars - left_there)
    )
    return pl.pallas_call(
        kernel,
        name=name,
        out_shape=[jax.ShapeDtypeStruct(shape, dtype) for shape, dtype in outputs],
        in_specs=in_specs,
        out_specs=[pl.BlockSpec(memory_space=pltpu.SMEM)] * listed
        + [pl.BlockSpec(memory_space=pltpu.VMEM)] * (len(outputs) - listed),
        cost_estimate=pl.CostEstimate(
            flops=int(flops), bytes_accessed=int(flops / 300), transcendentals=0
        ),
        scratch_shapes=scratch,
        compiler_params=pltpu.CompilerParams(vmem_limit_bytes=limit * mib),
    )(*inputs)


def vmem(*shape):
    return pltpu.VMEM(shape, f32)


def on_device(
    subvoxel_location_share,
    point_motion_vector,
    linear_gradient_matrix,
    kirchhoff_tension_matrix,
    point_inertia_amounts,
    point_thermal_state,
    anchor_voxel_shift,
    group_resting_volume,
    group_migration_label,
    cylinder_shell_flag,
    rough_surface_flag,
    voxel_facing_choice,
    facing_unit_vectors,
    rim_thermal_level,
):
    offset = anchor_voxel_shift.reshape(128, 128)
    info, static, sxp, sxm = call(
        prepare_kernel,
        "prepare",
        (
            facing_unit_vectors,
            group_migration_label,
            cylinder_shell_flag,
            rough_surface_flag,
            voxel_facing_choice,
            rim_thermal_level,
            subvoxel_location_share,
            offset,
        ),
        2,
        [
            ((640,), jnp.int32),
            ((6, 96, 128), f32),
            ((352, 128), f32),
            ((224, 128), f32),
        ],
        [vmem(64, 512), vmem(520, 128), pltpu.SMEM((16,), jnp.int32)],
        limit=64,
        flops=2e9,
        listed=1,
    )
    rsxp = neighbor(sxp, 1, 0)
    rsxm = neighbor(sxm, -1, 0)
    block_args = (
        group_resting_volume,
        subvoxel_location_share,
        point_motion_vector,
        linear_gradient_matrix,
        kirchhoff_tension_matrix,
        point_inertia_amounts.reshape(128, 128),
        point_thermal_state.reshape(128, 128),
        offset,
    )
    block_scratch = [
        vmem(3, 16384),
        vmem(3, 16384),
        vmem(9, 16384),
        vmem(9, 16384),
        vmem(128, 128),
        vmem(128, 128),
        pltpu.VMEM((128, 128), jnp.int32),
        pltpu.SemaphoreType.DMA((7,)),
        vmem(320, 128),
        vmem(96 * 8, 128),
        vmem(120 * 8, 128),
        vmem(320, 128),
        vmem(96 * 8, 128),
        vmem(120 * 8, 128),
        vmem(129 * 32, 128),
    ]
    xm, ym, yp, xp = call(
        outgoing_kernel,
        "outgoing",
        (info,) + block_args,
        2,
        [
            ((3 * msg_rows, 128), f32),
            ((msg_rows, 128), f32),
            ((msg_rows, 128), f32),
            ((3 * msg_rows, 128), f32),
        ],
        block_scratch,
        7,
        64,
        flops=6e9,
    )
    xm, xp, rsxp, rsxm = lax.optimization_barrier((xm, xp, rsxp, rsxm))
    rxp = neighbor(xp, 1, 0)
    rxm = neighbor(xm, -1, 0)
    up, down = call(
        relay_kernel,
        "relay",
        (rsxp, rsxm, static),
        0,
        [((448, 128), f32), ((288, 128), f32)],
        [],
        flops=5e8,
    )
    rsyp = neighbor(up, 0, 1)
    rsym = neighbor(down, 0, -1)
    up = jnp.concatenate([rxp[2 * msg_rows :], yp, rxm[2 * msg_rows :]], axis=0)
    down = jnp.concatenate([rxp[:msg_rows], ym, rxm[:msg_rows]], axis=0)
    up, down, info = lax.optimization_barrier((up, down, info))
    ryp = neighbor(up, 0, 1)
    rym = neighbor(down, 0, -1)
    own, frac = call(
        staying_kernel,
        "staying",
        (info,) + block_args,
        2,
        [((tiles, 128, 128), f32), ((3, 128, 128), f32)],
        block_scratch,
        7,
        50,
        flops=1e10,
    )
    region, rough, normal, solid = call(
        assemble_kernel,
        "assemble",
        (static, rsxp, rsxm, rsyp, rsym),
        0,
        [
            ((2, 4, 36, 128), f32),
            ((4, 16, 128), f32),
            ((3, 4, 16, 128), f32),
            ((4, 104, 128), f32),
        ],
        [],
        flops=5e8,
    )

    ml, mb, md, mo, came = call(
        total_kernel,
        "total",
        (own, rxp, rxm, ryp, rym),
        0,
        [
            ((4, 56, 128), f32),
            ((4, 56, 128), f32),
            ((4, 48, 128), f32),
            ((4, 80, 128), f32),
            ((1, 128), jnp.int32),
        ],
        [vmem(tiles * 128, 128), vmem(4, 184, 128)],
    )
    hl, hb, hd, ko = call(
        update_kernel,
        "update",
        (mo, neighbor(ml, 1, 0), neighbor(mb, 0, 1), neighbor(md, 1, 1), region, rough, normal),
        0,
        [
            ((4, 48, 128), f32),
            ((4, 48, 128), f32),
            ((4, 32, 128), f32),
            ((4, 88, 128), f32),
        ],
        [vmem(2, 4, 40, 128), vmem(5, 4, 16, 128)],
    )
    move, grad, warm, gvel, gtemp = call(
        collect_kernel,
        "collect",
        (
            group_migration_label,
            group_resting_volume,
            came,
            ko,
            neighbor(hl, -1, 0),
            neighbor(hb, 0, -1),
            neighbor(hd, -1, -1),
            solid,
            frac,
            offset,
            rsxp,
            rsxm,
            rsyp,
            rsym,
        ),
        3,
        [
            ((3, 32768), f32),
            ((9, 32768), f32),
            ((256, 128), f32),
            ((3, 4, 4, 512), f32),
            ((4, 4, 512), f32),
        ],
        [
            vmem(3, 4, 136, 128),
            vmem(4, 4, 40, 128),
            vmem(64, 512),
            vmem(4, 6, 40, 128),
            vmem(4, 6, 40, 128),
            vmem(2, 128, 128),
            vmem(128 * 24, 128),
            vmem(4, 256, 128),
            vmem(120 * 8, 128),
            vmem(48 * 8, 128),
            vmem(120 * 8, 128),
            vmem(48 * 8, 128),
        ],
    )
    return move, grad, warm.reshape(-1), gvel, gtemp


def solution(mesh):
    in_specs = (
        P(None, ("gx", "gy")),
        P(None, ("gx", "gy")),
        P(None, ("gx", "gy")),
        P(None, ("gx", "gy")),
        P(("gx", "gy")),
        P(("gx", "gy")),
        P(("gx", "gy")),
        P(("gx", "gy")),
        P(("gx", "gy")),
        P("gx", "gy", None),
        P("gx", "gy", None),
        P("gx", "gy", None),
        P(),
        P("gx", "gy", None),
    )
    out_specs = (
        P(None, ("gx", "gy")),
        P(None, ("gx", "gy")),
        P(("gx", "gy")),
        P(None, "gx", "gy", None),
        P("gx", "gy", None),
    )
    return jax.shard_map(
        on_device, mesh=mesh, in_specs=in_specs, out_specs=out_specs, check_vma=False
    )
```

```python
import jax
import jax.numpy as jnp
from jax import lax
from jax.experimental import pallas as pl
from jax.experimental.pallas import tpu as pltpu
from jax.sharding import PartitionSpec as P

f32 = jnp.float32
bf16 = jnp.bfloat16
mass_floor = 0.25
slip_floor = 0.1
friction = 0.4
gravity_step = 0.5
conduct = 0.15
stress_coef = 0.25
mib = 1024 * 1024
pieces = 31
tiles = 9
msg_rows = tiles * 16
way_rows = 64


def axis_tables(shift, inside, scale):
    near = 0.5 * (1.5 - inside) ** 2
    middle = 0.75 - (inside - 1.0) ** 2
    far = 0.5 * (inside - 0.5) ** 2
    at = [shift == step for step in range(4)]
    zero = jnp.zeros_like(inside)
    weight = [
        jnp.where(at[0], near, zero),
        jnp.where(at[0], middle, jnp.where(at[1], near, zero)),
        jnp.where(at[0], far, jnp.where(at[1], middle, jnp.where(at[2], near, zero))),
        jnp.where(at[1], far, jnp.where(at[2], middle, jnp.where(at[3], near, zero))),
        jnp.where(at[2], far, jnp.where(at[3], middle, zero)),
        jnp.where(at[3], far, zero),
    ]
    place = shift.astype(f32) + inside
    first = [weight[step] * (scale * (step - place)) for step in range(6)]
    return weight, first


def split_two(value):
    high = value.astype(bf16).astype(f32)
    return high, value - high


def clear_rows(ref, rows):
    def step(n, carry):
        ref[pl.ds(pl.multiple_of(n * 128, 128), 128), :] = jnp.zeros((128, 128), f32)
        return carry

    lax.fori_loop(0, rows // 128, step, 0)


def deposit_blocks(
    base, count, info_s, target_of, refs, first, second, acc, after
):
    f_ref, v_ref, c_ref, k_ref, m_ref, t_ref, o_ref = refs
    clear_rows(acc, 128 * 40)
    for _, sa, sb in (first, second):
        sa[...] = jnp.zeros(sa.shape, f32)
        sb[...] = jnp.zeros(sb.shape, f32)
    row_no = lax.broadcasted_iota(jnp.int32, (32, 1), 0)

    def build(g, raw, sa, sb):
        blocks = [info_s[base + g * 8 + j] for j in range(8)]
        for j in range(8):
            lanes = pl.ds(pl.multiple_of(blocks[j] * 128, 128), 128)
            raw[j * 40 : j * 40 + 3, :] = f_ref[:, lanes]
            raw[j * 40 + 3 : j * 40 + 6, :] = v_ref[:, lanes]
            raw[j * 40 + 6 : j * 40 + 7, :] = m_ref[pl.ds(blocks[j], 1), :]
            raw[j * 40 + 7 : j * 40 + 8, :] = t_ref[pl.ds(blocks[j], 1), :]
            raw[j * 40 + 8 : j * 40 + 17, :] = c_ref[:, lanes]
            raw[j * 40 + 24 : j * 40 + 33, :] = k_ref[:, lanes]
            raw[j * 40 + 33 : j * 40 + 34, :] = o_ref[pl.ds(blocks[j], 1), :].astype(f32)

        def get(row):
            return raw[pl.ds(row, 8, stride=40), :]

        mass = get(6)
        heat = mass * get(7)
        offset = get(33).astype(jnp.int32)
        inside = [get(d) for d in range(3)]
        wx, rx = axis_tables(offset >> 4, inside[0], 1.0)
        for a in range(3):
            push = mass * get(3 + a)
            q = [
                mass * get(8 + a * 3 + k) - stress_coef * get(24 + a * 3 + k) for k in range(3)
            ]
            for j in range(6):
                sa[pl.ds((a * 6 + j) * 8, 8), :] = push * wx[j] + q[0] * rx[j]
                sa[pl.ds((32 + a * 6 + j) * 8, 8), :] = q[1] * wx[j]
                sa[pl.ds((64 + a * 6 + j) * 8, 8), :] = q[2] * wx[j]
        for j in range(6):
            sa[pl.ds((18 + j) * 8, 8), :] = mass * wx[j]
            sa[pl.ds((24 + j) * 8, 8), :] = heat * wx[j]
        wy, ry = axis_tables((offset >> 2) & 3, inside[1], 1.0)
        wz, rz = axis_tables(offset & 3, inside[2], 1.0)
        for jy in range(6):
            for jz in range(6):
                r = jy * 6 + jz
                sb[pl.ds(r * 8, 8), :] = wy[jy] * wz[jz]
                sb[pl.ds((40 + r) * 8, 8), :] = ry[jy] * wz[jz]
                sb[pl.ds((80 + r) * 8, 8), :] = wy[jy] * rz[jz]

    def work(g, raw, sa, sb):
        blocks = [info_s[base + g * 8 + j] for j in range(8)]
        sums = []
        for j in range(8):
            left = jnp.concatenate(
                [sa[pl.ds(n * 256 + j, 32, stride=8), :] for n in range(3)], axis=1
            )
            right = jnp.concatenate(
                [sb[pl.ds(n * 320 + j, 40, stride=8), :] for n in range(3)], axis=1
            )
            left = jnp.concatenate(split_two(left), axis=0).astype(bf16)
            right = jnp.concatenate(split_two(right), axis=0).astype(bf16)
            both = lax.dot_general(
                left, right, (((1,), (1,)), ((), ())), preferred_element_type=f32
            )
            both = both[:32] + both[32:]
            sums.append(both[:, :40] + both[:, 40:])
        for j in range(8):
            target, mark = target_of(g * 8 + j, blocks[j])
            spot = pl.ds(pl.multiple_of(target * 40, 8), 32)
            acc[spot, 0:40] = acc[spot, 0:40] + (sums[j] + jnp.where(row_no == 30, mark, 0.0))
            after(j, blocks[j], raw)

    def pair(i, carry):
        build(2 * i + 1, *second)
        work(2 * i, *first)
        build(2 * i + 2, *first)
        work(2 * i + 1, *second)
        return carry

    build(0, *first)
    lax.fori_loop(0, (count + 15) // 16, pair, 0)


def packed(acc, chunk):
    lane = lax.broadcasted_iota(jnp.int32, (8, 128), 1)
    total = [jnp.zeros((8, 128), f32) for _ in range(tiles)]
    for i in range(pieces):
        piece = acc[pl.ds(chunk * 320 + i, 8, stride=40), :]
        if i == 30:
            piece = jnp.where(lane < 36, piece, 0.0)
        tile, at = divmod(i * 36, 128)
        if at:
            piece = pltpu.roll(piece, at, 1)
        if at + 36 > 128:
            total[tile] = total[tile] + jnp.where(lane >= at, piece, 0.0)
            total[tile + 1] = total[tile + 1] + jnp.where(lane < at, piece, 0.0)
        else:
            total[tile] = total[tile] + piece
    return total


def outgoing_kernel(
    info_s, f_ref, v_ref, c_ref, k_ref, m_ref, t_ref, o_ref,
    xm_ref, ym_ref, yp_ref, xp_ref,
    raw, sa, sb, raw2, sa2, sb2, acc,
):
    def target_of(entry, block):
        return info_s[160 + entry], (info_s[640 + block] + 1).astype(f32)

    deposit_blocks(
        0, info_s[544], info_s, target_of,
        (f_ref, v_ref, c_ref, k_ref, m_ref, t_ref, o_ref),
        (raw, sa, sb), (raw2, sa2, sb2), acc, lambda j, block, raw: None,
    )
    for first, count, ref in ((0, 3, xm_ref), (3, 1, ym_ref), (4, 1, yp_ref), (5, 3, xp_ref)):
        for n in range(count):
            for half in range(2):

                def some(n=n, half=half, first=first, ref=ref):
                    for tile, value in enumerate(packed(acc, (first + n) * 2 + half)):
                        at = n * msg_rows + tile * 16 + half * 8
                        ref[at : at + 8, :] = value

                def none(n=n, half=half, ref=ref):
                    for tile in range(tiles):
                        at = n * msg_rows + tile * 16 + half * 8
                        ref[at : at + 8, :] = jnp.zeros((8, 128), f32)

                lax.cond(info_s[552 + first + n] > half * 8, some, none)


def staying_kernel(
    info_s, f_ref, v_ref, c_ref, k_ref, m_ref, t_ref, o_ref,
    own_ref, frac_ref,
    raw, sa, sb, raw2, sa2, sb2, acc,
):
    frac_ref[...] = jnp.zeros(frac_ref.shape, f32)

    def target_of(entry, block):
        return jnp.where(entry < info_s[545], info_s[640 + block], 128), jnp.float32(0.0)

    def after(j, block, raw):
        for d in range(3):
            frac_ref[d, pl.ds(block, 1), :] = raw[j * 40 + d : j * 40 + d + 1, :]

    deposit_blocks(
        320, info_s[545], info_s, target_of,
        (f_ref, v_ref, c_ref, k_ref, m_ref, t_ref, o_ref),
        (raw, sa, sb), (raw2, sa2, sb2), acc, after,
    )

    def pack_own(chunk, carry):
        for tile, value in enumerate(packed(acc, chunk)):
            own_ref[tile, pl.ds(pl.multiple_of(chunk * 8, 8), 8), :] = value
        return carry

    lax.fori_loop(0, 16, pack_own, 0)


def runs_left():
    return (
        [(3, x, 0, 4) for x in range(2, 6)]
        + [(4, x, 0, 4) for x in range(2, 6)]
        + [(c, x, 0, 4) for c in range(3) for x in (4, 5)]
    )


def runs_below():
    return (
        [(3, x, 2, 4) for x in range(4)]
        + [(4, x, 2, 4) for x in range(4)]
        + [(c, x, 4, 2) for c in range(3) for x in range(4)]
    )


def runs_diagonal():
    return (
        [(3, x, 2, 4) for x in range(2, 6)]
        + [(4, x, 2, 4) for x in range(2, 6)]
        + [(c, x, 4, 2) for c in range(3) for x in (4, 5)]
    )


def runs_own():
    return [(c, x, 0, 4) for c in range(5) for x in range(4)]


def total_kernel(own_ref, rxp, rxm, ryp, rym, ml, mb, md, mo, brick_ref, wide, grid):
    places = [(ryp, 0), (rxp, 1), (rym, 0), (ryp, 1), (rym, 1), (ryp, 2), (rxm, 1), (rym, 2)]

    def arrived(tile):
        return jnp.concatenate(
            [ref[pl.ds(at * msg_rows + tile * 16, 16), :] for ref, at in places], axis=0
        )

    rows = lax.broadcasted_iota(jnp.int32, (128, 128), 0)
    lanes = lax.broadcasted_iota(jnp.int32, (128, 128), 1)
    column = arrived(8)[:, 56:57]
    row = jnp.sum(jnp.where(rows == lanes, column, 0.0), axis=0, keepdims=True)
    brick_ref[...] = row.astype(jnp.int32) - 1
    hits = (row == (rows + 1).astype(f32)).astype(f32).astype(bf16)
    hits = jnp.concatenate([hits, hits], axis=1)
    for tile in range(tiles):
        high, low = split_two(arrived(tile))
        stack = jnp.concatenate([high.astype(bf16), low.astype(bf16)], axis=0)
        value = own_ref[tile] + jnp.dot(hits, stack, preferred_element_type=f32)
        wide[tile * 128 : tile * 128 + 128, :] = jnp.transpose(value)
    lane = lax.broadcasted_iota(jnp.int32, (184, 128), 1)

    def layer(jz):
        return wide[pl.ds(jz, 184, stride=6), :]

    grid[0] = layer(1) + jnp.where(lane == 0, 0.0, pltpu.roll(layer(5), 1, 1))
    grid[1] = layer(2)
    grid[2] = layer(3)
    grid[3] = layer(4) + jnp.where(lane == 127, 0.0, pltpu.roll(layer(0), 127, 1))
    for ref, runs in ((ml, runs_left()), (mb, runs_below()), (md, runs_diagonal()), (mo, runs_own())):
        for kz in range(4):
            to = 0
            for c, x, y, count in runs:
                ref[kz, to : to + count, :] = grid[kz, c * 36 + x * 6 + y : c * 36 + x * 6 + y + count, :]
                to += count
            if to < ref.shape[1]:
                ref[kz, to:, :] = jnp.zeros((ref.shape[1] - to, 128), f32)


def prepare_kernel(
    table_hbm, code_hbm, solid_hbm, rough_hbm, choice_hbm, rim_hbm,
    brick_hbm, f_hbm, v_hbm, c_hbm, k_hbm, m_hbm, t_hbm, o_hbm,
    info, own, xp, xm, f_ref, v_ref, c_ref, k_ref, m_ref, t_ref, o_ref,
    table, code_s, brick_s, solid_ref, rough_ref, choice_ref, rim_ref, sems,
    cells, fo, cnt,
):
    pairs = (
        (code_hbm, code_s), (f_hbm, f_ref), (o_hbm, o_ref), (table_hbm, table),
        (solid_hbm, solid_ref), (rough_hbm, rough_ref), (choice_hbm, choice_ref), (rim_hbm, rim_ref),
        (brick_hbm, brick_s), (v_hbm, v_ref), (c_hbm, c_ref), (k_hbm, k_ref), (m_hbm, m_ref),
        (t_hbm, t_ref),
    )
    copies = [pltpu.make_async_copy(a, b, sems.at[n]) for n, (a, b) in enumerate(pairs)]
    for copy in copies:
        copy.start()
    fo[...] = jnp.zeros(fo.shape, f32)
    for copy in copies[:9]:
        copy.wait()
    for n in range(10):
        cnt[n] = 0

    def sort(b, carry):
        code = code_s[b]
        rank = cnt[code]
        cnt[code] = rank + 1
        leaves = code != 4
        way = jnp.where(code > 4, code - 1, code)
        gone = cnt[9]
        slot = way * 16 + rank
        info[jnp.where(leaves, gone, 320 + b - gone)] = b
        info[640 + b] = brick_s[b]
        info[jnp.where(leaves, 160 + gone, 639)] = slot
        cnt[9] = gone + jnp.where(leaves, 1, 0)
        at = pl.multiple_of(jnp.where(leaves, slot, 128) * 4, 4)
        lanes = pl.ds(pl.multiple_of(b * 128, 128), 128)
        fo[pl.ds(at, 3), :] = f_ref[:, lanes]
        fo[pl.ds(at + 3, 1), :] = o_ref[pl.ds(b, 1), :].astype(f32)
        return carry

    lax.fori_loop(0, 128, sort, 0, unroll=4)
    gone = cnt[9]
    for n in range(24):
        info[gone + n] = 0
        info[160 + gone + n] = 128
        info[320 + 128 - gone + n] = 0
    for n in range(8):
        info[552 + n] = cnt[n if n < 4 else n + 1]
    info[544] = gone
    info[545] = 128 - gone
    for x in range(4):
        rows = slice(x * 4, x * 4 + 4)
        cells[rows, :] = solid_ref[x].astype(f32)
        cells[16 + x * 4 : 20 + x * 4, :] = rough_ref[x].astype(f32)
        cells[32 + x * 4 : 36 + x * 4, :] = choice_ref[x].astype(f32)
        cells[48 + x * 4 : 52 + x * 4, :] = rim_ref[x]
    value = cells[...]
    high, rest = split_two(value[48:64])
    middle, low = split_two(rest)
    value = jnp.concatenate([value[0:48], high, middle, low], axis=0).astype(bf16)
    source = lax.broadcasted_iota(jnp.int32, (512, 512), 0)
    wanted = (source % 4) * 128 + source // 4
    permute = (wanted == lax.broadcasted_iota(jnp.int32, (512, 512), 1)).astype(f32).astype(bf16)
    value = jnp.dot(value, permute, preferred_element_type=f32)
    rim = value[48:64] + value[64:80] + value[80:96]
    choice = value[32:48]
    normal = [jnp.zeros(choice.shape, f32) for _ in range(3)]
    for n in range(table.shape[1]):
        hit = choice == float(n)
        normal = [jnp.where(hit, table[d, n], normal[d]) for d in range(3)]
    for kz in range(4):
        lanes = slice(kz * 128, kz * 128 + 128)
        for field, part in enumerate((value[0:16], rim, value[16:32], *normal)):
            own[kz, field * 16 : field * 16 + 16, :] = part[:, lanes]
        at = 192 + kz * 40
        xp[at : at + 12, :] = own[kz, 4:16, :]
        xp[at + 12 : at + 24, :] = own[kz, 20:32, :]
        for field in range(4):
            row = 32 + field * 16
            xp[at + 24 + field * 4 : at + 28 + field * 4, :] = own[kz, row + 12 : row + 16, :]
        xm[192 + kz * 8 : 200 + kz * 8, :] = own[kz, 0:8, :]
    for copy in copies[9:]:
        copy.wait()
    xm[0:192, :] = fo[0:192, :]
    for way in range(2):
        own[4 + way, 0:64, :] = fo[192 + way * 64 : 256 + way * 64, :]
        own[4 + way, 64:96, :] = jnp.zeros((32, 128), f32)
    xp[0:192, :] = fo[320:512, :]


def relay_kernel(left, right, own, up, down):
    for way, ref in ((0, down), (1, up)):
        at = 128 * way
        ref[0:64, :] = left[at : at + 64, :]
        ref[64:128, :] = own[4 + way, 0:64, :]
        ref[128:192, :] = right[at : at + 64, :]
    for kz in range(4):
        lrow, rrow = 192 + kz * 40, 192 + kz * 8
        to = 192 + kz * 64
        for x in range(4):
            up[to + x * 3 : to + x * 3 + 3, :] = own[kz, x * 4 + 1 : x * 4 + 4, :]
        for x in range(3):
            row = 16 + x * 4
            up[to + 12 + x * 3 : to + 15 + x * 3, :] = own[kz, row + 1 : row + 4, :]
            up[to + 33 + x * 3 : to + 36 + x * 3, :] = left[lrow + x * 4 + 1 : lrow + x * 4 + 4, :]
            row = lrow + 12 + x * 4
            up[to + 42 + x * 3 : to + 45 + x * 3, :] = left[row + 1 : row + 4, :]
            for field in range(4):
                row = 32 + field * 16 + x * 4 + 3
                at = to + 21 + field * 3 + x
                up[at : at + 1, :] = own[kz, row : row + 1, :]
        for field in range(4):
            row = lrow + 24 + field * 4 + 3
            up[to + 51 + field : to + 52 + field, :] = left[row : row + 1, :]
        for x in range(2):
            up[to + 55 + x * 3 : to + 58 + x * 3, :] = right[rrow + x * 4 + 1 : rrow + x * 4 + 4, :]
        up[to + 61 : to + 64, :] = jnp.zeros((3, 128), f32)
        to = 192 + kz * 24
        for x in range(4):
            down[to + x * 2 : to + x * 2 + 2, :] = own[kz, x * 4 : x * 4 + 2, :]
        for x in range(3):
            down[to + 8 + x * 2 : to + 10 + x * 2, :] = left[lrow + x * 4 : lrow + x * 4 + 2, :]
        for x in range(2):
            down[to + 14 + x * 2 : to + 16 + x * 2, :] = right[rrow + x * 4 : rrow + x * 4 + 2, :]
        down[to + 18 : to + 24, :] = jnp.zeros((6, 128), f32)


def assemble_kernel(own, left, right, below, above, region, rough, normal, solid):
    solid[...] = jnp.zeros(solid.shape, f32)
    for kz in range(4):
        lrow, rrow, brow, arow = 192 + kz * 40, 192 + kz * 8, 192 + kz * 64, 192 + kz * 24
        for x in range(3):
            for field in range(2):
                inner, outer = x * 6, (x + 3) * 6
                diagonal = brow + 33 + field * 9 + x * 3
                region[field, kz, inner : inner + 3, :] = below[diagonal : diagonal + 3, :]
                row = lrow + field * 12 + x * 4
                region[field, kz, inner + 3 : inner + 6, :] = left[row : row + 3, :]
                row = brow + field * 12 + x * 3
                region[field, kz, outer : outer + 3, :] = below[row : row + 3, :]
                row = field * 16 + x * 4
                region[field, kz, outer + 3 : outer + 6, :] = own[kz, row : row + 3, :]
            to = x * 10
            solid[kz, to : to + 3, :] = below[brow + 33 + x * 3 : brow + 36 + x * 3, :]
            solid[kz, to + 3 : to + 7, :] = left[lrow + x * 4 : lrow + x * 4 + 4, :]
            solid[kz, to + 7 : to + 9, :] = above[arow + 8 + x * 2 : arow + 10 + x * 2, :]
        for x in range(4):
            to = (x + 3) * 10
            solid[kz, to : to + 3, :] = below[brow + x * 3 : brow + x * 3 + 3, :]
            solid[kz, to + 3 : to + 7, :] = own[kz, x * 4 : x * 4 + 4, :]
            solid[kz, to + 7 : to + 9, :] = above[arow + x * 2 : arow + x * 2 + 2, :]
        for x in range(2):
            to = (x + 7) * 10
            solid[kz, to : to + 3, :] = below[brow + 55 + x * 3 : brow + 58 + x * 3, :]
            solid[kz, to + 3 : to + 7, :] = right[rrow + x * 4 : rrow + x * 4 + 4, :]
            solid[kz, to + 7 : to + 9, :] = above[arow + 14 + x * 2 : arow + 16 + x * 2, :]
        for field in range(4):
            ref = rough if field == 0 else normal.at[field - 1]
            ref[kz, 0:1, :] = below[brow + 51 + field : brow + 52 + field, :]
            row = lrow + 24 + field * 4
            ref[kz, 1:4, :] = left[row : row + 3, :]
            for x in range(3):
                to = (x + 1) * 4
                row = brow + 21 + field * 3 + x
                ref[kz, to : to + 1, :] = below[row : row + 1, :]
                row = 32 + field * 16 + x * 4
                ref[kz, to + 1 : to + 4, :] = own[kz, row : row + 3, :]


def update_kernel(mo, rl, rb, rd, region, rough, normal, hl, hb, hd, ko, warm, push):
    warm[...] = jnp.zeros(warm.shape, f32)
    for kz in range(4):
        for ref, dx, dy in ((mo, 2, 2), (rl, 0, 2), (rb, 2, 0), (rd, 0, 0)):
            for c in range(2):
                for x in range(4):
                    at = (48 if ref is mo else 0) + c * 16 + x * 4
                    to = (x + dx) * 6 + dy
                    warm[c, kz, to : to + 4, :] = warm[c, kz, to : to + 4, :] + ref[kz, at : at + 4, :]
        for c in range(3):
            push[c, kz] = mo[kz, c * 16 : c * 16 + 16, :]
            push[c, kz, 0:8, :] = push[c, kz, 0:8, :] + rl[kz, 32 + c * 8 : 40 + c * 8, :]
            for x in range(4):
                at = 32 + c * 8 + x * 2
                push[c, kz, x * 4 : x * 4 + 2, :] = push[c, kz, x * 4 : x * 4 + 2, :] + rb[kz, at : at + 2, :]
            for x in range(2):
                at = 32 + c * 4 + x * 2
                push[c, kz, x * 4 : x * 4 + 2, :] = push[c, kz, x * 4 : x * 4 + 2, :] + rd[kz, at : at + 2, :]
        for x in range(4):
            for c in range(2):
                push[3 + c, kz, x * 4 : x * 4 + 4, :] = (
                    warm[0, kz, (x + 2) * 6 + 2 : (x + 2) * 6 + 6, :]
                    if c == 0
                    else region[0, kz, (x + 2) * 6 + 2 : (x + 2) * 6 + 6, :]
                )
    width_x = 4 * lax.axis_size("gx")
    height_z = 512
    spin = 2.0 / height_z
    shape = (16, 128)
    cell_x = lax.broadcasted_iota(jnp.int32, shape, 0) // 4 - 1 + 4 * lax.axis_index("gx")
    cell_x = jnp.where(cell_x < 0, cell_x + width_x, cell_x).astype(f32)
    wall_w = -spin * (cell_x + 0.5 - 0.5 * width_x)
    for kz in range(4):
        cell_z = (lax.broadcasted_iota(jnp.int32, shape, 1) * 4 + kz).astype(f32)
        wall = [spin * (cell_z + 0.5 - 0.5 * height_z), jnp.zeros(shape, f32), wall_w]
        inverse = 1.0 / jnp.maximum(push[3, kz], mass_floor)
        moving = [push[a, kz] * inverse for a in range(3)]
        moving[2] = moving[2] - gravity_step
        relative = [moving[a] - wall[a] for a in range(3)]
        facing = [normal[a, kz] for a in range(3)]
        normal_part = sum(relative[a] * facing[a] for a in range(3))
        tangent = [relative[a] - normal_part * facing[a] for a in range(3)]
        length = jnp.sqrt(sum(part * part for part in tangent))
        factor = jnp.maximum(
            0.0, 1.0 + friction * normal_part / jnp.maximum(length, slip_floor)
        )
        slips = (rough[kz] == 1.0) & (normal_part < 0.0)
        solid = push[4, kz] == 1.0
        for a in range(3):
            value = jnp.where(slips, wall[a] + tangent[a] * factor, moving[a])
            push[a, kz] = jnp.where(solid, wall[a], value)
        heat = warm[1, kz, 0:36, :] / jnp.maximum(warm[0, kz, 0:36, :], mass_floor)
        warm[1, kz, 0:36, :] = jnp.where(region[0, kz] == 1.0, region[1, kz], heat)
    for kz in range(4):
        ko[kz, 0:36, :] = warm[1, kz, 0:36, :]
        ko[kz, 36:40, :] = jnp.zeros((4, 128), f32)
        hl[kz, 0:24, :] = warm[1, kz, 12:36, :]
        for c in range(3):
            ko[kz, 40 + c * 16 : 56 + c * 16, :] = push[c, kz]
            hl[kz, 24 + c * 8 : 32 + c * 8, :] = push[c, kz, 0:8, :]
            for x in range(4):
                at = 24 + c * 8 + x * 2
                hb[kz, at : at + 2, :] = push[c, kz, x * 4 : x * 4 + 2, :]
            for x in range(2):
                at = 16 + c * 4 + x * 2
                hd[kz, at : at + 2, :] = push[c, kz, x * 4 : x * 4 + 2, :]
        for x in range(6):
            hb[kz, x * 4 : x * 4 + 4, :] = warm[1, kz, x * 6 + 2 : x * 6 + 6, :]
        for x in range(4):
            hd[kz, x * 4 : x * 4 + 4, :] = warm[1, kz, (x + 2) * 6 + 2 : (x + 2) * 6 + 6, :]
        hd[kz, 28:32, :] = jnp.zeros((4, 128), f32)


def collect_kernel(
    code_s, brick_s, came_s, ko, rl, rb, rd, solid, frac, o_ref, rxp, rxm, ryp, rym,
    move_ref, grad_ref, warm_ref, gvel_ref, gtemp_ref,
    heat, speed, cells, fine, coarse, turn, lu, fo, sb, sw, sb2, sw2,
):
    lane = lax.broadcasted_iota(jnp.int32, (8, 128), 1)[0:1]
    heat[...] = jnp.zeros(heat.shape, f32)
    for kz in range(4):
        for x in range(6):
            to = 16 + x * 10
            heat[0, kz, to : to + 6, :] = ko[kz, x * 6 : x * 6 + 6, :]
            heat[0, kz, to + 6 : to + 10, :] = rb[kz, x * 4 : x * 4 + 4, :]
        for x in range(4):
            to = 16 + (x + 6) * 10
            heat[0, kz, to : to + 6, :] = rl[kz, x * 6 : x * 6 + 6, :]
            heat[0, kz, to + 6 : to + 10, :] = rd[kz, x * 4 : x * 4 + 4, :]
        for c in range(3):
            for x in range(4):
                speed[c, kz, x * 6 : x * 6 + 4, :] = ko[kz, 40 + c * 16 + x * 4 : 44 + c * 16 + x * 4, :]
                at = 24 + c * 8 + x * 2
                speed[c, kz, x * 6 + 4 : x * 6 + 6, :] = rb[kz, at : at + 2, :]
            for x in range(2):
                at = 24 + c * 8 + x * 4
                speed[c, kz, 24 + x * 6 : 28 + x * 6, :] = rl[kz, at : at + 4, :]
                at = 16 + c * 4 + x * 2
                speed[c, kz, 28 + x * 6 : 30 + x * 6, :] = rd[kz, at : at + 2, :]
    for sweep in range(2):
        now, later = sweep, sweep + 1
        layers = [heat[now, kz, 16:120, :] for kz in range(4)]
        above = jnp.where(lane == 127, layers[3], pltpu.roll(layers[0], 127, 1))
        below = jnp.where(lane == 0, layers[0], pltpu.roll(layers[3], 1, 1))
        for kz in range(4):
            upper = layers[kz + 1] if kz < 3 else above
            lower = layers[kz - 1] if kz else below
            laplace = (
                heat[now, kz, 6:110, :]
                + heat[now, kz, 26:130, :]
                + heat[now, kz, 15:119, :]
                + heat[now, kz, 17:121, :]
                + upper
                + lower
                - 6.0 * layers[kz]
            )
            heat[later, kz, 16:120, :] = jnp.where(
                solid[kz] == 1.0, heat[0, kz, 16:120, :], layers[kz] + conduct * laplace
            )
    for kz in range(4):
        for x in range(6):
            to = 16 + (x + 2) * 10 + 2
            speed[3, kz, x * 6 : x * 6 + 6, :] = heat[2, kz, to : to + 6, :]
    for c in range(4):
        for kz in range(4):
            for x in range(4):
                at = (x + 1) * 6 + 1
                cells[c * 16 + x * 4 : c * 16 + x * 4 + 4, kz * 128 : kz * 128 + 128] = speed[c, kz, at : at + 4, :]
    source = lax.broadcasted_iota(jnp.int32, (512, 512), 0)
    wanted = (source % 128) * 4 + source // 128
    permute = (wanted == lax.broadcasted_iota(jnp.int32, (512, 512), 1)).astype(f32).astype(bf16)
    value = cells[...]
    high, rest = split_two(value)
    middle, low = split_two(rest)
    spread = jnp.concatenate([high, middle, low], axis=0).astype(bf16)
    spread = jnp.dot(spread, permute, preferred_element_type=f32)
    value = spread[0:64] + spread[64:128] + spread[128:192]
    for x in range(4):
        for c in range(3):
            gvel_ref[c, x] = value[c * 16 + x * 4 : c * 16 + x * 4 + 4]
        gtemp_ref[x] = value[48 + x * 4 : 52 + x * 4]
    for c in range(4):
        for jz in range(6):
            kz = (jz - 1) % 4
            layer = speed[c, kz]
            if jz == 0:
                layer = jnp.where(lane == 0, 0.0, pltpu.roll(layer, 1, 1))
            if jz == 5:
                layer = jnp.where(lane == 127, 0.0, pltpu.roll(layer, 127, 1))
            high, low = split_two(layer)
            coarse[c, jz] = high
            fine[c, jz] = low
    turn[...] = jnp.zeros(turn.shape, f32)
    for jx in range(6):
        for c in range(4):
            side = c % 2
            for jz in range(6):
                rows = slice(jx * 6, jx * 6 + 6)
                turn[side, jz * 6 : jz * 6 + 6, :] = coarse[c, jz, rows, :]
                turn[side, 40 + jz * 6 : 46 + jz * 6, :] = fine[c, jz, rows, :]
                turn[side, 80 + jz * 6 : 86 + jz * 6, :] = coarse[c, jz, rows, :]
            lu[pl.ds(jx * 4 + c, 128, stride=24), :] = jnp.transpose(turn[side])
    for d in range(3):
        fo[d, 0:128, :] = frac[d]
    fo[3, 0:128, :] = o_ref[...].astype(f32)
    places = [(ryp, 0), (rxp, 1), (rym, 0), (ryp, 1), (rym, 1), (ryp, 2), (rxm, 1), (rym, 2)]
    for g, (ref, at) in enumerate(places):
        for d in range(4):
            fo[d, 128 + g * 16 : 144 + g * 16, :] = ref[pl.ds(at * way_rows + d, 16, stride=4), :]
    sb[...] = jnp.zeros(sb.shape, f32)
    sb2[...] = jnp.zeros(sb2.shape, f32)

    def build(g, sb, sw):
        rows = pl.ds(pl.multiple_of(g * 8, 8), 8)
        offset = fo[3, rows, :].astype(jnp.int32)
        wx, rx = axis_tables(offset >> 4, fo[0, rows, :], 4.0)
        for j in range(6):
            for copy in range(4):
                sw[pl.ds((j * 4 + copy) * 8, 8), :] = wx[j]
                sw[pl.ds((24 + j * 4 + copy) * 8, 8), :] = rx[j]
        wy, ry = axis_tables((offset >> 2) & 3, fo[1, rows, :], 4.0)
        wz, rz = axis_tables(offset & 3, fo[2, rows, :], 4.0)
        for jz in range(6):
            for jy in range(6):
                r = jz * 6 + jy
                sb[pl.ds(r * 8, 8), :] = wy[jy] * wz[jz]
                sb[pl.ds((40 + r) * 8, 8), :] = ry[jy] * wz[jz]
                sb[pl.ds((80 + r) * 8, 8), :] = wy[jy] * rz[jz]

    def work(g, sb, sw):
        for j in range(8):
            slot = g * 8 + j
            home = jnp.minimum(slot, 127)
            stays = jnp.where(code_s[home] == 4, brick_s[home], -1)
            brick = jnp.where(slot < 128, stays, came_s[0, jnp.maximum(slot - 128, 0)])
            live = jnp.where(brick >= 0, 1.0, 0.0).astype(f32)
            spot = pl.ds(pl.multiple_of(jnp.maximum(brick, 0) * 24, 8), 24)
            left = lu[spot, :].astype(bf16)
            right = jnp.concatenate(
                [sb[pl.ds(n * 320 + j, 40, stride=8), :] for n in range(3)], axis=1
            )
            high, low = split_two(right)
            right = jnp.concatenate([high, high, low, jnp.zeros((8, 384), f32)], axis=0).astype(bf16)
            both = jnp.dot(left, right, preferred_element_type=f32)
            plain = sw[pl.ds(j, 24, stride=8), :]
            tilt = sw[pl.ds(192 + j, 24, stride=8), :]

            def over_x(weight, column):
                part = weight * both[:, column * 128 : column * 128 + 128]
                part = part[0:8] + part[8:16] + part[16:24]
                return (part[0:4] + part[4:8]) * live

            lanes = pl.ds(pl.multiple_of(slot * 128, 128), 128)
            moved = over_x(plain, 0)
            move_ref[:, lanes] = moved[0:3]
            warm_ref[pl.ds(slot, 1), :] = moved[3:4]
            for k, (weight, column) in enumerate(((tilt, 0), (plain, 1), (plain, 2))):
                part = over_x(weight, column)
                for a in range(3):
                    grad_ref[a * 3 + k : a * 3 + k + 1, lanes] = part[a : a + 1]

    def pair(i, carry):
        build(2 * i + 1, sb2, sw2)
        work(2 * i, sb, sw)
        build(jnp.minimum(2 * i + 2, 31), sb, sw)
        work(2 * i + 1, sb2, sw2)
        return carry

    build(0, sb, sw)
    lax.fori_loop(0, 16, pair, 0)


def neighbor(value, dx, dy):
    size_x, size_y = lax.axis_size("gx"), lax.axis_size("gy")
    if dy == 0:
        return lax.ppermute(value, "gx", [(i, (i + dx) % size_x) for i in range(size_x)])
    if dx == 0:
        return lax.ppermute(value, "gy", [(i, (i + dy) % size_y) for i in range(size_y)])
    pairs = [
        (i * size_y + j, (i + dx) % size_x * size_y + (j + dy) % size_y)
        for i in range(size_x)
        for j in range(size_y)
    ]
    return lax.ppermute(value, ("gx", "gy"), pairs)


def call(
    kernel, name, inputs, scalars, outputs, scratch, left_there=0, limit=50, flops=1e8, listed=0
):
    in_specs = (
        [pl.BlockSpec(memory_space=pltpu.SMEM)] * scalars
        + [pl.BlockSpec(memory_space=pltpu.HBM)] * left_there
        + [pl.BlockSpec(memory_space=pltpu.VMEM)] * (len(inputs) - scalars - left_there)
    )
    return pl.pallas_call(
        kernel,
        name=name,
        out_shape=[jax.ShapeDtypeStruct(shape, dtype) for shape, dtype in outputs],
        in_specs=in_specs,
        out_specs=[pl.BlockSpec(memory_space=pltpu.SMEM)] * listed
        + [pl.BlockSpec(memory_space=pltpu.VMEM)] * (len(outputs) - listed),
        cost_estimate=pl.CostEstimate(
            flops=int(flops), bytes_accessed=int(flops / 300), transcendentals=0
        ),
        scratch_shapes=scratch,
        compiler_params=pltpu.CompilerParams(vmem_limit_bytes=limit * mib),
    )(
        *inputs[:scalars],
        *[pltpu.with_memory_space_constraint(x, pltpu.HBM) for x in inputs[scalars : scalars + left_there]],
        *inputs[scalars + left_there :],
    )


def vmem(*shape):
    return pltpu.VMEM(shape, f32)


def on_device(
    subvoxel_location_share,
    point_motion_vector,
    linear_gradient_matrix,
    kirchhoff_tension_matrix,
    point_inertia_amounts,
    point_thermal_state,
    anchor_voxel_shift,
    group_resting_volume,
    group_migration_label,
    cylinder_shell_flag,
    rough_surface_flag,
    voxel_facing_choice,
    facing_unit_vectors,
    rim_thermal_level,
):
    offset = anchor_voxel_shift.reshape(128, 128)
    info, static, sxp, sxm, *block_args = call(
        prepare_kernel,
        "prepare",
        (
            facing_unit_vectors,
            group_migration_label,
            cylinder_shell_flag,
            rough_surface_flag,
            voxel_facing_choice,
            rim_thermal_level,
            group_resting_volume,
            subvoxel_location_share,
            point_motion_vector,
            linear_gradient_matrix,
            kirchhoff_tension_matrix,
            point_inertia_amounts.reshape(128, 128),
            point_thermal_state.reshape(128, 128),
            offset,
        ),
        0,
        [
            ((768,), jnp.int32),
            ((6, 96, 128), f32),
            ((352, 128), f32),
            ((224, 128), f32),
            ((3, 16384), f32),
            ((3, 16384), f32),
            ((9, 16384), f32),
            ((9, 16384), f32),
            ((128, 128), f32),
            ((128, 128), f32),
            ((128, 128), jnp.int32),
        ],
        [
            pltpu.SMEM((3, 64), f32),
            pltpu.SMEM((128,), jnp.int32),
            pltpu.SMEM((128,), jnp.int32),
            pltpu.VMEM((4, 4, 512), jnp.int32),
            pltpu.VMEM((4, 4, 512), jnp.int32),
            pltpu.VMEM((4, 4, 512), jnp.int32),
            vmem(4, 4, 512),
            pltpu.SemaphoreType.DMA((14,)),
            vmem(64, 512),
            vmem(520, 128),
            pltpu.SMEM((16,), jnp.int32),
        ],
        14,
        24,
        flops=2e9,
        listed=1,
    )
    rsxp = neighbor(sxp, 1, 0)
    rsxm = neighbor(sxm, -1, 0)
    block_scratch = [
        vmem(320, 128),
        vmem(96 * 8, 128),
        vmem(120 * 8, 128),
        vmem(320, 128),
        vmem(96 * 8, 128),
        vmem(120 * 8, 128),
        vmem(130 * 40, 128),
    ]
    xm, ym, yp, xp = call(
        outgoing_kernel,
        "outgoing",
        (info, *block_args),
        1,
        [
            ((3 * msg_rows, 128), f32),
            ((msg_rows, 128), f32),
            ((msg_rows, 128), f32),
            ((3 * msg_rows, 128), f32),
        ],
        block_scratch,
        limit=24,
        flops=6e9,
    )
    xm, xp, rsxp, rsxm = lax.optimization_barrier((xm, xp, rsxp, rsxm))
    rxp = neighbor(xp, 1, 0)
    rxm = neighbor(xm, -1, 0)
    up, down = call(
        relay_kernel,
        "relay",
        (rsxp, rsxm, static),
        0,
        [((448, 128), f32), ((288, 128), f32)],
        [],
        flops=5e8,
    )
    rsyp = neighbor(up, 0, 1)
    rsym = neighbor(down, 0, -1)
    up = jnp.concatenate([rxp[2 * msg_rows :], yp, rxm[2 * msg_rows :]], axis=0)
    down = jnp.concatenate([rxp[:msg_rows], ym, rxm[:msg_rows]], axis=0)
    up, down, info = lax.optimization_barrier((up, down, info))
    ryp = neighbor(up, 0, 1)
    rym = neighbor(down, 0, -1)
    own, frac = call(
        staying_kernel,
        "staying",
        (info, *block_args),
        1,
        [((tiles, 128, 128), f32), ((3, 128, 128), f32)],
        block_scratch,
        limit=24,
        flops=1e10,
    )
    region, rough, normal, solid = call(
        assemble_kernel,
        "assemble",
        (static, rsxp, rsxm, rsyp, rsym),
        0,
        [
            ((2, 4, 36, 128), f32),
            ((4, 16, 128), f32),
            ((3, 4, 16, 128), f32),
            ((4, 104, 128), f32),
        ],
        [],
        flops=5e8,
    )

    ml, mb, md, mo, came = call(
        total_kernel,
        "total",
        (own, rxp, rxm, ryp, rym),
        0,
        [
            ((4, 56, 128), f32),
            ((4, 56, 128), f32),
            ((4, 48, 128), f32),
            ((4, 80, 128), f32),
            ((1, 128), jnp.int32),
        ],
        [vmem(tiles * 128, 128), vmem(4, 184, 128)],
    )
    hl, hb, hd, ko = call(
        update_kernel,
        "update",
        (mo, neighbor(ml, 1, 0), neighbor(mb, 0, 1), neighbor(md, 1, 1), region, rough, normal),
        0,
        [
            ((4, 48, 128), f32),
            ((4, 48, 128), f32),
            ((4, 32, 128), f32),
            ((4, 88, 128), f32),
        ],
        [vmem(2, 4, 40, 128), vmem(5, 4, 16, 128)],
    )
    move, grad, warm, gvel, gtemp = call(
        collect_kernel,
        "collect",
        (
            group_migration_label,
            group_resting_volume,
            came,
            ko,
            neighbor(hl, -1, 0),
            neighbor(hb, 0, -1),
            neighbor(hd, -1, -1),
            solid,
            frac,
            offset,
            rsxp,
            rsxm,
            rsyp,
            rsym,
        ),
        3,
        [
            ((3, 32768), f32),
            ((9, 32768), f32),
            ((256, 128), f32),
            ((3, 4, 4, 512), f32),
            ((4, 4, 512), f32),
        ],
        [
            vmem(3, 4, 136, 128),
            vmem(4, 4, 40, 128),
            vmem(64, 512),
            vmem(4, 6, 40, 128),
            vmem(4, 6, 40, 128),
            vmem(2, 128, 128),
            vmem(128 * 24, 128),
            vmem(4, 256, 128),
            vmem(120 * 8, 128),
            vmem(48 * 8, 128),
            vmem(120 * 8, 128),
            vmem(48 * 8, 128),
        ],
    )
    return move, grad, warm.reshape(-1), gvel, gtemp


def solution(mesh):
    in_specs = (
        P(None, ("gx", "gy")),
        P(None, ("gx", "gy")),
        P(None, ("gx", "gy")),
        P(None, ("gx", "gy")),
        P(("gx", "gy")),
        P(("gx", "gy")),
        P(("gx", "gy")),
        P(("gx", "gy")),
        P(("gx", "gy")),
        P("gx", "gy", None),
        P("gx", "gy", None),
        P("gx", "gy", None),
        P(),
        P("gx", "gy", None),
    )
    out_specs = (
        P(None, ("gx", "gy")),
        P(None, ("gx", "gy")),
        P(("gx", "gy")),
        P(None, "gx", "gy", None),
        P("gx", "gy", None),
    )
    return jax.shard_map(
        on_device, mesh=mesh, in_specs=in_specs, out_specs=out_specs, check_vma=False
    )
```

```python
import jax
import jax.numpy as jnp
from jax import lax
from jax.experimental import pallas as pl
from jax.experimental.pallas import tpu as pltpu
from jax.sharding import PartitionSpec as P

f32 = jnp.float32
bf16 = jnp.bfloat16
mass_floor = 0.25
slip_floor = 0.1
friction = 0.4
gravity_step = 0.5
conduct = 0.15
stress_coef = 0.25
mib = 1024 * 1024
pieces = 31
tiles = 9
msg_rows = tiles * 16
way_rows = 64


def axis_tables(shift, inside, scale):
    near = 0.5 * (1.5 - inside) ** 2
    middle = 0.75 - (inside - 1.0) ** 2
    far = 0.5 * (inside - 0.5) ** 2
    at = [shift == step for step in range(4)]
    zero = jnp.zeros_like(inside)
    weight = [
        jnp.where(at[0], near, zero),
        jnp.where(at[0], middle, jnp.where(at[1], near, zero)),
        jnp.where(at[0], far, jnp.where(at[1], middle, jnp.where(at[2], near, zero))),
        jnp.where(at[1], far, jnp.where(at[2], middle, jnp.where(at[3], near, zero))),
        jnp.where(at[2], far, jnp.where(at[3], middle, zero)),
        jnp.where(at[3], far, zero),
    ]
    place = shift.astype(f32) + inside
    first = [weight[step] * (scale * (step - place)) for step in range(6)]
    return weight, first


def split_two(value):
    high = value.astype(bf16).astype(f32)
    return high, value - high


def clear_rows(ref, rows):
    def step(n, carry):
        ref[pl.ds(pl.multiple_of(n * 128, 128), 128), :] = jnp.zeros((128, 128), f32)
        return carry

    lax.fori_loop(0, rows // 128, step, 0)


def deposit_blocks(
    base, count, info_s, target_of, refs, first, second, acc, after
):
    f_ref, v_ref, c_ref, k_ref, m_ref, t_ref, o_ref = refs
    clear_rows(acc, 128 * 40)
    for _, sa, sb in (first, second):
        sa[...] = jnp.zeros(sa.shape, f32)
        sb[...] = jnp.zeros(sb.shape, f32)
    row_no = lax.broadcasted_iota(jnp.int32, (32, 1), 0)

    def build(g, raw, sa, sb):
        blocks = [info_s[base + g * 8 + j] for j in range(8)]
        for j in range(8):
            lanes = pl.ds(pl.multiple_of(blocks[j] * 128, 128), 128)
            raw[j * 40 : j * 40 + 3, :] = f_ref[:, lanes]
            raw[j * 40 + 3 : j * 40 + 6, :] = v_ref[:, lanes]
            raw[j * 40 + 6 : j * 40 + 7, :] = m_ref[pl.ds(blocks[j], 1), :]
            raw[j * 40 + 7 : j * 40 + 8, :] = t_ref[pl.ds(blocks[j], 1), :]
            raw[j * 40 + 8 : j * 40 + 17, :] = c_ref[:, lanes]
            raw[j * 40 + 24 : j * 40 + 33, :] = k_ref[:, lanes]
            raw[j * 40 + 33 : j * 40 + 34, :] = o_ref[pl.ds(blocks[j], 1), :].astype(f32)

        def get(row):
            return raw[pl.ds(row, 8, stride=40), :]

        mass = get(6)
        heat = mass * get(7)
        offset = get(33).astype(jnp.int32)
        inside = [get(d) for d in range(3)]
        wx, rx = axis_tables(offset >> 4, inside[0], 1.0)
        for a in range(3):
            push = mass * get(3 + a)
            q = [
                mass * get(8 + a * 3 + k) - stress_coef * get(24 + a * 3 + k) for k in range(3)
            ]
            for j in range(6):
                sa[pl.ds((a * 6 + j) * 8, 8), :] = push * wx[j] + q[0] * rx[j]
                sa[pl.ds((32 + a * 6 + j) * 8, 8), :] = q[1] * wx[j]
                sa[pl.ds((64 + a * 6 + j) * 8, 8), :] = q[2] * wx[j]
        for j in range(6):
            sa[pl.ds((18 + j) * 8, 8), :] = mass * wx[j]
            sa[pl.ds((24 + j) * 8, 8), :] = heat * wx[j]
        wy, ry = axis_tables((offset >> 2) & 3, inside[1], 1.0)
        wz, rz = axis_tables(offset & 3, inside[2], 1.0)
        for jy in range(6):
            for jz in range(6):
                r = jy * 6 + jz
                sb[pl.ds(r * 8, 8), :] = wy[jy] * wz[jz]
                sb[pl.ds((40 + r) * 8, 8), :] = ry[jy] * wz[jz]
                sb[pl.ds((80 + r) * 8, 8), :] = wy[jy] * rz[jz]

    def work(g, raw, sa, sb):
        blocks = [info_s[base + g * 8 + j] for j in range(8)]
        sums = []
        for j in range(8):
            left = jnp.concatenate(
                [sa[pl.ds(n * 256 + j, 32, stride=8), :] for n in range(3)], axis=1
            )
            right = jnp.concatenate(
                [sb[pl.ds(n * 320 + j, 40, stride=8), :] for n in range(3)], axis=1
            )
            left = jnp.concatenate(split_two(left), axis=0).astype(bf16)
            right = jnp.concatenate(split_two(right), axis=0).astype(bf16)
            both = lax.dot_general(
                left, right, (((1,), (1,)), ((), ())), preferred_element_type=f32
            )
            both = both[:32] + both[32:]
            sums.append(both[:, :40] + both[:, 40:])
        for j in range(8):
            target, mark = target_of(g * 8 + j, blocks[j])
            spot = pl.ds(pl.multiple_of(target * 40, 8), 32)
            acc[spot, 0:40] = acc[spot, 0:40] + (sums[j] + jnp.where(row_no == 30, mark, 0.0))
            after(j, blocks[j], raw)

    def pair(i, carry):
        build(2 * i + 1, *second)
        work(2 * i, *first)
        build(2 * i + 2, *first)
        work(2 * i + 1, *second)
        return carry

    build(0, *first)
    lax.fori_loop(0, (count + 15) // 16, pair, 0)


def packed(acc, chunk):
    lane = lax.broadcasted_iota(jnp.int32, (8, 128), 1)
    total = [jnp.zeros((8, 128), f32) for _ in range(tiles)]
    for i in range(pieces):
        piece = acc[pl.ds(chunk * 320 + i, 8, stride=40), :]
        if i == 30:
            piece = jnp.where(lane < 36, piece, 0.0)
        tile, at = divmod(i * 36, 128)
        if at:
            piece = pltpu.roll(piece, at, 1)
        if at + 36 > 128:
            total[tile] = total[tile] + jnp.where(lane >= at, piece, 0.0)
            total[tile + 1] = total[tile + 1] + jnp.where(lane < at, piece, 0.0)
        else:
            total[tile] = total[tile] + piece
    return total


def outgoing_kernel(
    info_s, f_ref, v_ref, c_ref, k_ref, m_ref, t_ref, o_ref,
    xm_ref, ym_ref, yp_ref, xp_ref,
    raw, sa, sb, raw2, sa2, sb2, acc,
):
    def target_of(entry, block):
        return info_s[160 + entry], (info_s[640 + block] + 1).astype(f32)

    deposit_blocks(
        0, info_s[544], info_s, target_of,
        (f_ref, v_ref, c_ref, k_ref, m_ref, t_ref, o_ref),
        (raw, sa, sb), (raw2, sa2, sb2), acc, lambda j, block, raw: None,
    )
    for first, count, ref in ((0, 3, xm_ref), (3, 1, ym_ref), (4, 1, yp_ref), (5, 3, xp_ref)):
        for n in range(count):
            for half in range(2):

                def some(n=n, half=half, first=first, ref=ref):
                    for tile, value in enumerate(packed(acc, (first + n) * 2 + half)):
                        at = n * msg_rows + tile * 16 + half * 8
                        ref[at : at + 8, :] = value

                def none(n=n, half=half, ref=ref):
                    for tile in range(tiles):
                        at = n * msg_rows + tile * 16 + half * 8
                        ref[at : at + 8, :] = jnp.zeros((8, 128), f32)

                lax.cond(info_s[552 + first + n] > half * 8, some, none)


def staying_kernel(
    info_s, f_ref, v_ref, c_ref, k_ref, m_ref, t_ref, o_ref,
    own_ref, frac_ref,
    raw, sa, sb, raw2, sa2, sb2, acc,
):
    frac_ref[...] = jnp.zeros(frac_ref.shape, f32)

    def target_of(entry, block):
        return jnp.where(entry < info_s[545], info_s[640 + block], 128), jnp.float32(0.0)

    def after(j, block, raw):
        for d in range(3):
            frac_ref[d, pl.ds(block, 1), :] = raw[j * 40 + d : j * 40 + d + 1, :]

    deposit_blocks(
        320, info_s[545], info_s, target_of,
        (f_ref, v_ref, c_ref, k_ref, m_ref, t_ref, o_ref),
        (raw, sa, sb), (raw2, sa2, sb2), acc, after,
    )

    def pack_own(chunk, carry):
        for tile, value in enumerate(packed(acc, chunk)):
            own_ref[tile, pl.ds(pl.multiple_of(chunk * 8, 8), 8), :] = value
        return carry

    lax.fori_loop(0, 16, pack_own, 0)


def runs_left():
    return (
        [(3, x, 0, 4) for x in range(2, 6)]
        + [(4, x, 0, 4) for x in range(2, 6)]
        + [(c, x, 0, 4) for c in range(3) for x in (4, 5)]
    )


def runs_below():
    return (
        [(3, x, 2, 4) for x in range(4)]
        + [(4, x, 2, 4) for x in range(4)]
        + [(c, x, 4, 2) for c in range(3) for x in range(4)]
    )


def runs_diagonal():
    return (
        [(3, x, 2, 4) for x in range(2, 6)]
        + [(4, x, 2, 4) for x in range(2, 6)]
        + [(c, x, 4, 2) for c in range(3) for x in (4, 5)]
    )


def runs_own():
    return [(c, x, 0, 4) for c in range(5) for x in range(4)]


def total_kernel(own_ref, rxp, rxm, ryp, rym, ml, mb, md, mo, brick_ref, wide, grid):
    places = [(ryp, 0), (rxp, 1), (rym, 0), (ryp, 1), (rym, 1), (ryp, 2), (rxm, 1), (rym, 2)]

    def arrived(tile):
        return jnp.concatenate(
            [ref[pl.ds(at * msg_rows + tile * 16, 16), :] for ref, at in places], axis=0
        )

    rows = lax.broadcasted_iota(jnp.int32, (128, 128), 0)
    lanes = lax.broadcasted_iota(jnp.int32, (128, 128), 1)
    column = arrived(8)[:, 56:57]
    row = jnp.sum(jnp.where(rows == lanes, column, 0.0), axis=0, keepdims=True)
    brick_ref[...] = row.astype(jnp.int32) - 1
    hits = (row == (rows + 1).astype(f32)).astype(f32).astype(bf16)
    hits = jnp.concatenate([hits, hits], axis=1)
    for tile in range(tiles):
        high, low = split_two(arrived(tile))
        stack = jnp.concatenate([high.astype(bf16), low.astype(bf16)], axis=0)
        value = own_ref[tile] + jnp.dot(hits, stack, preferred_element_type=f32)
        wide[tile * 128 : tile * 128 + 128, :] = jnp.transpose(value)
    lane = lax.broadcasted_iota(jnp.int32, (184, 128), 1)

    def layer(jz):
        return wide[pl.ds(jz, 184, stride=6), :]

    grid[0] = layer(1) + jnp.where(lane == 0, 0.0, pltpu.roll(layer(5), 1, 1))
    grid[1] = layer(2)
    grid[2] = layer(3)
    grid[3] = layer(4) + jnp.where(lane == 127, 0.0, pltpu.roll(layer(0), 127, 1))
    for ref, runs in ((ml, runs_left()), (mb, runs_below()), (md, runs_diagonal()), (mo, runs_own())):
        for kz in range(4):
            to = 0
            for c, x, y, count in runs:
                ref[kz, to : to + count, :] = grid[kz, c * 36 + x * 6 + y : c * 36 + x * 6 + y + count, :]
                to += count
            if to < ref.shape[1]:
                ref[kz, to:, :] = jnp.zeros((ref.shape[1] - to, 128), f32)


def prepare_kernel(
    table_hbm, code_hbm, solid_hbm, rough_hbm, choice_hbm, rim_hbm,
    brick_hbm, f_hbm, v_hbm, c_hbm, k_hbm, m_hbm, t_hbm, o_hbm,
    info, own, xp, xm, f_ref, v_ref, c_ref, k_ref, m_ref, t_ref, o_ref,
    table, code_s, brick_s, solid_ref, rough_ref, choice_ref, rim_ref, sems,
    cells, fo, cnt,
):
    pairs = (
        (code_hbm, code_s), (f_hbm, f_ref), (o_hbm, o_ref), (table_hbm, table),
        (solid_hbm, solid_ref), (rough_hbm, rough_ref), (choice_hbm, choice_ref), (rim_hbm, rim_ref),
        (brick_hbm, brick_s), (v_hbm, v_ref), (c_hbm, c_ref), (k_hbm, k_ref), (m_hbm, m_ref),
        (t_hbm, t_ref),
    )
    copies = [pltpu.make_async_copy(a, b, sems.at[n]) for n, (a, b) in enumerate(pairs)]
    for copy in copies:
        copy.start()
    fo[...] = jnp.zeros(fo.shape, f32)
    for copy in copies[:9]:
        copy.wait()
    for n in range(10):
        cnt[n] = 0

    def sort(b, carry):
        code = code_s[b]
        rank = cnt[code]
        cnt[code] = rank + 1
        leaves = code != 4
        way = jnp.where(code > 4, code - 1, code)
        gone = cnt[9]
        slot = way * 16 + rank
        info[jnp.where(leaves, gone, 320 + b - gone)] = b
        info[640 + b] = brick_s[b]
        info[jnp.where(leaves, 160 + gone, 639)] = slot
        cnt[9] = gone + jnp.where(leaves, 1, 0)
        at = pl.multiple_of(jnp.where(leaves, slot, 128) * 4, 4)
        lanes = pl.ds(pl.multiple_of(b * 128, 128), 128)
        fo[pl.ds(at, 3), :] = f_ref[:, lanes]
        fo[pl.ds(at + 3, 1), :] = o_ref[pl.ds(b, 1), :].astype(f32)
        return carry

    lax.fori_loop(0, 128, sort, 0, unroll=4)
    gone = cnt[9]
    for n in range(24):
        info[gone + n] = 0
        info[160 + gone + n] = 128
        info[320 + 128 - gone + n] = 0
    for n in range(8):
        info[552 + n] = cnt[n if n < 4 else n + 1]
    info[544] = gone
    info[545] = 128 - gone
    for x in range(4):
        rows = slice(x * 4, x * 4 + 4)
        cells[rows, :] = solid_ref[x].astype(f32)
        cells[16 + x * 4 : 20 + x * 4, :] = rough_ref[x].astype(f32)
        cells[32 + x * 4 : 36 + x * 4, :] = choice_ref[x].astype(f32)
        cells[48 + x * 4 : 52 + x * 4, :] = rim_ref[x]
    value = cells[...]
    high, rest = split_two(value[48:64])
    middle, low = split_two(rest)
    value = jnp.concatenate([value[0:48], high, middle, low], axis=0).astype(bf16)
    source = lax.broadcasted_iota(jnp.int32, (512, 512), 0)
    wanted = (source % 4) * 128 + source // 4
    permute = (wanted == lax.broadcasted_iota(jnp.int32, (512, 512), 1)).astype(f32).astype(bf16)
    value = jnp.dot(value, permute, preferred_element_type=f32)
    rim = value[48:64] + value[64:80] + value[80:96]
    choice = value[32:48]
    normal = [jnp.zeros(choice.shape, f32) for _ in range(3)]
    for n in range(table.shape[1]):
        hit = choice == float(n)
        normal = [jnp.where(hit, table[d, n], normal[d]) for d in range(3)]
    for kz in range(4):
        lanes = slice(kz * 128, kz * 128 + 128)
        for field, part in enumerate((value[0:16], rim, value[16:32], *normal)):
            own[kz, field * 16 : field * 16 + 16, :] = part[:, lanes]
        at = 192 + kz * 40
        xp[at : at + 12, :] = own[kz, 4:16, :]
        xp[at + 12 : at + 24, :] = own[kz, 20:32, :]
        for field in range(4):
            row = 32 + field * 16
            xp[at + 24 + field * 4 : at + 28 + field * 4, :] = own[kz, row + 12 : row + 16, :]
        xm[192 + kz * 8 : 200 + kz * 8, :] = own[kz, 0:8, :]
    for copy in copies[9:]:
        copy.wait()
    xm[0:192, :] = fo[0:192, :]
    for way in range(2):
        own[4 + way, 0:64, :] = fo[192 + way * 64 : 256 + way * 64, :]
        own[4 + way, 64:96, :] = jnp.zeros((32, 128), f32)
    xp[0:192, :] = fo[320:512, :]


def relay_kernel(left, right, own, up, down):
    for way, ref in ((0, down), (1, up)):
        at = 128 * way
        ref[0:64, :] = left[at : at + 64, :]
        ref[64:128, :] = own[4 + way, 0:64, :]
        ref[128:192, :] = right[at : at + 64, :]
    for kz in range(4):
        lrow, rrow = 192 + kz * 40, 192 + kz * 8
        to = 192 + kz * 64
        for x in range(4):
            up[to + x * 3 : to + x * 3 + 3, :] = own[kz, x * 4 + 1 : x * 4 + 4, :]
        for x in range(3):
            row = 16 + x * 4
            up[to + 12 + x * 3 : to + 15 + x * 3, :] = own[kz, row + 1 : row + 4, :]
            up[to + 33 + x * 3 : to + 36 + x * 3, :] = left[lrow + x * 4 + 1 : lrow + x * 4 + 4, :]
            row = lrow + 12 + x * 4
            up[to + 42 + x * 3 : to + 45 + x * 3, :] = left[row + 1 : row + 4, :]
            for field in range(4):
                row = 32 + field * 16 + x * 4 + 3
                at = to + 21 + field * 3 + x
                up[at : at + 1, :] = own[kz, row : row + 1, :]
        for field in range(4):
            row = lrow + 24 + field * 4 + 3
            up[to + 51 + field : to + 52 + field, :] = left[row : row + 1, :]
        for x in range(2):
            up[to + 55 + x * 3 : to + 58 + x * 3, :] = right[rrow + x * 4 + 1 : rrow + x * 4 + 4, :]
        up[to + 61 : to + 64, :] = jnp.zeros((3, 128), f32)
        to = 192 + kz * 24
        for x in range(4):
            down[to + x * 2 : to + x * 2 + 2, :] = own[kz, x * 4 : x * 4 + 2, :]
        for x in range(3):
            down[to + 8 + x * 2 : to + 10 + x * 2, :] = left[lrow + x * 4 : lrow + x * 4 + 2, :]
        for x in range(2):
            down[to + 14 + x * 2 : to + 16 + x * 2, :] = right[rrow + x * 4 : rrow + x * 4 + 2, :]
        down[to + 18 : to + 24, :] = jnp.zeros((6, 128), f32)


def assemble_kernel(own, left, right, below, above, region, rough, normal, solid):
    solid[...] = jnp.zeros(solid.shape, f32)
    for kz in range(4):
        lrow, rrow, brow, arow = 192 + kz * 40, 192 + kz * 8, 192 + kz * 64, 192 + kz * 24
        for x in range(3):
            for field in range(2):
                inner, outer = x * 6, (x + 3) * 6
                diagonal = brow + 33 + field * 9 + x * 3
                region[field, kz, inner : inner + 3, :] = below[diagonal : diagonal + 3, :]
                row = lrow + field * 12 + x * 4
                region[field, kz, inner + 3 : inner + 6, :] = left[row : row + 3, :]
                row = brow + field * 12 + x * 3
                region[field, kz, outer : outer + 3, :] = below[row : row + 3, :]
                row = field * 16 + x * 4
                region[field, kz, outer + 3 : outer + 6, :] = own[kz, row : row + 3, :]
            to = x * 10
            solid[kz, to : to + 3, :] = below[brow + 33 + x * 3 : brow + 36 + x * 3, :]
            solid[kz, to + 3 : to + 7, :] = left[lrow + x * 4 : lrow + x * 4 + 4, :]
            solid[kz, to + 7 : to + 9, :] = above[arow + 8 + x * 2 : arow + 10 + x * 2, :]
        for x in range(4):
            to = (x + 3) * 10
            solid[kz, to : to + 3, :] = below[brow + x * 3 : brow + x * 3 + 3, :]
            solid[kz, to + 3 : to + 7, :] = own[kz, x * 4 : x * 4 + 4, :]
            solid[kz, to + 7 : to + 9, :] = above[arow + x * 2 : arow + x * 2 + 2, :]
        for x in range(2):
            to = (x + 7) * 10
            solid[kz, to : to + 3, :] = below[brow + 55 + x * 3 : brow + 58 + x * 3, :]
            solid[kz, to + 3 : to + 7, :] = right[rrow + x * 4 : rrow + x * 4 + 4, :]
            solid[kz, to + 7 : to + 9, :] = above[arow + 14 + x * 2 : arow + 16 + x * 2, :]
        for field in range(4):
            ref = rough if field == 0 else normal.at[field - 1]
            ref[kz, 0:1, :] = below[brow + 51 + field : brow + 52 + field, :]
            row = lrow + 24 + field * 4
            ref[kz, 1:4, :] = left[row : row + 3, :]
            for x in range(3):
                to = (x + 1) * 4
                row = brow + 21 + field * 3 + x
                ref[kz, to : to + 1, :] = below[row : row + 1, :]
                row = 32 + field * 16 + x * 4
                ref[kz, to + 1 : to + 4, :] = own[kz, row : row + 3, :]


def update_kernel(mo, rl, rb, rd, region, rough, normal, hl, hb, hd, ko, warm, push):
    warm[...] = jnp.zeros(warm.shape, f32)
    for kz in range(4):
        for ref, dx, dy in ((mo, 2, 2), (rl, 0, 2), (rb, 2, 0), (rd, 0, 0)):
            for c in range(2):
                for x in range(4):
                    at = (48 if ref is mo else 0) + c * 16 + x * 4
                    to = (x + dx) * 6 + dy
                    warm[c, kz, to : to + 4, :] = warm[c, kz, to : to + 4, :] + ref[kz, at : at + 4, :]
        for c in range(3):
            push[c, kz] = mo[kz, c * 16 : c * 16 + 16, :]
            push[c, kz, 0:8, :] = push[c, kz, 0:8, :] + rl[kz, 32 + c * 8 : 40 + c * 8, :]
            for x in range(4):
                at = 32 + c * 8 + x * 2
                push[c, kz, x * 4 : x * 4 + 2, :] = push[c, kz, x * 4 : x * 4 + 2, :] + rb[kz, at : at + 2, :]
            for x in range(2):
                at = 32 + c * 4 + x * 2
                push[c, kz, x * 4 : x * 4 + 2, :] = push[c, kz, x * 4 : x * 4 + 2, :] + rd[kz, at : at + 2, :]
        for x in range(4):
            for c in range(2):
                push[3 + c, kz, x * 4 : x * 4 + 4, :] = (
                    warm[0, kz, (x + 2) * 6 + 2 : (x + 2) * 6 + 6, :]
                    if c == 0
                    else region[0, kz, (x + 2) * 6 + 2 : (x + 2) * 6 + 6, :]
                )
    width_x = 4 * lax.axis_size("gx")
    height_z = 512
    spin = 2.0 / height_z
    shape = (16, 128)
    cell_x = lax.broadcasted_iota(jnp.int32, shape, 0) // 4 - 1 + 4 * lax.axis_index("gx")
    cell_x = jnp.where(cell_x < 0, cell_x + width_x, cell_x).astype(f32)
    wall_w = -spin * (cell_x + 0.5 - 0.5 * width_x)
    for kz in range(4):
        cell_z = (lax.broadcasted_iota(jnp.int32, shape, 1) * 4 + kz).astype(f32)
        wall = [spin * (cell_z + 0.5 - 0.5 * height_z), jnp.zeros(shape, f32), wall_w]
        inverse = 1.0 / jnp.maximum(push[3, kz], mass_floor)
        moving = [push[a, kz] * inverse for a in range(3)]
        moving[2] = moving[2] - gravity_step
        relative = [moving[a] - wall[a] for a in range(3)]
        facing = [normal[a, kz] for a in range(3)]
        normal_part = sum(relative[a] * facing[a] for a in range(3))
        tangent = [relative[a] - normal_part * facing[a] for a in range(3)]
        length = jnp.sqrt(sum(part * part for part in tangent))
        factor = jnp.maximum(
            0.0, 1.0 + friction * normal_part / jnp.maximum(length, slip_floor)
        )
        slips = (rough[kz] == 1.0) & (normal_part < 0.0)
        solid = push[4, kz] == 1.0
        for a in range(3):
            value = jnp.where(slips, wall[a] + tangent[a] * factor, moving[a])
            push[a, kz] = jnp.where(solid, wall[a], value)
        heat = warm[1, kz, 0:36, :] / jnp.maximum(warm[0, kz, 0:36, :], mass_floor)
        warm[1, kz, 0:36, :] = jnp.where(region[0, kz] == 1.0, region[1, kz], heat)
    for kz in range(4):
        ko[kz, 0:36, :] = warm[1, kz, 0:36, :]
        ko[kz, 36:40, :] = jnp.zeros((4, 128), f32)
        hl[kz, 0:24, :] = warm[1, kz, 12:36, :]
        for c in range(3):
            ko[kz, 40 + c * 16 : 56 + c * 16, :] = push[c, kz]
            hl[kz, 24 + c * 8 : 32 + c * 8, :] = push[c, kz, 0:8, :]
            for x in range(4):
                at = 24 + c * 8 + x * 2
                hb[kz, at : at + 2, :] = push[c, kz, x * 4 : x * 4 + 2, :]
            for x in range(2):
                at = 16 + c * 4 + x * 2
                hd[kz, at : at + 2, :] = push[c, kz, x * 4 : x * 4 + 2, :]
        for x in range(6):
            hb[kz, x * 4 : x * 4 + 4, :] = warm[1, kz, x * 6 + 2 : x * 6 + 6, :]
        for x in range(4):
            hd[kz, x * 4 : x * 4 + 4, :] = warm[1, kz, (x + 2) * 6 + 2 : (x + 2) * 6 + 6, :]
        hd[kz, 28:32, :] = jnp.zeros((4, 128), f32)


def shape_slots(fo, out, sb, sb2):
    sb[...] = jnp.zeros(sb.shape, f32)
    sb2[...] = jnp.zeros(sb2.shape, f32)

    def build(g, sb):
        rows = pl.ds(pl.multiple_of(g * 8, 8), 8)
        offset = fo[2, rows, :].astype(jnp.int32)
        wy, ry = axis_tables((offset >> 2) & 3, fo[0, rows, :], 4.0)
        wz, rz = axis_tables(offset & 3, fo[1, rows, :], 4.0)
        for jz in range(6):
            for jy in range(6):
                r = jz * 6 + jy
                sb[pl.ds(r * 8, 8), :] = wy[jy] * wz[jz]
                sb[pl.ds((40 + r) * 8, 8), :] = ry[jy] * wz[jz]
                sb[pl.ds((80 + r) * 8, 8), :] = wy[jy] * rz[jz]

    def work(g, sb):
        for j in range(8):
            right = jnp.concatenate(
                [sb[pl.ds(n * 320 + j, 40, stride=8), :] for n in range(3)], axis=1
            )
            high, low = split_two(right)
            right = jnp.concatenate([high, high, low, jnp.zeros((8, 384), f32)], axis=0).astype(bf16)
            out[pl.ds(pl.multiple_of((g * 8 + j) * 128, 128), 128), :] = right

    def pair(i, carry):
        build(2 * i + 1, sb2)
        work(2 * i, sb)
        build(jnp.minimum(2 * i + 2, 15), sb)
        work(2 * i + 1, sb2)
        return carry

    build(0, sb)
    lax.fori_loop(0, 8, pair, 0)


def shape_own_kernel(frac, o_ref, out, fo, sb, sb2):
    fo[0] = frac[1]
    fo[1] = frac[2]
    fo[2] = o_ref[...].astype(f32)
    shape_slots(fo, out, sb, sb2)


def shape_new_kernel(rxp, rxm, ryp, rym, out, fo, sb, sb2):
    places = [(ryp, 0), (rxp, 1), (rym, 0), (ryp, 1), (rym, 1), (ryp, 2), (rxm, 1), (rym, 2)]
    for g, (ref, at) in enumerate(places):
        for d in range(3):
            fo[d, g * 16 : g * 16 + 16, :] = ref[pl.ds(at * way_rows + 1 + d, 16, stride=4), :]
    shape_slots(fo, out, sb, sb2)


def collect_kernel(
    code_s, brick_s, came_s, ko, rl, rb, rd, solid, frac, o_ref, rxp, rxm, ryp, rym, own_shape, new_shape,
    move_ref, grad_ref, warm_ref, gvel_ref, gtemp_ref,
    heat, speed, cells, fine, coarse, turn, lu, fo, sw, sw2,
):
    lane = lax.broadcasted_iota(jnp.int32, (8, 128), 1)[0:1]
    heat[...] = jnp.zeros(heat.shape, f32)
    for kz in range(4):
        for x in range(6):
            to = 16 + x * 10
            heat[0, kz, to : to + 6, :] = ko[kz, x * 6 : x * 6 + 6, :]
            heat[0, kz, to + 6 : to + 10, :] = rb[kz, x * 4 : x * 4 + 4, :]
        for x in range(4):
            to = 16 + (x + 6) * 10
            heat[0, kz, to : to + 6, :] = rl[kz, x * 6 : x * 6 + 6, :]
            heat[0, kz, to + 6 : to + 10, :] = rd[kz, x * 4 : x * 4 + 4, :]
        for c in range(3):
            for x in range(4):
                speed[c, kz, x * 6 : x * 6 + 4, :] = ko[kz, 40 + c * 16 + x * 4 : 44 + c * 16 + x * 4, :]
                at = 24 + c * 8 + x * 2
                speed[c, kz, x * 6 + 4 : x * 6 + 6, :] = rb[kz, at : at + 2, :]
            for x in range(2):
                at = 24 + c * 8 + x * 4
                speed[c, kz, 24 + x * 6 : 28 + x * 6, :] = rl[kz, at : at + 4, :]
                at = 16 + c * 4 + x * 2
                speed[c, kz, 28 + x * 6 : 30 + x * 6, :] = rd[kz, at : at + 2, :]
    for sweep in range(2):
        now, later = sweep, sweep + 1
        layers = [heat[now, kz, 16:120, :] for kz in range(4)]
        above = jnp.where(lane == 127, layers[3], pltpu.roll(layers[0], 127, 1))
        below = jnp.where(lane == 0, layers[0], pltpu.roll(layers[3], 1, 1))
        for kz in range(4):
            upper = layers[kz + 1] if kz < 3 else above
            lower = layers[kz - 1] if kz else below
            laplace = (
                heat[now, kz, 6:110, :]
                + heat[now, kz, 26:130, :]
                + heat[now, kz, 15:119, :]
                + heat[now, kz, 17:121, :]
                + upper
                + lower
                - 6.0 * layers[kz]
            )
            heat[later, kz, 16:120, :] = jnp.where(
                solid[kz] == 1.0, heat[0, kz, 16:120, :], layers[kz] + conduct * laplace
            )
    for kz in range(4):
        for x in range(6):
            to = 16 + (x + 2) * 10 + 2
            speed[3, kz, x * 6 : x * 6 + 6, :] = heat[2, kz, to : to + 6, :]
    for c in range(4):
        for kz in range(4):
            for x in range(4):
                at = (x + 1) * 6 + 1
                cells[c * 16 + x * 4 : c * 16 + x * 4 + 4, kz * 128 : kz * 128 + 128] = speed[c, kz, at : at + 4, :]
    source = lax.broadcasted_iota(jnp.int32, (512, 512), 0)
    wanted = (source % 128) * 4 + source // 128
    permute = (wanted == lax.broadcasted_iota(jnp.int32, (512, 512), 1)).astype(f32).astype(bf16)
    value = cells[...]
    high, rest = split_two(value)
    middle, low = split_two(rest)
    spread = jnp.concatenate([high, middle, low], axis=0).astype(bf16)
    spread = jnp.dot(spread, permute, preferred_element_type=f32)
    value = spread[0:64] + spread[64:128] + spread[128:192]
    for x in range(4):
        for c in range(3):
            gvel_ref[c, x] = value[c * 16 + x * 4 : c * 16 + x * 4 + 4]
        gtemp_ref[x] = value[48 + x * 4 : 52 + x * 4]
    for c in range(4):
        for jz in range(6):
            kz = (jz - 1) % 4
            layer = speed[c, kz]
            if jz == 0:
                layer = jnp.where(lane == 0, 0.0, pltpu.roll(layer, 1, 1))
            if jz == 5:
                layer = jnp.where(lane == 127, 0.0, pltpu.roll(layer, 127, 1))
            high, low = split_two(layer)
            coarse[c, jz] = high
            fine[c, jz] = low
    turn[...] = jnp.zeros(turn.shape, f32)
    for jx in range(6):
        for c in range(4):
            side = c % 2
            for jz in range(6):
                rows = slice(jx * 6, jx * 6 + 6)
                turn[side, jz * 6 : jz * 6 + 6, :] = coarse[c, jz, rows, :]
                turn[side, 40 + jz * 6 : 46 + jz * 6, :] = fine[c, jz, rows, :]
                turn[side, 80 + jz * 6 : 86 + jz * 6, :] = coarse[c, jz, rows, :]
            lu[pl.ds(jx * 4 + c, 128, stride=24), :] = jnp.transpose(turn[side])
    fo[0, 0:128, :] = frac[0]
    fo[1, 0:128, :] = o_ref[...].astype(f32)
    places = [(ryp, 0), (rxp, 1), (rym, 0), (ryp, 1), (rym, 1), (ryp, 2), (rxm, 1), (rym, 2)]
    for g, (ref, at) in enumerate(places):
        for d in range(2):
            fo[d, 128 + g * 16 : 144 + g * 16, :] = ref[pl.ds(at * way_rows + 3 * d, 16, stride=4), :]

    def build(g, sw):
        rows = pl.ds(pl.multiple_of(g * 8, 8), 8)
        offset = fo[1, rows, :].astype(jnp.int32)
        wx, rx = axis_tables(offset >> 4, fo[0, rows, :], 4.0)
        for j in range(6):
            for copy in range(4):
                sw[pl.ds((j * 4 + copy) * 8, 8), :] = wx[j]
                sw[pl.ds((24 + j * 4 + copy) * 8, 8), :] = rx[j]

    def work(g, shaped, first, sw):
        for j in range(8):
            slot = g * 8 + j
            home = jnp.minimum(slot, 127)
            stays = jnp.where(code_s[home] == 4, brick_s[home], -1)
            brick = jnp.where(slot < 128, stays, came_s[0, jnp.maximum(slot - 128, 0)])
            live = jnp.where(brick >= 0, 1.0, 0.0).astype(f32)
            spot = pl.ds(pl.multiple_of(jnp.maximum(brick, 0) * 24, 8), 24)
            left = lu[spot, :].astype(bf16)
            right = shaped[pl.ds(pl.multiple_of((slot - first) * 128, 128), 128), :]
            both = jnp.dot(left, right, preferred_element_type=f32)
            plain = sw[pl.ds(j, 24, stride=8), :]
            tilt = sw[pl.ds(192 + j, 24, stride=8), :]

            def over_x(weight, column):
                part = weight * both[:, column * 128 : column * 128 + 128]
                part = part[0:8] + part[8:16] + part[16:24]
                return (part[0:4] + part[4:8]) * live

            lanes = pl.ds(pl.multiple_of(slot * 128, 128), 128)
            moved = over_x(plain, 0)
            move_ref[:, lanes] = moved[0:3]
            warm_ref[pl.ds(slot, 1), :] = moved[3:4]
            for k, (weight, column) in enumerate(((tilt, 0), (plain, 1), (plain, 2))):
                part = over_x(weight, column)
                for a in range(3):
                    grad_ref[a * 3 + k : a * 3 + k + 1, lanes] = part[a : a + 1]

    for shaped, first in ((own_shape, 0), (new_shape, 128)):
        last = first // 8 + 15

        def pair(i, carry, shaped=shaped, first=first, last=last):
            g = first // 8 + 2 * i
            build(g + 1, sw2)
            work(g, shaped, first, sw)
            build(jnp.minimum(g + 2, last), sw)
            work(g + 1, shaped, first, sw2)
            return carry

        build(first // 8, sw)
        lax.fori_loop(0, 8, pair, 0)


def neighbor(value, dx, dy):
    size_x, size_y = lax.axis_size("gx"), lax.axis_size("gy")
    if dy == 0:
        return lax.ppermute(value, "gx", [(i, (i + dx) % size_x) for i in range(size_x)])
    if dx == 0:
        return lax.ppermute(value, "gy", [(i, (i + dy) % size_y) for i in range(size_y)])
    pairs = [
        (i * size_y + j, (i + dx) % size_x * size_y + (j + dy) % size_y)
        for i in range(size_x)
        for j in range(size_y)
    ]
    return lax.ppermute(value, ("gx", "gy"), pairs)


def call(
    kernel, name, inputs, scalars, outputs, scratch, left_there=0, limit=24, flops=1e8, listed=0
):
    in_specs = (
        [pl.BlockSpec(memory_space=pltpu.SMEM)] * scalars
        + [pl.BlockSpec(memory_space=pltpu.HBM)] * left_there
        + [pl.BlockSpec(memory_space=pltpu.VMEM)] * (len(inputs) - scalars - left_there)
    )
    return pl.pallas_call(
        kernel,
        name=name,
        out_shape=[jax.ShapeDtypeStruct(shape, dtype) for shape, dtype in outputs],
        in_specs=in_specs,
        out_specs=[pl.BlockSpec(memory_space=pltpu.SMEM)] * listed
        + [pl.BlockSpec(memory_space=pltpu.VMEM)] * (len(outputs) - listed),
        cost_estimate=pl.CostEstimate(
            flops=int(flops), bytes_accessed=int(flops / 300), transcendentals=0
        ),
        scratch_shapes=scratch,
        compiler_params=pltpu.CompilerParams(vmem_limit_bytes=limit * mib),
    )(
        *inputs[:scalars],
        *[pltpu.with_memory_space_constraint(x, pltpu.HBM) for x in inputs[scalars : scalars + left_there]],
        *inputs[scalars + left_there :],
    )


def vmem(*shape):
    return pltpu.VMEM(shape, f32)


def on_device(
    subvoxel_location_share,
    point_motion_vector,
    linear_gradient_matrix,
    kirchhoff_tension_matrix,
    point_inertia_amounts,
    point_thermal_state,
    anchor_voxel_shift,
    group_resting_volume,
    group_migration_label,
    cylinder_shell_flag,
    rough_surface_flag,
    voxel_facing_choice,
    facing_unit_vectors,
    rim_thermal_level,
):
    offset = anchor_voxel_shift.reshape(128, 128)
    info, static, sxp, sxm, *block_args = call(
        prepare_kernel,
        "prepare",
        (
            facing_unit_vectors,
            group_migration_label,
            cylinder_shell_flag,
            rough_surface_flag,
            voxel_facing_choice,
            rim_thermal_level,
            group_resting_volume,
            subvoxel_location_share,
            point_motion_vector,
            linear_gradient_matrix,
            kirchhoff_tension_matrix,
            point_inertia_amounts.reshape(128, 128),
            point_thermal_state.reshape(128, 128),
            offset,
        ),
        0,
        [
            ((768,), jnp.int32),
            ((6, 96, 128), f32),
            ((352, 128), f32),
            ((224, 128), f32),
            ((3, 16384), f32),
            ((3, 16384), f32),
            ((9, 16384), f32),
            ((9, 16384), f32),
            ((128, 128), f32),
            ((128, 128), f32),
            ((128, 128), jnp.int32),
        ],
        [
            pltpu.SMEM((3, 64), f32),
            pltpu.SMEM((128,), jnp.int32),
            pltpu.SMEM((128,), jnp.int32),
            pltpu.VMEM((4, 4, 512), jnp.int32),
            pltpu.VMEM((4, 4, 512), jnp.int32),
            pltpu.VMEM((4, 4, 512), jnp.int32),
            vmem(4, 4, 512),
            pltpu.SemaphoreType.DMA((14,)),
            vmem(64, 512),
            vmem(520, 128),
            pltpu.SMEM((16,), jnp.int32),
        ],
        14,
        24,
        flops=2e9,
        listed=1,
    )
    rsxp = neighbor(sxp, 1, 0)
    rsxm = neighbor(sxm, -1, 0)
    block_scratch = [
        vmem(320, 128),
        vmem(96 * 8, 128),
        vmem(120 * 8, 128),
        vmem(320, 128),
        vmem(96 * 8, 128),
        vmem(120 * 8, 128),
        vmem(130 * 40, 128),
    ]
    xm, ym, yp, xp = call(
        outgoing_kernel,
        "outgoing",
        (info, *block_args),
        1,
        [
            ((3 * msg_rows, 128), f32),
            ((msg_rows, 128), f32),
            ((msg_rows, 128), f32),
            ((3 * msg_rows, 128), f32),
        ],
        block_scratch,
        limit=24,
        flops=6e9,
    )
    xm, xp, rsxp, rsxm = lax.optimization_barrier((xm, xp, rsxp, rsxm))
    rxp = neighbor(xp, 1, 0)
    rxm = neighbor(xm, -1, 0)
    up, down = call(
        relay_kernel,
        "relay",
        (rsxp, rsxm, static),
        0,
        [((448, 128), f32), ((288, 128), f32)],
        [],
        flops=5e8,
    )
    rsyp = neighbor(up, 0, 1)
    rsym = neighbor(down, 0, -1)
    up = jnp.concatenate([rxp[2 * msg_rows :], yp, rxm[2 * msg_rows :]], axis=0)
    down = jnp.concatenate([rxp[:msg_rows], ym, rxm[:msg_rows]], axis=0)
    up, down, info = lax.optimization_barrier((up, down, info))
    ryp = neighbor(up, 0, 1)
    rym = neighbor(down, 0, -1)
    own, frac = call(
        staying_kernel,
        "staying",
        (info, *block_args),
        1,
        [((tiles, 128, 128), f32), ((3, 128, 128), f32)],
        block_scratch,
        limit=24,
        flops=1e10,
    )
    region, rough, normal, solid = call(
        assemble_kernel,
        "assemble",
        (static, rsxp, rsxm, rsyp, rsym),
        0,
        [
            ((2, 4, 36, 128), f32),
            ((4, 16, 128), f32),
            ((3, 4, 16, 128), f32),
            ((4, 104, 128), f32),
        ],
        [],
        flops=5e8,
    )

    ml, mb, md, mo, came = call(
        total_kernel,
        "total",
        (own, rxp, rxm, ryp, rym),
        0,
        [
            ((4, 56, 128), f32),
            ((4, 56, 128), f32),
            ((4, 48, 128), f32),
            ((4, 80, 128), f32),
            ((1, 128), jnp.int32),
        ],
        [vmem(tiles * 128, 128), vmem(4, 184, 128)],
    )
    shape_scratch = [vmem(3, 128, 128), vmem(120 * 8, 128), vmem(120 * 8, 128)]
    shape_out = [((128 * 128, 384), bf16)]
    frac, ml, mb, md = lax.optimization_barrier((frac, ml, mb, md))
    (own_shape,) = call(
        shape_own_kernel, "shape_own", (frac, offset), 0, shape_out, shape_scratch, flops=4e9
    )
    region, own_shape = lax.optimization_barrier((region, own_shape))
    hl, hb, hd, ko = call(
        update_kernel,
        "update",
        (mo, neighbor(ml, 1, 0), neighbor(mb, 0, 1), neighbor(md, 1, 1), region, rough, normal),
        0,
        [
            ((4, 48, 128), f32),
            ((4, 48, 128), f32),
            ((4, 32, 128), f32),
            ((4, 88, 128), f32),
        ],
        [vmem(2, 4, 40, 128), vmem(5, 4, 16, 128)],
    )
    came_from, hl, hb, hd = lax.optimization_barrier(((rsxp, rsxm, rsyp, rsym), hl, hb, hd))
    (new_shape,) = call(
        shape_new_kernel, "shape_new", came_from, 0, shape_out, shape_scratch, flops=4e9
    )
    move, grad, warm, gvel, gtemp = call(
        collect_kernel,
        "collect",
        (
            group_migration_label,
            group_resting_volume,
            came,
            ko,
            neighbor(hl, -1, 0),
            neighbor(hb, 0, -1),
            neighbor(hd, -1, -1),
            solid,
            frac,
            offset,
            rsxp,
            rsxm,
            rsyp,
            rsym,
            own_shape,
            new_shape,
        ),
        3,
        [
            ((3, 32768), f32),
            ((9, 32768), f32),
            ((256, 128), f32),
            ((3, 4, 4, 512), f32),
            ((4, 4, 512), f32),
        ],
        [
            vmem(3, 4, 136, 128),
            vmem(4, 4, 40, 128),
            vmem(64, 512),
            vmem(4, 6, 40, 128),
            vmem(4, 6, 40, 128),
            vmem(2, 128, 128),
            vmem(128 * 24, 128),
            vmem(2, 256, 128),
            vmem(48 * 8, 128),
            vmem(48 * 8, 128),
        ],
    )
    return move, grad, warm.reshape(-1), gvel, gtemp


def solution(mesh):
    in_specs = (
        P(None, ("gx", "gy")),
        P(None, ("gx", "gy")),
        P(None, ("gx", "gy")),
        P(None, ("gx", "gy")),
        P(("gx", "gy")),
        P(("gx", "gy")),
        P(("gx", "gy")),
        P(("gx", "gy")),
        P(("gx", "gy")),
        P("gx", "gy", None),
        P("gx", "gy", None),
        P("gx", "gy", None),
        P(),
        P("gx", "gy", None),
    )
    out_specs = (
        P(None, ("gx", "gy")),
        P(None, ("gx", "gy")),
        P(("gx", "gy")),
        P(None, "gx", "gy", None),
        P("gx", "gy", None),
    )
    return jax.shard_map(
        on_device, mesh=mesh, in_specs=in_specs, out_specs=out_specs, check_vma=False
    )
```

```python
import jax
import jax.numpy as jnp
from jax import lax
from jax.experimental import pallas as pl
from jax.experimental.pallas import tpu as pltpu
from jax.sharding import PartitionSpec as P

f32 = jnp.float32
bf16 = jnp.bfloat16
mass_floor = 0.25
slip_floor = 0.1
friction = 0.4
gravity_step = 0.5
conduct = 0.15
stress_coef = 0.25
mib = 1024 * 1024
pieces = 31
tiles = 9
msg_rows = tiles * 16
way_rows = 64


def axis_tables(shift, inside, scale):
    near = 0.5 * (1.5 - inside) ** 2
    middle = 0.75 - (inside - 1.0) ** 2
    far = 0.5 * (inside - 0.5) ** 2
    at = [shift == step for step in range(4)]
    zero = jnp.zeros_like(inside)
    weight = [
        jnp.where(at[0], near, zero),
        jnp.where(at[0], middle, jnp.where(at[1], near, zero)),
        jnp.where(at[0], far, jnp.where(at[1], middle, jnp.where(at[2], near, zero))),
        jnp.where(at[1], far, jnp.where(at[2], middle, jnp.where(at[3], near, zero))),
        jnp.where(at[2], far, jnp.where(at[3], middle, zero)),
        jnp.where(at[3], far, zero),
    ]
    place = shift.astype(f32) + inside
    first = [weight[step] * (scale * (step - place)) for step in range(6)]
    return weight, first


def split_two(value):
    high = value.astype(bf16).astype(f32)
    return high, value - high


def clear_rows(ref, rows):
    def step(n, carry):
        ref[pl.ds(pl.multiple_of(n * 128, 128), 128), :] = jnp.zeros((128, 128), f32)
        return carry

    lax.fori_loop(0, rows // 128, step, 0)


def deposit_blocks(
    base, count, info_s, target_of, refs, first, second, acc, after
):
    f_ref, v_ref, c_ref, k_ref, m_ref, t_ref, o_ref = refs
    clear_rows(acc, 128 * 40)
    for _, sa, sb in (first, second):
        sa[...] = jnp.zeros(sa.shape, f32)
        sb[...] = jnp.zeros(sb.shape, f32)
    row_no = lax.broadcasted_iota(jnp.int32, (32, 1), 0)

    def build(g, raw, sa, sb):
        blocks = [info_s[base + g * 8 + j] for j in range(8)]
        for j in range(8):
            lanes = pl.ds(pl.multiple_of(blocks[j] * 128, 128), 128)
            raw[j * 40 : j * 40 + 3, :] = f_ref[:, lanes]
            raw[j * 40 + 3 : j * 40 + 6, :] = v_ref[:, lanes]
            raw[j * 40 + 6 : j * 40 + 7, :] = m_ref[pl.ds(blocks[j], 1), :]
            raw[j * 40 + 7 : j * 40 + 8, :] = t_ref[pl.ds(blocks[j], 1), :]
            raw[j * 40 + 8 : j * 40 + 17, :] = c_ref[:, lanes]
            raw[j * 40 + 24 : j * 40 + 33, :] = k_ref[:, lanes]
            raw[j * 40 + 33 : j * 40 + 34, :] = o_ref[pl.ds(blocks[j], 1), :].astype(f32)

        def get(row):
            return raw[pl.ds(row, 8, stride=40), :]

        mass = get(6)
        heat = mass * get(7)
        offset = get(33).astype(jnp.int32)
        inside = [get(d) for d in range(3)]
        wx, rx = axis_tables(offset >> 4, inside[0], 1.0)
        for a in range(3):
            push = mass * get(3 + a)
            q = [
                mass * get(8 + a * 3 + k) - stress_coef * get(24 + a * 3 + k) for k in range(3)
            ]
            for j in range(6):
                sa[pl.ds((a * 6 + j) * 8, 8), :] = push * wx[j] + q[0] * rx[j]
                sa[pl.ds((32 + a * 6 + j) * 8, 8), :] = q[1] * wx[j]
                sa[pl.ds((64 + a * 6 + j) * 8, 8), :] = q[2] * wx[j]
        for j in range(6):
            sa[pl.ds((18 + j) * 8, 8), :] = mass * wx[j]
            sa[pl.ds((24 + j) * 8, 8), :] = heat * wx[j]
        wy, ry = axis_tables((offset >> 2) & 3, inside[1], 1.0)
        wz, rz = axis_tables(offset & 3, inside[2], 1.0)
        for jy in range(6):
            for jz in range(6):
                r = jy * 6 + jz
                sb[pl.ds(r * 8, 8), :] = wy[jy] * wz[jz]
                sb[pl.ds((40 + r) * 8, 8), :] = ry[jy] * wz[jz]
                sb[pl.ds((80 + r) * 8, 8), :] = wy[jy] * rz[jz]

    def work(g, raw, sa, sb):
        blocks = [info_s[base + g * 8 + j] for j in range(8)]
        sums = []
        for j in range(8):
            left = jnp.concatenate(
                [sa[pl.ds(n * 256 + j, 32, stride=8), :] for n in range(3)], axis=1
            )
            right = jnp.concatenate(
                [sb[pl.ds(n * 320 + j, 40, stride=8), :] for n in range(3)], axis=1
            )
            left = jnp.concatenate(split_two(left), axis=0).astype(bf16)
            right = jnp.concatenate(split_two(right), axis=0).astype(bf16)
            both = lax.dot_general(
                left, right, (((1,), (1,)), ((), ())), preferred_element_type=f32
            )
            both = both[:32] + both[32:]
            sums.append(both[:, :40] + both[:, 40:])
        for j in range(8):
            target, mark = target_of(g * 8 + j, blocks[j])
            spot = pl.ds(pl.multiple_of(target * 40, 8), 32)
            acc[spot, 0:40] = acc[spot, 0:40] + (sums[j] + jnp.where(row_no == 30, mark, 0.0))
            after(j, blocks[j], raw)

    def pair(i, carry):
        build(2 * i + 1, *second)
        work(2 * i, *first)
        build(2 * i + 2, *first)
        work(2 * i + 1, *second)
        return carry

    build(0, *first)
    lax.fori_loop(0, (count + 15) // 16, pair, 0)


def packed(acc, chunk):
    lane = lax.broadcasted_iota(jnp.int32, (8, 128), 1)
    total = [jnp.zeros((8, 128), f32) for _ in range(tiles)]
    for i in range(pieces):
        piece = acc[pl.ds(chunk * 320 + i, 8, stride=40), :]
        if i == 30:
            piece = jnp.where(lane < 36, piece, 0.0)
        tile, at = divmod(i * 36, 128)
        if at:
            piece = pltpu.roll(piece, at, 1)
        if at + 36 > 128:
            total[tile] = total[tile] + jnp.where(lane >= at, piece, 0.0)
            total[tile + 1] = total[tile + 1] + jnp.where(lane < at, piece, 0.0)
        else:
            total[tile] = total[tile] + piece
    return total


def outgoing_kernel(
    info_s, f_ref, v_ref, c_ref, k_ref, m_ref, t_ref, o_ref,
    xm_ref, ym_ref, yp_ref, xp_ref,
    raw, sa, sb, raw2, sa2, sb2, acc,
):
    def target_of(entry, block):
        return info_s[160 + entry], (info_s[640 + block] + 1).astype(f32)

    deposit_blocks(
        0, info_s[544], info_s, target_of,
        (f_ref, v_ref, c_ref, k_ref, m_ref, t_ref, o_ref),
        (raw, sa, sb), (raw2, sa2, sb2), acc, lambda j, block, raw: None,
    )
    for first, count, ref in ((0, 3, xm_ref), (3, 1, ym_ref), (4, 1, yp_ref), (5, 3, xp_ref)):
        for n in range(count):
            for half in range(2):

                def some(n=n, half=half, first=first, ref=ref):
                    for tile, value in enumerate(packed(acc, (first + n) * 2 + half)):
                        at = n * msg_rows + tile * 16 + half * 8
                        ref[at : at + 8, :] = value

                def none(n=n, half=half, ref=ref):
                    for tile in range(tiles):
                        at = n * msg_rows + tile * 16 + half * 8
                        ref[at : at + 8, :] = jnp.zeros((8, 128), f32)

                lax.cond(info_s[552 + first + n] > half * 8, some, none)


def staying_kernel(
    info_s, f_ref, v_ref, c_ref, k_ref, m_ref, t_ref, o_ref,
    own_ref, frac_ref,
    raw, sa, sb, raw2, sa2, sb2, acc,
):
    frac_ref[...] = jnp.zeros(frac_ref.shape, f32)

    def target_of(entry, block):
        return jnp.where(entry < info_s[545], info_s[640 + block], 128), jnp.float32(0.0)

    def after(j, block, raw):
        for d in range(3):
            frac_ref[d, pl.ds(block, 1), :] = raw[j * 40 + d : j * 40 + d + 1, :]

    deposit_blocks(
        320, info_s[545], info_s, target_of,
        (f_ref, v_ref, c_ref, k_ref, m_ref, t_ref, o_ref),
        (raw, sa, sb), (raw2, sa2, sb2), acc, after,
    )

    def pack_own(chunk, carry):
        for tile, value in enumerate(packed(acc, chunk)):
            own_ref[tile, pl.ds(pl.multiple_of(chunk * 8, 8), 8), :] = value
        return carry

    lax.fori_loop(0, 16, pack_own, 0)


def runs_left():
    return (
        [(3, x, 0, 4) for x in range(2, 6)]
        + [(4, x, 0, 4) for x in range(2, 6)]
        + [(c, x, 0, 4) for c in range(3) for x in (4, 5)]
    )


def runs_below():
    return (
        [(3, x, 2, 4) for x in range(4)]
        + [(4, x, 2, 4) for x in range(4)]
        + [(c, x, 4, 2) for c in range(3) for x in range(4)]
    )


def runs_diagonal():
    return (
        [(3, x, 2, 4) for x in range(2, 6)]
        + [(4, x, 2, 4) for x in range(2, 6)]
        + [(c, x, 4, 2) for c in range(3) for x in (4, 5)]
    )


def runs_own():
    return [(c, x, 0, 4) for c in range(5) for x in range(4)]


def total_kernel(own_ref, rxp, rxm, ryp, rym, ml, mb, md, mo, brick_ref, wide, grid):
    places = [(ryp, 0), (rxp, 1), (rym, 0), (ryp, 1), (rym, 1), (ryp, 2), (rxm, 1), (rym, 2)]

    def arrived(tile):
        return jnp.concatenate(
            [ref[pl.ds(at * msg_rows + tile * 16, 16), :] for ref, at in places], axis=0
        )

    rows = lax.broadcasted_iota(jnp.int32, (128, 128), 0)
    lanes = lax.broadcasted_iota(jnp.int32, (128, 128), 1)
    column = arrived(8)[:, 56:57]
    row = jnp.sum(jnp.where(rows == lanes, column, 0.0), axis=0, keepdims=True)
    brick_ref[...] = row.astype(jnp.int32) - 1
    hits = (row == (rows + 1).astype(f32)).astype(f32).astype(bf16)
    hits = jnp.concatenate([hits, hits], axis=1)
    for tile in range(tiles):
        high, low = split_two(arrived(tile))
        stack = jnp.concatenate([high.astype(bf16), low.astype(bf16)], axis=0)
        value = own_ref[tile] + jnp.dot(hits, stack, preferred_element_type=f32)
        wide[tile * 128 : tile * 128 + 128, :] = jnp.transpose(value)
    lane = lax.broadcasted_iota(jnp.int32, (184, 128), 1)

    def layer(jz):
        return wide[pl.ds(jz, 184, stride=6), :]

    grid[0] = layer(1) + jnp.where(lane == 0, 0.0, pltpu.roll(layer(5), 1, 1))
    grid[1] = layer(2)
    grid[2] = layer(3)
    grid[3] = layer(4) + jnp.where(lane == 127, 0.0, pltpu.roll(layer(0), 127, 1))
    for ref, runs in ((ml, runs_left()), (mb, runs_below()), (md, runs_diagonal()), (mo, runs_own())):
        for kz in range(4):
            to = 0
            for c, x, y, count in runs:
                ref[kz, to : to + count, :] = grid[kz, c * 36 + x * 6 + y : c * 36 + x * 6 + y + count, :]
                to += count
            if to < ref.shape[1]:
                ref[kz, to:, :] = jnp.zeros((ref.shape[1] - to, 128), f32)


def prepare_kernel(
    table_hbm, code_hbm, solid_hbm, rough_hbm, choice_hbm, rim_hbm,
    brick_hbm, f_hbm, v_hbm, c_hbm, k_hbm, m_hbm, t_hbm, o_hbm,
    info, own, xp, xm, f_ref, v_ref, c_ref, k_ref, m_ref, t_ref, o_ref,
    table, code_s, brick_s, solid_ref, rough_ref, choice_ref, rim_ref, sems,
    cells, fo, cnt,
):
    pairs = (
        (code_hbm, code_s), (f_hbm, f_ref), (o_hbm, o_ref), (table_hbm, table),
        (solid_hbm, solid_ref), (rough_hbm, rough_ref), (choice_hbm, choice_ref), (rim_hbm, rim_ref),
        (brick_hbm, brick_s), (v_hbm, v_ref), (c_hbm, c_ref), (k_hbm, k_ref), (m_hbm, m_ref),
        (t_hbm, t_ref),
    )
    copies = [pltpu.make_async_copy(a, b, sems.at[n]) for n, (a, b) in enumerate(pairs)]
    for copy in copies:
        copy.start()
    fo[...] = jnp.zeros(fo.shape, f32)
    for copy in copies[:9]:
        copy.wait()
    for n in range(10):
        cnt[n] = 0

    def sort(b, carry):
        code = code_s[b]
        rank = cnt[code]
        cnt[code] = rank + 1
        leaves = code != 4
        way = jnp.where(code > 4, code - 1, code)
        gone = cnt[9]
        slot = way * 16 + rank
        info[jnp.where(leaves, gone, 320 + b - gone)] = b
        info[640 + b] = brick_s[b]
        info[jnp.where(leaves, 160 + gone, 639)] = slot
        cnt[9] = gone + jnp.where(leaves, 1, 0)
        at = pl.multiple_of(jnp.where(leaves, slot, 128) * 4, 4)
        lanes = pl.ds(pl.multiple_of(b * 128, 128), 128)
        fo[pl.ds(at, 3), :] = f_ref[:, lanes]
        fo[pl.ds(at + 3, 1), :] = o_ref[pl.ds(b, 1), :].astype(f32)
        return carry

    lax.fori_loop(0, 128, sort, 0, unroll=4)
    gone = cnt[9]
    for n in range(24):
        info[gone + n] = 0
        info[160 + gone + n] = 128
        info[320 + 128 - gone + n] = 0
    for n in range(8):
        info[552 + n] = cnt[n if n < 4 else n + 1]
    info[544] = gone
    info[545] = 128 - gone
    for x in range(4):
        rows = slice(x * 4, x * 4 + 4)
        cells[rows, :] = solid_ref[x].astype(f32)
        cells[16 + x * 4 : 20 + x * 4, :] = rough_ref[x].astype(f32)
        cells[32 + x * 4 : 36 + x * 4, :] = choice_ref[x].astype(f32)
        cells[48 + x * 4 : 52 + x * 4, :] = rim_ref[x]
    value = cells[...]
    high, rest = split_two(value[48:64])
    middle, low = split_two(rest)
    value = jnp.concatenate([value[0:48], high, middle, low], axis=0).astype(bf16)
    source = lax.broadcasted_iota(jnp.int32, (512, 512), 0)
    wanted = (source % 4) * 128 + source // 4
    permute = (wanted == lax.broadcasted_iota(jnp.int32, (512, 512), 1)).astype(f32).astype(bf16)
    value = jnp.dot(value, permute, preferred_element_type=f32)
    rim = value[48:64] + value[64:80] + value[80:96]
    choice = value[32:48]
    normal = [jnp.zeros(choice.shape, f32) for _ in range(3)]
    for n in range(table.shape[1]):
        hit = choice == float(n)
        normal = [jnp.where(hit, table[d, n], normal[d]) for d in range(3)]
    for kz in range(4):
        lanes = slice(kz * 128, kz * 128 + 128)
        for field, part in enumerate((value[0:16], rim, value[16:32], *normal)):
            own[kz, field * 16 : field * 16 + 16, :] = part[:, lanes]
        at = 192 + kz * 40
        xp[at : at + 12, :] = own[kz, 4:16, :]
        xp[at + 12 : at + 24, :] = own[kz, 20:32, :]
        for field in range(4):
            row = 32 + field * 16
            xp[at + 24 + field * 4 : at + 28 + field * 4, :] = own[kz, row + 12 : row + 16, :]
        xm[192 + kz * 8 : 200 + kz * 8, :] = own[kz, 0:8, :]
    for copy in copies[9:]:
        copy.wait()
    xm[0:192, :] = fo[0:192, :]
    for way in range(2):
        own[4 + way, 0:64, :] = fo[192 + way * 64 : 256 + way * 64, :]
        own[4 + way, 64:96, :] = jnp.zeros((32, 128), f32)
    xp[0:192, :] = fo[320:512, :]


def relay_kernel(left, right, own, up, down):
    for way, ref in ((0, down), (1, up)):
        at = 128 * way
        ref[0:64, :] = left[at : at + 64, :]
        ref[64:128, :] = own[4 + way, 0:64, :]
        ref[128:192, :] = right[at : at + 64, :]
    for kz in range(4):
        lrow, rrow = 192 + kz * 40, 192 + kz * 8
        to = 192 + kz * 64
        for x in range(4):
            up[to + x * 3 : to + x * 3 + 3, :] = own[kz, x * 4 + 1 : x * 4 + 4, :]
        for x in range(3):
            row = 16 + x * 4
            up[to + 12 + x * 3 : to + 15 + x * 3, :] = own[kz, row + 1 : row + 4, :]
            up[to + 33 + x * 3 : to + 36 + x * 3, :] = left[lrow + x * 4 + 1 : lrow + x * 4 + 4, :]
            row = lrow + 12 + x * 4
            up[to + 42 + x * 3 : to + 45 + x * 3, :] = left[row + 1 : row + 4, :]
            for field in range(4):
                row = 32 + field * 16 + x * 4 + 3
                at = to + 21 + field * 3 + x
                up[at : at + 1, :] = own[kz, row : row + 1, :]
        for field in range(4):
            row = lrow + 24 + field * 4 + 3
            up[to + 51 + field : to + 52 + field, :] = left[row : row + 1, :]
        for x in range(2):
            up[to + 55 + x * 3 : to + 58 + x * 3, :] = right[rrow + x * 4 + 1 : rrow + x * 4 + 4, :]
        up[to + 61 : to + 64, :] = jnp.zeros((3, 128), f32)
        to = 192 + kz * 24
        for x in range(4):
            down[to + x * 2 : to + x * 2 + 2, :] = own[kz, x * 4 : x * 4 + 2, :]
        for x in range(3):
            down[to + 8 + x * 2 : to + 10 + x * 2, :] = left[lrow + x * 4 : lrow + x * 4 + 2, :]
        for x in range(2):
            down[to + 14 + x * 2 : to + 16 + x * 2, :] = right[rrow + x * 4 : rrow + x * 4 + 2, :]
        down[to + 18 : to + 24, :] = jnp.zeros((6, 128), f32)


def assemble_kernel(own, left, right, below, above, region, rough, normal, solid):
    solid[...] = jnp.zeros(solid.shape, f32)
    for kz in range(4):
        lrow, rrow, brow, arow = 192 + kz * 40, 192 + kz * 8, 192 + kz * 64, 192 + kz * 24
        for x in range(3):
            for field in range(2):
                inner, outer = x * 6, (x + 3) * 6
                diagonal = brow + 33 + field * 9 + x * 3
                region[field, kz, inner : inner + 3, :] = below[diagonal : diagonal + 3, :]
                row = lrow + field * 12 + x * 4
                region[field, kz, inner + 3 : inner + 6, :] = left[row : row + 3, :]
                row = brow + field * 12 + x * 3
                region[field, kz, outer : outer + 3, :] = below[row : row + 3, :]
                row = field * 16 + x * 4
                region[field, kz, outer + 3 : outer + 6, :] = own[kz, row : row + 3, :]
            to = x * 10
            solid[kz, to : to + 3, :] = below[brow + 33 + x * 3 : brow + 36 + x * 3, :]
            solid[kz, to + 3 : to + 7, :] = left[lrow + x * 4 : lrow + x * 4 + 4, :]
            solid[kz, to + 7 : to + 9, :] = above[arow + 8 + x * 2 : arow + 10 + x * 2, :]
        for x in range(4):
            to = (x + 3) * 10
            solid[kz, to : to + 3, :] = below[brow + x * 3 : brow + x * 3 + 3, :]
            solid[kz, to + 3 : to + 7, :] = own[kz, x * 4 : x * 4 + 4, :]
            solid[kz, to + 7 : to + 9, :] = above[arow + x * 2 : arow + x * 2 + 2, :]
        for x in range(2):
            to = (x + 7) * 10
            solid[kz, to : to + 3, :] = below[brow + 55 + x * 3 : brow + 58 + x * 3, :]
            solid[kz, to + 3 : to + 7, :] = right[rrow + x * 4 : rrow + x * 4 + 4, :]
            solid[kz, to + 7 : to + 9, :] = above[arow + 14 + x * 2 : arow + 16 + x * 2, :]
        for field in range(4):
            ref = rough if field == 0 else normal.at[field - 1]
            ref[kz, 0:1, :] = below[brow + 51 + field : brow + 52 + field, :]
            row = lrow + 24 + field * 4
            ref[kz, 1:4, :] = left[row : row + 3, :]
            for x in range(3):
                to = (x + 1) * 4
                row = brow + 21 + field * 3 + x
                ref[kz, to : to + 1, :] = below[row : row + 1, :]
                row = 32 + field * 16 + x * 4
                ref[kz, to + 1 : to + 4, :] = own[kz, row : row + 3, :]


def update_kernel(mo, rl, rb, rd, region, rough, normal, hl, hb, hd, ko, warm, push):
    warm[...] = jnp.zeros(warm.shape, f32)
    for kz in range(4):
        for ref, dx, dy in ((mo, 2, 2), (rl, 0, 2), (rb, 2, 0), (rd, 0, 0)):
            for c in range(2):
                for x in range(4):
                    at = (48 if ref is mo else 0) + c * 16 + x * 4
                    to = (x + dx) * 6 + dy
                    warm[c, kz, to : to + 4, :] = warm[c, kz, to : to + 4, :] + ref[kz, at : at + 4, :]
        for c in range(3):
            push[c, kz] = mo[kz, c * 16 : c * 16 + 16, :]
            push[c, kz, 0:8, :] = push[c, kz, 0:8, :] + rl[kz, 32 + c * 8 : 40 + c * 8, :]
            for x in range(4):
                at = 32 + c * 8 + x * 2
                push[c, kz, x * 4 : x * 4 + 2, :] = push[c, kz, x * 4 : x * 4 + 2, :] + rb[kz, at : at + 2, :]
            for x in range(2):
                at = 32 + c * 4 + x * 2
                push[c, kz, x * 4 : x * 4 + 2, :] = push[c, kz, x * 4 : x * 4 + 2, :] + rd[kz, at : at + 2, :]
        for x in range(4):
            for c in range(2):
                push[3 + c, kz, x * 4 : x * 4 + 4, :] = (
                    warm[0, kz, (x + 2) * 6 + 2 : (x + 2) * 6 + 6, :]
                    if c == 0
                    else region[0, kz, (x + 2) * 6 + 2 : (x + 2) * 6 + 6, :]
                )
    width_x = 4 * lax.axis_size("gx")
    height_z = 512
    spin = 2.0 / height_z
    shape = (16, 128)
    cell_x = lax.broadcasted_iota(jnp.int32, shape, 0) // 4 - 1 + 4 * lax.axis_index("gx")
    cell_x = jnp.where(cell_x < 0, cell_x + width_x, cell_x).astype(f32)
    wall_w = -spin * (cell_x + 0.5 - 0.5 * width_x)
    for kz in range(4):
        cell_z = (lax.broadcasted_iota(jnp.int32, shape, 1) * 4 + kz).astype(f32)
        wall = [spin * (cell_z + 0.5 - 0.5 * height_z), jnp.zeros(shape, f32), wall_w]
        inverse = 1.0 / jnp.maximum(push[3, kz], mass_floor)
        moving = [push[a, kz] * inverse for a in range(3)]
        moving[2] = moving[2] - gravity_step
        relative = [moving[a] - wall[a] for a in range(3)]
        facing = [normal[a, kz] for a in range(3)]
        normal_part = sum(relative[a] * facing[a] for a in range(3))
        tangent = [relative[a] - normal_part * facing[a] for a in range(3)]
        length = jnp.sqrt(sum(part * part for part in tangent))
        factor = jnp.maximum(
            0.0, 1.0 + friction * normal_part / jnp.maximum(length, slip_floor)
        )
        slips = (rough[kz] == 1.0) & (normal_part < 0.0)
        solid = push[4, kz] == 1.0
        for a in range(3):
            value = jnp.where(slips, wall[a] + tangent[a] * factor, moving[a])
            push[a, kz] = jnp.where(solid, wall[a], value)
        heat = warm[1, kz, 0:36, :] / jnp.maximum(warm[0, kz, 0:36, :], mass_floor)
        warm[1, kz, 0:36, :] = jnp.where(region[0, kz] == 1.0, region[1, kz], heat)
    for kz in range(4):
        ko[kz, 0:36, :] = warm[1, kz, 0:36, :]
        ko[kz, 36:40, :] = jnp.zeros((4, 128), f32)
        hl[kz, 0:24, :] = warm[1, kz, 12:36, :]
        for c in range(3):
            ko[kz, 40 + c * 16 : 56 + c * 16, :] = push[c, kz]
            hl[kz, 24 + c * 8 : 32 + c * 8, :] = push[c, kz, 0:8, :]
            for x in range(4):
                at = 24 + c * 8 + x * 2
                hb[kz, at : at + 2, :] = push[c, kz, x * 4 : x * 4 + 2, :]
            for x in range(2):
                at = 16 + c * 4 + x * 2
                hd[kz, at : at + 2, :] = push[c, kz, x * 4 : x * 4 + 2, :]
        for x in range(6):
            hb[kz, x * 4 : x * 4 + 4, :] = warm[1, kz, x * 6 + 2 : x * 6 + 6, :]
        for x in range(4):
            hd[kz, x * 4 : x * 4 + 4, :] = warm[1, kz, (x + 2) * 6 + 2 : (x + 2) * 6 + 6, :]
        hd[kz, 28:32, :] = jnp.zeros((4, 128), f32)


def shape_slots(fo, out, sb, sb2):
    sb[...] = jnp.zeros(sb.shape, f32)
    sb2[...] = jnp.zeros(sb2.shape, f32)

    def build(g, sb):
        rows = pl.ds(pl.multiple_of(g * 8, 8), 8)
        offset = fo[2, rows, :].astype(jnp.int32)
        wy, ry = axis_tables((offset >> 2) & 3, fo[0, rows, :], 4.0)
        wz, rz = axis_tables(offset & 3, fo[1, rows, :], 4.0)
        for jz in range(6):
            for jy in range(6):
                r = jz * 6 + jy
                sb[pl.ds(r * 8, 8), :] = wy[jy] * wz[jz]
                sb[pl.ds((40 + r) * 8, 8), :] = ry[jy] * wz[jz]
                sb[pl.ds((80 + r) * 8, 8), :] = wy[jy] * rz[jz]

    def work(g, sb):
        for j in range(8):
            right = jnp.concatenate(
                [sb[pl.ds(n * 320 + j, 40, stride=8), :] for n in range(3)], axis=1
            )
            high, low = split_two(right)
            right = jnp.concatenate([high, high, low, jnp.zeros((8, 384), f32)], axis=0).astype(bf16)
            out[pl.ds(pl.multiple_of((g * 8 + j) * 128, 128), 128), :] = right

    def pair(i, carry):
        build(2 * i + 1, sb2)
        work(2 * i, sb)
        build(jnp.minimum(2 * i + 2, 15), sb)
        work(2 * i + 1, sb2)
        return carry

    build(0, sb)
    lax.fori_loop(0, 8, pair, 0)


def shape_own_kernel(frac, o_ref, out, fo, sb, sb2):
    fo[0] = frac[1]
    fo[1] = frac[2]
    fo[2] = o_ref[...].astype(f32)
    shape_slots(fo, out, sb, sb2)


def shape_new_kernel(rxp, rxm, ryp, rym, out, fo, sb, sb2):
    places = [(ryp, 0), (rxp, 1), (rym, 0), (ryp, 1), (rym, 1), (ryp, 2), (rxm, 1), (rym, 2)]
    for g, (ref, at) in enumerate(places):
        for d in range(3):
            fo[d, g * 16 : g * 16 + 16, :] = ref[pl.ds(at * way_rows + 1 + d, 16, stride=4), :]
    shape_slots(fo, out, sb, sb2)


def collect_kernel(
    code_s, brick_s, came_s, ko, rl, rb, rd, solid, frac, o_ref, rxp, rxm, ryp, rym, own_shape, new_shape,
    move_ref, grad_ref, warm_ref, gvel_ref, gtemp_ref,
    heat, speed, cells, fine, coarse, turn, lu, fo, sw, sw2,
):
    lane = lax.broadcasted_iota(jnp.int32, (8, 128), 1)[0:1]
    heat[...] = jnp.zeros(heat.shape, f32)
    for kz in range(4):
        for x in range(6):
            to = 16 + x * 10
            heat[0, kz, to : to + 6, :] = ko[kz, x * 6 : x * 6 + 6, :]
            heat[0, kz, to + 6 : to + 10, :] = rb[kz, x * 4 : x * 4 + 4, :]
        for x in range(4):
            to = 16 + (x + 6) * 10
            heat[0, kz, to : to + 6, :] = rl[kz, x * 6 : x * 6 + 6, :]
            heat[0, kz, to + 6 : to + 10, :] = rd[kz, x * 4 : x * 4 + 4, :]
        for c in range(3):
            for x in range(4):
                speed[c, kz, x * 6 : x * 6 + 4, :] = ko[kz, 40 + c * 16 + x * 4 : 44 + c * 16 + x * 4, :]
                at = 24 + c * 8 + x * 2
                speed[c, kz, x * 6 + 4 : x * 6 + 6, :] = rb[kz, at : at + 2, :]
            for x in range(2):
                at = 24 + c * 8 + x * 4
                speed[c, kz, 24 + x * 6 : 28 + x * 6, :] = rl[kz, at : at + 4, :]
                at = 16 + c * 4 + x * 2
                speed[c, kz, 28 + x * 6 : 30 + x * 6, :] = rd[kz, at : at + 2, :]
    for sweep in range(2):
        now, later = sweep, sweep + 1
        layers = [heat[now, kz, 16:120, :] for kz in range(4)]
        above = jnp.where(lane == 127, layers[3], pltpu.roll(layers[0], 127, 1))
        below = jnp.where(lane == 0, layers[0], pltpu.roll(layers[3], 1, 1))
        for kz in range(4):
            upper = layers[kz + 1] if kz < 3 else above
            lower = layers[kz - 1] if kz else below
            laplace = (
                heat[now, kz, 6:110, :]
                + heat[now, kz, 26:130, :]
                + heat[now, kz, 15:119, :]
                + heat[now, kz, 17:121, :]
                + upper
                + lower
                - 6.0 * layers[kz]
            )
            heat[later, kz, 16:120, :] = jnp.where(
                solid[kz] == 1.0, heat[0, kz, 16:120, :], layers[kz] + conduct * laplace
            )
    for kz in range(4):
        for x in range(6):
            to = 16 + (x + 2) * 10 + 2
            speed[3, kz, x * 6 : x * 6 + 6, :] = heat[2, kz, to : to + 6, :]
    for c in range(4):
        for kz in range(4):
            for x in range(4):
                at = (x + 1) * 6 + 1
                cells[c * 16 + x * 4 : c * 16 + x * 4 + 4, kz * 128 : kz * 128 + 128] = speed[c, kz, at : at + 4, :]
    source = lax.broadcasted_iota(jnp.int32, (512, 512), 0)
    wanted = (source % 128) * 4 + source // 128
    permute = (wanted == lax.broadcasted_iota(jnp.int32, (512, 512), 1)).astype(f32).astype(bf16)
    value = cells[...]
    high, rest = split_two(value)
    middle, low = split_two(rest)
    spread = jnp.concatenate([high, middle, low], axis=0).astype(bf16)
    spread = jnp.dot(spread, permute, preferred_element_type=f32)
    value = spread[0:64] + spread[64:128] + spread[128:192]
    for x in range(4):
        for c in range(3):
            gvel_ref[c, x] = value[c * 16 + x * 4 : c * 16 + x * 4 + 4]
        gtemp_ref[x] = value[48 + x * 4 : 52 + x * 4]
    for c in range(4):
        for jz in range(6):
            kz = (jz - 1) % 4
            layer = speed[c, kz]
            if jz == 0:
                layer = jnp.where(lane == 0, 0.0, pltpu.roll(layer, 1, 1))
            if jz == 5:
                layer = jnp.where(lane == 127, 0.0, pltpu.roll(layer, 127, 1))
            high, low = split_two(layer)
            coarse[c, jz] = high
            fine[c, jz] = low
    turn[...] = jnp.zeros(turn.shape, f32)
    for jx in range(6):
        for c in range(4):
            side = c % 2
            for jz in range(6):
                rows = slice(jx * 6, jx * 6 + 6)
                turn[side, jz * 6 : jz * 6 + 6, :] = coarse[c, jz, rows, :]
                turn[side, 40 + jz * 6 : 46 + jz * 6, :] = fine[c, jz, rows, :]
                turn[side, 80 + jz * 6 : 86 + jz * 6, :] = coarse[c, jz, rows, :]
            lu[pl.ds(jx * 4 + c, 128, stride=24), :] = jnp.transpose(turn[side])
    fo[0, 0:128, :] = frac[0]
    fo[1, 0:128, :] = o_ref[...].astype(f32)
    places = [(ryp, 0), (rxp, 1), (rym, 0), (ryp, 1), (rym, 1), (ryp, 2), (rxm, 1), (rym, 2)]
    for g, (ref, at) in enumerate(places):
        for d in range(2):
            fo[d, 128 + g * 16 : 144 + g * 16, :] = ref[pl.ds(at * way_rows + 3 * d, 16, stride=4), :]

    def build(g, sw):
        rows = pl.ds(pl.multiple_of(g * 8, 8), 8)
        offset = fo[1, rows, :].astype(jnp.int32)
        wx, rx = axis_tables(offset >> 4, fo[0, rows, :], 4.0)
        for j in range(6):
            for copy in range(4):
                sw[pl.ds((j * 4 + copy) * 8, 8), :] = wx[j]
                sw[pl.ds((24 + j * 4 + copy) * 8, 8), :] = rx[j]

    def work(g, shaped, first, sw):
        for j in range(8):
            slot = g * 8 + j
            home = jnp.minimum(slot, 127)
            stays = jnp.where(code_s[home] == 4, brick_s[home], -1)
            brick = jnp.where(slot < 128, stays, came_s[0, jnp.maximum(slot - 128, 0)])
            live = jnp.where(brick >= 0, 1.0, 0.0).astype(f32)
            spot = pl.ds(pl.multiple_of(jnp.maximum(brick, 0) * 24, 8), 24)
            left = lu[spot, :].astype(bf16)
            right = shaped[pl.ds(pl.multiple_of((slot - first) * 128, 128), 128), :]
            both = jnp.dot(left, right, preferred_element_type=f32)
            plain = sw[pl.ds(j, 24, stride=8), :]
            tilt = sw[pl.ds(192 + j, 24, stride=8), :]

            def over_x(weight, column):
                part = weight * both[:, column * 128 : column * 128 + 128]
                part = part[0:8] + part[8:16] + part[16:24]
                return (part[0:4] + part[4:8]) * live

            lanes = pl.ds(pl.multiple_of(slot * 128, 128), 128)
            moved = over_x(plain, 0)
            move_ref[:, lanes] = moved[0:3]
            warm_ref[pl.ds(slot, 1), :] = moved[3:4]
            for k, (weight, column) in enumerate(((tilt, 0), (plain, 1), (plain, 2))):
                part = over_x(weight, column)
                for a in range(3):
                    grad_ref[a * 3 + k : a * 3 + k + 1, lanes] = part[a : a + 1]

    for shaped, first in ((own_shape, 0), (new_shape, 128)):
        last = first // 8 + 15

        def pair(i, carry, shaped=shaped, first=first, last=last):
            g = first // 8 + 2 * i
            build(g + 1, sw2)
            work(g, shaped, first, sw)
            build(jnp.minimum(g + 2, last), sw)
            work(g + 1, shaped, first, sw2)
            return carry

        build(first // 8, sw)
        lax.fori_loop(0, 8, pair, 0)


def neighbor(value, dx, dy):
    size_x, size_y = lax.axis_size("gx"), lax.axis_size("gy")
    if dy == 0:
        return lax.ppermute(value, "gx", [(i, (i + dx) % size_x) for i in range(size_x)])
    if dx == 0:
        return lax.ppermute(value, "gy", [(i, (i + dy) % size_y) for i in range(size_y)])
    pairs = [
        (i * size_y + j, (i + dx) % size_x * size_y + (j + dy) % size_y)
        for i in range(size_x)
        for j in range(size_y)
    ]
    return lax.ppermute(value, ("gx", "gy"), pairs)


def call(
    kernel, name, inputs, scalars, outputs, scratch, left_there=0, limit=24, flops=1e8, listed=0
):
    in_specs = (
        [pl.BlockSpec(memory_space=pltpu.SMEM)] * scalars
        + [pl.BlockSpec(memory_space=pltpu.HBM)] * left_there
        + [pl.BlockSpec(memory_space=pltpu.VMEM)] * (len(inputs) - scalars - left_there)
    )
    return pl.pallas_call(
        kernel,
        name=name,
        out_shape=[jax.ShapeDtypeStruct(shape, dtype) for shape, dtype in outputs],
        in_specs=in_specs,
        out_specs=[pl.BlockSpec(memory_space=pltpu.SMEM)] * listed
        + [pl.BlockSpec(memory_space=pltpu.VMEM)] * (len(outputs) - listed),
        cost_estimate=pl.CostEstimate(
            flops=int(flops), bytes_accessed=int(flops / 300), transcendentals=0
        ),
        scratch_shapes=scratch,
        compiler_params=pltpu.CompilerParams(vmem_limit_bytes=limit * mib),
    )(
        *inputs[:scalars],
        *[pltpu.with_memory_space_constraint(x, pltpu.HBM) for x in inputs[scalars : scalars + left_there]],
        *inputs[scalars + left_there :],
    )


def vmem(*shape):
    return pltpu.VMEM(shape, f32)


def on_device(
    subvoxel_location_share,
    point_motion_vector,
    linear_gradient_matrix,
    kirchhoff_tension_matrix,
    point_inertia_amounts,
    point_thermal_state,
    anchor_voxel_shift,
    group_resting_volume,
    group_migration_label,
    cylinder_shell_flag,
    rough_surface_flag,
    voxel_facing_choice,
    facing_unit_vectors,
    rim_thermal_level,
):
    offset = anchor_voxel_shift.reshape(128, 128)
    info, static, sxp, sxm, *block_args = call(
        prepare_kernel,
        "prepare",
        (
            facing_unit_vectors,
            group_migration_label,
            cylinder_shell_flag,
            rough_surface_flag,
            voxel_facing_choice,
            rim_thermal_level,
            group_resting_volume,
            subvoxel_location_share,
            point_motion_vector,
            linear_gradient_matrix,
            kirchhoff_tension_matrix,
            point_inertia_amounts.reshape(128, 128),
            point_thermal_state.reshape(128, 128),
            offset,
        ),
        0,
        [
            ((768,), jnp.int32),
            ((6, 96, 128), f32),
            ((352, 128), f32),
            ((224, 128), f32),
            ((3, 16384), f32),
            ((3, 16384), f32),
            ((9, 16384), f32),
            ((9, 16384), f32),
            ((128, 128), f32),
            ((128, 128), f32),
            ((128, 128), jnp.int32),
        ],
        [
            pltpu.SMEM((3, 64), f32),
            pltpu.SMEM((128,), jnp.int32),
            pltpu.SMEM((128,), jnp.int32),
            pltpu.VMEM((4, 4, 512), jnp.int32),
            pltpu.VMEM((4, 4, 512), jnp.int32),
            pltpu.VMEM((4, 4, 512), jnp.int32),
            vmem(4, 4, 512),
            pltpu.SemaphoreType.DMA((14,)),
            vmem(64, 512),
            vmem(520, 128),
            pltpu.SMEM((16,), jnp.int32),
        ],
        14,
        24,
        flops=2e9,
        listed=1,
    )
    rsxp = neighbor(sxp, 1, 0)
    rsxm = neighbor(sxm, -1, 0)
    block_scratch = [
        vmem(320, 128),
        vmem(96 * 8, 128),
        vmem(120 * 8, 128),
        vmem(320, 128),
        vmem(96 * 8, 128),
        vmem(120 * 8, 128),
        vmem(130 * 40, 128),
    ]
    xm, ym, yp, xp = call(
        outgoing_kernel,
        "outgoing",
        (info, *block_args),
        1,
        [
            ((3 * msg_rows, 128), f32),
            ((msg_rows, 128), f32),
            ((msg_rows, 128), f32),
            ((3 * msg_rows, 128), f32),
        ],
        block_scratch,
        limit=24,
        flops=6e9,
    )
    rxp = neighbor(xp, 1, 0)
    rxm = neighbor(xm, -1, 0)
    up, down = call(
        relay_kernel,
        "relay",
        (rsxp, rsxm, static),
        0,
        [((448, 128), f32), ((288, 128), f32)],
        [],
        flops=5e8,
    )
    rsyp = neighbor(up, 0, 1)
    rsym = neighbor(down, 0, -1)
    up = jnp.concatenate([rxp[2 * msg_rows :], yp, rxm[2 * msg_rows :]], axis=0)
    down = jnp.concatenate([rxp[:msg_rows], ym, rxm[:msg_rows]], axis=0)
    up, down, info = lax.optimization_barrier((up, down, info))
    ryp = neighbor(up, 0, 1)
    rym = neighbor(down, 0, -1)
    own, frac = call(
        staying_kernel,
        "staying",
        (info, *block_args),
        1,
        [((tiles, 128, 128), f32), ((3, 128, 128), f32)],
        block_scratch,
        limit=24,
        flops=1e10,
    )
    region, rough, normal, solid = call(
        assemble_kernel,
        "assemble",
        (static, rsxp, rsxm, rsyp, rsym),
        0,
        [
            ((2, 4, 36, 128), f32),
            ((4, 16, 128), f32),
            ((3, 4, 16, 128), f32),
            ((4, 104, 128), f32),
        ],
        [],
        flops=5e8,
    )

    ml, mb, md, mo, came = call(
        total_kernel,
        "total",
        (own, rxp, rxm, ryp, rym),
        0,
        [
            ((4, 56, 128), f32),
            ((4, 56, 128), f32),
            ((4, 48, 128), f32),
            ((4, 80, 128), f32),
            ((1, 128), jnp.int32),
        ],
        [vmem(tiles * 128, 128), vmem(4, 184, 128)],
    )
    shape_scratch = [vmem(3, 128, 128), vmem(120 * 8, 128), vmem(120 * 8, 128)]
    shape_out = [((128 * 128, 384), bf16)]
    frac, ml, mb, md = lax.optimization_barrier((frac, ml, mb, md))
    (own_shape,) = call(
        shape_own_kernel, "shape_own", (frac, offset), 0, shape_out, shape_scratch, flops=4e9
    )
    region, own_shape = lax.optimization_barrier((region, own_shape))
    hl, hb, hd, ko = call(
        update_kernel,
        "update",
        (mo, neighbor(ml, 1, 0), neighbor(mb, 0, 1), neighbor(md, 1, 1), region, rough, normal),
        0,
        [
            ((4, 48, 128), f32),
            ((4, 48, 128), f32),
            ((4, 32, 128), f32),
            ((4, 88, 128), f32),
        ],
        [vmem(2, 4, 40, 128), vmem(5, 4, 16, 128)],
    )
    came_from, hl, hb, hd = lax.optimization_barrier(((rsxp, rsxm, rsyp, rsym), hl, hb, hd))
    (new_shape,) = call(
        shape_new_kernel, "shape_new", came_from, 0, shape_out, shape_scratch, flops=4e9
    )
    move, grad, warm, gvel, gtemp = call(
        collect_kernel,
        "collect",
        (
            group_migration_label,
            group_resting_volume,
            came,
            ko,
            neighbor(hl, -1, 0),
            neighbor(hb, 0, -1),
            neighbor(hd, -1, -1),
            solid,
            frac,
            offset,
            rsxp,
            rsxm,
            rsyp,
            rsym,
            own_shape,
            new_shape,
        ),
        3,
        [
            ((3, 32768), f32),
            ((9, 32768), f32),
            ((256, 128), f32),
            ((3, 4, 4, 512), f32),
            ((4, 4, 512), f32),
        ],
        [
            vmem(3, 4, 136, 128),
            vmem(4, 4, 40, 128),
            vmem(64, 512),
            vmem(4, 6, 40, 128),
            vmem(4, 6, 40, 128),
            vmem(2, 128, 128),
            vmem(128 * 24, 128),
            vmem(2, 256, 128),
            vmem(48 * 8, 128),
            vmem(48 * 8, 128),
        ],
    )
    return move, grad, warm.reshape(-1), gvel, gtemp


def solution(mesh):
    in_specs = (
        P(None, ("gx", "gy")),
        P(None, ("gx", "gy")),
        P(None, ("gx", "gy")),
        P(None, ("gx", "gy")),
        P(("gx", "gy")),
        P(("gx", "gy")),
        P(("gx", "gy")),
        P(("gx", "gy")),
        P(("gx", "gy")),
        P("gx", "gy", None),
        P("gx", "gy", None),
        P("gx", "gy", None),
        P(),
        P("gx", "gy", None),
    )
    out_specs = (
        P(None, ("gx", "gy")),
        P(None, ("gx", "gy")),
        P(("gx", "gy")),
        P(None, "gx", "gy", None),
        P("gx", "gy", None),
    )
    return jax.shard_map(
        on_device, mesh=mesh, in_specs=in_specs, out_specs=out_specs, check_vma=False
    )
```
